32 devices in a mesh: dp: 2 (over y), expert: 16 (over z, x, core).
Axes of the slice: x: 2, y: 2, z: 4, core: 2. Of those that a mesh axis runs over, the one named last changes fastest.
Arguments:
- pre_query: bfloat16 [512, 16, 576], P(('dp', 'expert')), may hold values from -25 to 25
- pre_latent: bfloat16 [512, 576], P(('dp', 'expert')), may hold values from -5 to 5
- pre_resid: bfloat16 [512, 2048], P(('dp', 'expert')), may hold values from -6 to 6
- dec_query: bfloat16 [32, 16, 576], P(('dp', 'expert')), may hold values from -25 to 25
- dec_latent: bfloat16 [32, 576], P(('dp', 'expert')), may hold values from -5 to 5
- dec_resid: bfloat16 [32, 2048], P(('dp', 'expert')), may hold values from -6 to 6
- cache_lengths: int32 [32], P(('dp', 'expert')), may hold values from 1 to 32768
- latent_cache: bfloat16 [32, 1024, 576], P(('dp', 'expert')), may hold values from -5 to 5
- sink_logits: float32 [16], replicated, may hold values from -1 to 3
- uv_weight: bfloat16 [16, 512, 128], P('dp', 'expert'), may hold values from -0.25 to 0.25
- out_weight: bfloat16 [16, 128, 2048], P('dp', 'expert'), may hold values from -0.125 to 0.125
- norm_gain: bfloat16 [2048], replicated, may hold values from 0.5 to 1.5
- router: bfloat16 [2048, 16], P(None, 'expert'), may hold values from -0.125 to 0.125
- routes: int32 [544, 6], P(('dp', 'expert')), may hold values from 0 to 15, all different within a row; in each aligned block of 17 rows (0 to 16, 17 to 33, ...) at most 7 rows name the same one
- gate_weight: bfloat16 [16, 2048, 1408], P('expert', None, 'dp'), may hold values from -0.125 to 0.125
- up_weight: bfloat16 [16, 2048, 1408], P('expert', None, 'dp'), may hold values from -0.125 to 0.125
- down_weight: bfloat16 [16, 1408, 2048], P('expert', None, 'dp'), may hold values from -0.15625 to 0.15625
- shared_gate: bfloat16 [2048, 1408], P('expert', 'dp'), may hold values from -0.125 to 0.125
- shared_up: bfloat16 [2048, 1408], P('expert', 'dp'), may hold values from -0.125 to 0.125
- shared_down: bfloat16 [1408, 2048], P('expert', 'dp'), may hold values from -0.15625 to 0.15625
Outputs:
- pre_out: bfloat16 [512, 2048], P(('dp', 'expert'))
- dec_out: bfloat16 [32, 2048], P(('dp', 'expert'))
The draws below stay inside these ranges and needn't reach their ends.
Inputs may be any that keep to these rules, and one draw needn't show every extreme that they name: `routes`: each row names 6 different experts; in each aligned block of 17 rows no expert is named by more than 7 rows.
All inputs are finite; a program needn't handle non-finite values.
Results may differ from the reference program's by a relative error of at most 0.015.
Values may be sent and summed in bfloat16 or wider, within the bound.
No kernel may reach another device: no remote copies, remote signals or barrier semaphores. Data moves between devices by JAX's collectives and lax.ppermute only.
A program may use at most 64 MiB of HBM per device.

```python
import math
from functools import partial
import jax
import jax.numpy as jnp
import numpy as np
from jax import lax

D = 2048
HEADS = 16
LATENT = 512
ROPE = 64
QK_NOPE = 128
VDIM = 128
MOE_FF = 1408
TOPK = 6
SHARED_FF = 1408
WINDOW = 1024
SPAN = 16
MAXLEN = 32768
EXPERTS = 16
QK = 576
HEADS_GROUP = 8
ROWS_DEV = 17
CAP = 7
REQUESTS = 32
PRE_TOKENS = 512
ROUTED_ROWS = 544
N_DP = 2


def prefill_pair(key):
    latent = jnp.clip(jax.random.normal(jax.random.fold_in(key, 11), (PRE_TOKENS, QK), jnp.float32), -5.0, 5.0)
    query = jnp.clip(jax.random.normal(jax.random.fold_in(key, 12), (PRE_TOKENS, HEADS, QK), jnp.float32), -5.0, 5.0)
    return (query, latent)


def draw_pre_query(key, part):
    return prefill_pair(key)[0].astype(jnp.bfloat16)


def draw_pre_latent(key, part):
    return prefill_pair(key)[1].astype(jnp.bfloat16)


def decode_lengths(key):
    bits = jax.random.randint(jax.random.fold_in(key, 21), (REQUESTS,), 1, 16)
    upper = jnp.power(2, bits) + 1
    lengths = jax.random.randint(jax.random.fold_in(key, 22), (REQUESTS,), 1, upper)
    longest = jax.random.randint(jax.random.fold_in(key, 23), (), 0, REQUESTS)
    return lengths.at[longest].set(MAXLEN).astype(jnp.int32)


def decode_latent_base(key):
    return jnp.clip(jax.random.normal(jax.random.fold_in(key, 32), (REQUESTS, QK), jnp.float32), -5.0, 5.0)


def draw_cache_lengths(key, part):
    return decode_lengths(key)


def draw_dec_latent(key, part):
    return decode_latent_base(key).astype(jnp.bfloat16)


def draw_dec_query(key, part):
    query = jnp.clip(jax.random.normal(jax.random.fold_in(key, 33), (REQUESTS, HEADS, QK), jnp.float32), -5.0, 5.0)
    return query.astype(jnp.bfloat16)


def draw_latent_cache(key, part):
    return jnp.clip(jax.random.normal(jax.random.fold_in(key, 42), (REQUESTS, WINDOW, QK), jnp.float32), -5.0, 5.0).astype(jnp.bfloat16)


def block_levels(key, extent, pieces, smallest, high):
    gain = 1.0
    for axis_at, blocks in pieces:
        heights = jax.random.uniform(jax.random.fold_in(jax.random.fold_in(key, 6), axis_at), (blocks,), jnp.float32, smallest / len(pieces), high / len(pieces))
        gain = gain * jnp.repeat(jnp.exp(heights), extent[axis_at] // blocks).reshape((-1,) + (1,) * (len(extent) - 1 - axis_at))
    return gain


def routed_block(key, own, number, rows, number_of, top, bound, slope):
    sequence = jax.random.permutation(key, number_of)
    packed, ordinary = shares(number_of, rows * top, bound, slope, True), shares(number_of, rows * top, bound, slope, False)
    places = jnp.arange(number_of)

    def named(sizes, offset_by):
        used = int((sizes > 0).sum())
        fixed = max(1, used // 4)
        shifted = fixed + (places - fixed + offset_by * (used - fixed)) % max(1, number_of - fixed)
        return jnp.zeros((number_of,), jnp.int32).at[sequence[jnp.where(places < fixed, places, shifted)]].set(jnp.asarray(sizes, jnp.int32))

    sizes = jnp.where(number % 4 == 0, named(packed, number // 4), named(ordinary, number - number // 4 - 1))
    mixed = jax.random.permutation(jax.random.fold_in(own, 3), number_of)
    donor, taker = mixed[0:number_of // 2 * 2:2], mixed[1:number_of // 2 * 2:2]
    slack = jnp.minimum(sizes[donor] - 1, bound - sizes[taker]) // 2
    slack = jnp.where((donor == sequence[0]) | (taker == sequence[0]) | (sizes[taker] == 0), 0, jnp.maximum(slack, 0))
    shifted = jax.random.randint(jax.random.fold_in(own, 4), (number_of // 2,), 0, 1 << 20) % (slack + 1)
    sizes = sizes.at[donor].add(-shifted).at[taker].add(shifted)
    members = jnp.searchsorted(jnp.cumsum(sizes), jnp.arange(rows * top), side="right").astype(jnp.int32)
    listing = members.reshape(top, rows).T
    listing = listing[jax.random.permutation(jax.random.fold_in(own, 1), rows)]
    offset_by = jax.random.randint(jax.random.fold_in(own, 2), (rows, 1), 0, top)
    return jnp.take_along_axis(listing, (jnp.arange(top)[None, :] + offset_by) % top, axis=1)


def shares(count, total, bound, lean, full):
    portions = [(1 << 20) // math.isqrt(grade ** lean) + 1 for grade in range(1, count + 1)]
    largest = bound if full else min(bound, max(-(-total // count), total * portions[0] // sum(portions)))
    least = 1 if total - largest >= count - 1 else 0
    given, surplus = [largest] + [least] * (count - 1), total - largest - least * (count - 1)
    while surplus > 0:
        movable = [i for i in range(1, count) if given[i] < largest] or [i for i in range(1, count) if given[i] < bound]
        mass, left = sum([portions[i] for i in movable]), surplus
        for i in movable:
            addition = min(bound - given[i], max(1, left * portions[i] // mass), surplus)
            given[i] = given[i] + addition
            surplus = surplus - addition
    return np.array(given)


def centred(stream_key, dims, deviation, limit, shards=(), kind=jnp.bfloat16):
    level = block_levels(stream_key, dims, shards, -0.22, 0.18) if shards else 1.0
    result = jax.random.normal(stream_key, dims, jnp.float32) * deviation * level
    return jnp.minimum(jnp.maximum(result, -limit), limit).astype(kind)


def setup_inputs(seed: int = 0) -> dict:
    key_list = jax.random.split(jax.random.key(seed), 21)
    pre_query = draw_pre_query(jax.random.fold_in(key_list[20], 71), 0)
    pre_latent = draw_pre_latent(jax.random.fold_in(key_list[20], 71), 0)
    pre_resid = centred(key_list[2], (PRE_TOKENS, D), 1.0, 6.0, ((0, 32),))
    dec_query = draw_dec_query(jax.random.fold_in(key_list[20], 71), 0)
    dec_latent = draw_dec_latent(jax.random.fold_in(key_list[20], 71), 0)
    dec_resid = centred(key_list[5], (REQUESTS, D), 1.0, 6.0, ((0, 32),))
    cache_lengths = draw_cache_lengths(jax.random.fold_in(key_list[20], 71), 0)
    latent_cache = draw_latent_cache(jax.random.fold_in(key_list[20], 71), 0)
    sink_logits = jnp.clip(jax.random.uniform(key_list[8], (HEADS,), jnp.float32, -1.0, 3.0), -1.0, 3.0)
    uv_weight = centred(key_list[9], (HEADS, LATENT, VDIM), LATENT ** -0.5, 0.25, ((0, 2), (1, 16)))
    out_weight = centred(key_list[10], (HEADS, VDIM, D), (HEADS * VDIM) ** -0.5, 0.125, ((0, 2), (1, 16)))
    norm_gain = jnp.clip(1.0 + 0.1 * jax.random.normal(key_list[11], (D,), jnp.float32), 0.5, 1.5).astype(jnp.bfloat16)
    router = centred(key_list[12], (D, EXPERTS), D ** -0.5, 0.125, ((1, 16),))
    routes_keys = jax.random.split(jax.random.fold_in(key_list[13], 1), ROUTED_ROWS // ROWS_DEV)
    routes_turns = jax.random.permutation(jax.random.fold_in(key_list[13], 3), ROUTED_ROWS // ROWS_DEV)
    routes = jax.vmap(lambda own, number: routed_block(jax.random.fold_in(key_list[13], 2), own, number, ROWS_DEV, EXPERTS, TOPK, CAP, 2))(routes_keys, routes_turns).reshape((ROUTED_ROWS, TOPK))
    gate_weight = centred(key_list[14], (EXPERTS, D, MOE_FF), D ** -0.5, 0.125, ((0, 16), (2, 2)))
    up_weight = centred(key_list[15], (EXPERTS, D, MOE_FF), D ** -0.5, 0.125, ((0, 16), (2, 2)))
    down_weight = centred(key_list[16], (EXPERTS, MOE_FF, D), MOE_FF ** -0.5, 0.15625, ((0, 16), (2, 2)))
    shared_gate = centred(key_list[17], (D, SHARED_FF), D ** -0.5, 0.125, ((0, 16), (1, 2)))
    shared_up = centred(key_list[18], (D, SHARED_FF), D ** -0.5, 0.125, ((0, 16), (1, 2)))
    shared_down = centred(key_list[19], (SHARED_FF, D), SHARED_FF ** -0.5, 0.15625, ((0, 16), (1, 2)))
    return {"pre_query": pre_query, "pre_latent": pre_latent, "pre_resid": pre_resid, "dec_query": dec_query, "dec_latent": dec_latent, "dec_resid": dec_resid, "cache_lengths": cache_lengths, "latent_cache": latent_cache, "sink_logits": sink_logits, "uv_weight": uv_weight, "out_weight": out_weight, "norm_gain": norm_gain, "router": router, "routes": routes, "gate_weight": gate_weight, "up_weight": up_weight, "down_weight": down_weight, "shared_gate": shared_gate, "shared_up": shared_up, "shared_down": shared_down}


ROUTE_SCALE = 2.446
NORM_EPS = 1e-06
NEG_FILL = -1e+30
PRECISE = lax.Precision.HIGHEST

def rounded(value):
    return lax.optimization_barrier(value.astype(jnp.bfloat16)).astype(jnp.float32)

def attend_span(operands, sinks):
    query, latent = operands
    scale_qk = (QK_NOPE + ROPE) ** (-0.5)
    scores = jnp.einsum('thc,uc->thu', query.astype(jnp.float32), latent.astype(jnp.float32), precision=PRECISE) * scale_qk
    places = jnp.arange(SPAN, dtype=jnp.int32)
    allowed = (places[None, :] <= places[:, None])[:, None, :]
    masked = jnp.where(allowed, scores, NEG_FILL)
    row_max = jnp.maximum(lax.optimization_barrier(jnp.max(masked, axis=2)), sinks[None, :])
    exp_terms = jnp.where(allowed, jnp.exp(masked - row_max[:, :, None]), 0.0)
    denominator = lax.optimization_barrier(jnp.sum(exp_terms, axis=2)) + jnp.exp(sinks[None, :] - row_max)
    numerator = jnp.einsum('thu,ul->thl', rounded(exp_terms), latent[:, :LATENT].astype(jnp.float32), precision=PRECISE)
    return (numerator / denominator[:, :, None]).astype(jnp.bfloat16)

def attend_request(operands, sinks):
    query, cache_rows, own_key, length = operands
    scale_qk = (QK_NOPE + ROPE) ** (-0.5)
    slot_ids = jnp.arange(WINDOW, dtype=jnp.int32)
    newest = length - 1
    position = newest - jnp.mod(newest - slot_ids, WINDOW)
    usable = (position >= 0) & (position > length - WINDOW)
    usable = jnp.concatenate([usable, jnp.arange(1, dtype=jnp.int32) >= 0])
    keys = jnp.concatenate([cache_rows, own_key[None, :]], axis=0)
    scores = jnp.einsum('hc,uc->hu', query.astype(jnp.float32), keys.astype(jnp.float32), precision=PRECISE) * scale_qk
    masked = jnp.where(usable[None, :], scores, NEG_FILL)
    row_max = jnp.maximum(lax.optimization_barrier(jnp.max(masked, axis=1)), sinks)
    exp_terms = jnp.where(usable[None, :], jnp.exp(masked - row_max[:, None]), 0.0)
    denominator = lax.optimization_barrier(jnp.sum(exp_terms, axis=1)) + jnp.exp(sinks - row_max)
    numerator = jnp.einsum('hu,ul->hl', rounded(exp_terms), keys[:, :LATENT].astype(jnp.float32), precision=PRECISE)
    return (numerator / denominator[:, None]).astype(jnp.bfloat16)

def project(attention, uv_weight, out_weight):
    head_values = jnp.einsum('thl,hlv->thv', attention.astype(jnp.float32), uv_weight.astype(jnp.float32), precision=PRECISE).astype(jnp.bfloat16)
    summed = jnp.zeros((attention.shape[0], D), jnp.float32)
    for block in range(N_DP):
        lower = block * HEADS_GROUP
        partial_sum = jnp.einsum('thv,hvd->td', head_values[:, lower:lower + HEADS_GROUP].astype(jnp.float32), out_weight[lower:lower + HEADS_GROUP].astype(jnp.float32), precision=PRECISE)
        summed = summed + rounded(partial_sum)
    return summed

def normalize(hidden, norm_gain):
    hidden_up = hidden.astype(jnp.float32)
    mean_square = lax.optimization_barrier(jnp.mean(hidden_up * hidden_up, axis=1, keepdims=True))
    return (hidden_up * lax.rsqrt(mean_square + NORM_EPS) * norm_gain.astype(jnp.float32)[None, :]).astype(jnp.bfloat16)

def reference(pre_query, pre_latent, pre_resid, dec_query, dec_latent, dec_resid, cache_lengths, latent_cache, sink_logits, uv_weight, out_weight, norm_gain, router, routes, gate_weight, up_weight, down_weight, shared_gate, shared_up, shared_down):
    sinks = sink_logits.astype(jnp.float32)
    pre_att = lax.map(partial(attend_span, sinks=sinks), (pre_query.reshape(REQUESTS, SPAN, HEADS, QK), pre_latent.reshape(REQUESTS, SPAN, QK)))
    pre_att = pre_att.reshape(PRE_TOKENS, HEADS, LATENT)
    dec_att = lax.map(partial(attend_request, sinks=sinks), (dec_query, latent_cache, dec_latent, cache_lengths.astype(jnp.int32)))
    pre_hidden = (pre_resid.astype(jnp.float32) + project(pre_att, uv_weight, out_weight)).astype(jnp.bfloat16)
    dec_hidden = (dec_resid.astype(jnp.float32) + project(dec_att, uv_weight, out_weight)).astype(jnp.bfloat16)
    hidden_rows = jnp.concatenate([pre_hidden.reshape(REQUESTS, SPAN, D), dec_hidden.reshape(REQUESTS, 1, D)], axis=1).reshape(ROUTED_ROWS, D)
    normed_rows = normalize(hidden_rows, norm_gain)
    expert_ids = routes.reshape(-1).astype(jnp.int32)
    assignments = expert_ids.shape[0]
    order = jnp.argsort(expert_ids, stable=True).astype(jnp.int32)
    counts = lax.optimization_barrier(jnp.sum((expert_ids[:, None] == jnp.arange(EXPERTS, dtype=jnp.int32)[None, :]).astype(jnp.int32), axis=0))
    starts = jnp.cumsum(counts) - counts
    inverse = jnp.zeros((assignments,), jnp.int32).at[order].set(jnp.arange(assignments, dtype=jnp.int32))
    ranks = inverse - starts[expert_ids]
    most_rows = REQUESTS * CAP

    def run_expert(expert_index):
        picks = jnp.clip(starts[expert_index] + jnp.arange(most_rows, dtype=jnp.int32), 0, assignments - 1)
        token_index = order[picks] // TOPK
        rows = normed_rows[token_index]
        gate_proj = jnp.dot(rows, gate_weight[expert_index], preferred_element_type=jnp.float32)
        up_proj = jnp.dot(rows, up_weight[expert_index], preferred_element_type=jnp.float32)
        activation = (jax.nn.silu(gate_proj) * up_proj).astype(jnp.bfloat16)
        return jnp.dot(activation, down_weight[expert_index], preferred_element_type=jnp.float32).astype(jnp.bfloat16)
    outputs = lax.map(run_expert, jnp.arange(EXPERTS, dtype=jnp.int32))
    chosen = outputs[expert_ids, ranks].reshape(ROUTED_ROWS, TOPK, D)
    logits = jnp.dot(normed_rows, router, preferred_element_type=jnp.float32)
    scores = jax.nn.sigmoid(jnp.take_along_axis(logits, routes.astype(jnp.int32), axis=1))
    route_weight = ROUTE_SCALE * scores / lax.optimization_barrier(jnp.sum(scores, axis=1, keepdims=True))
    shared_act = (jax.nn.silu(jnp.dot(normed_rows, shared_gate, preferred_element_type=jnp.float32)) * jnp.dot(normed_rows, shared_up, preferred_element_type=jnp.float32)).astype(jnp.bfloat16)
    shared_out = jnp.dot(shared_act, shared_down, preferred_element_type=jnp.float32).astype(jnp.bfloat16)
    moe_sum = shared_out.astype(jnp.float32) + lax.optimization_barrier(jnp.sum(route_weight[:, :, None] * chosen.astype(jnp.float32), axis=1))
    final_rows = (hidden_rows.astype(jnp.float32) + moe_sum).astype(jnp.bfloat16).reshape(REQUESTS, ROWS_DEV, D)
    pre_out = final_rows[:, :SPAN].reshape(PRE_TOKENS, D)
    dec_out = final_rows[:, SPAN]
    return (pre_out, dec_out)
```

```python
from functools import partial

import jax
import jax.numpy as jnp
from jax import lax
from jax.sharding import PartitionSpec as P

D = 2048
LATENT = 512
ROPE = 64
QK_NOPE = 128
TOPK = 6


ROUTE_SCALE = 2.446
NORM_EPS = 1e-06
NEG_FILL = -1e30


def assign_slots(route_rows, experts):
    flat_routes = route_rows.reshape(-1)
    one_hot = (flat_routes[:, None] == jnp.arange(experts, dtype=jnp.int32)[None, :]).astype(
        jnp.int32
    )
    running = jnp.cumsum(one_hot, axis=0)
    slot_rank = jnp.sum(running * one_hot, axis=1) - 1
    return slot_rank.reshape(route_rows.shape)


def dispatch_matrix(route_rows, slot_rows, experts, capacity):
    target = route_rows * capacity + slot_rows
    places = jnp.arange(experts * capacity, dtype=jnp.int32)
    total = jnp.zeros((route_rows.shape[0], experts * capacity), jnp.bfloat16)
    for column in range(route_rows.shape[1]):
        total = total + (target[:, column][:, None] == places[None, :]).astype(jnp.bfloat16)
    return total


def shards(
    pre_query,
    pre_latent,
    pre_resid,
    dec_query,
    dec_latent,
    dec_resid,
    cache_lengths,
    latent_cache,
    sink_logits,
    uv_weight,
    out_weight,
    norm_gain,
    router,
    routes,
    gate_weight,
    up_weight,
    down_weight,
    shared_gate,
    shared_up,
    shared_down,
):
    groups = lax.axis_size("dp")
    members = lax.axis_size("expert")
    pre_rows = pre_query.shape[0]
    rows_dev = pre_rows + 1
    scale_qk = (QK_NOPE + ROPE) ** (-0.5)
    pre_scores = (
        jnp.einsum("thc,uc->thu", pre_query, pre_latent, preferred_element_type=jnp.float32)
        * scale_qk
    )
    places = jnp.arange(pre_rows, dtype=jnp.int32)
    allowed = (places[None, :] <= places[:, None])[:, None, :]
    masked = jnp.where(allowed, pre_scores, NEG_FILL)
    pre_max = jnp.maximum(jnp.max(masked, axis=2), sink_logits[None, :])
    exp_terms = jnp.where(allowed, jnp.exp(masked - pre_max[:, :, None]), 0.0)
    denominator = jnp.sum(exp_terms, axis=2) + jnp.exp(sink_logits[None, :] - pre_max)
    numerator = jnp.einsum(
        "thu,ul->thl",
        exp_terms.astype(jnp.bfloat16),
        pre_latent[:, :LATENT],
        preferred_element_type=jnp.float32,
    )
    pre_att = (numerator / denominator[:, :, None]).astype(jnp.bfloat16)
    window = latent_cache.shape[1]
    slot_ids = jnp.arange(window, dtype=jnp.int32)
    newest = cache_lengths - 1
    position = newest[:, None] - jnp.mod(newest[:, None] - slot_ids[None, :], window)
    usable = ((position >= 0) & (position > cache_lengths[:, None] - window))[:, None, :]
    cache_scores = (
        jnp.einsum("rhc,rsc->rhs", dec_query, latent_cache, preferred_element_type=jnp.float32)
        * scale_qk
    )
    own_scores = (
        jnp.einsum("rhc,rc->rh", dec_query, dec_latent, preferred_element_type=jnp.float32)
        * scale_qk
    )
    cache_masked = jnp.where(usable, cache_scores, NEG_FILL)
    top_score = jnp.maximum(
        jnp.maximum(jnp.max(cache_masked, axis=2), own_scores), sink_logits[None, :]
    )
    cache_exp = jnp.where(usable, jnp.exp(cache_masked - top_score[:, :, None]), 0.0)
    own_exp = jnp.exp(own_scores - top_score)
    dec_numer = jnp.einsum(
        "rhs,rsl->rhl",
        cache_exp.astype(jnp.bfloat16),
        latent_cache[:, :, :LATENT],
        preferred_element_type=jnp.float32,
    )
    dec_numer = dec_numer + own_exp.astype(jnp.bfloat16).astype(jnp.float32)[
        :, :, None
    ] * dec_latent[:, None, :LATENT].astype(jnp.float32)
    dec_total = jnp.sum(cache_exp, axis=2) + own_exp + jnp.exp(sink_logits[None, :] - top_score)
    dec_att = (dec_numer / dec_total[:, :, None]).astype(jnp.bfloat16)
    attention = jnp.concatenate([pre_att, dec_att], axis=0)
    spread = lax.all_to_all(attention, "dp", split_axis=1, concat_axis=0, tiled=True)
    uv_full, out_full = (
        lax.all_gather(uv_weight, "expert", axis=1, tiled=True),
        lax.all_gather(out_weight, "expert", axis=1, tiled=True),
    )
    head_values = jnp.einsum(
        "thl,hlv->thv", spread, uv_full, preferred_element_type=jnp.float32
    ).astype(jnp.bfloat16)
    head_partial = jnp.einsum(
        "thv,hvd->td", head_values, out_full, preferred_element_type=jnp.float32
    )
    attn_out = lax.psum_scatter(
        head_partial.astype(jnp.bfloat16), "dp", scatter_dimension=0, tiled=True
    ).astype(jnp.float32)
    resid = jnp.concatenate([pre_resid, dec_resid], axis=0)
    hidden = (resid.astype(jnp.float32) + attn_out).astype(jnp.bfloat16)
    hidden_up = lax.optimization_barrier(hidden).astype(jnp.float32)
    mean_square = jnp.mean(hidden_up * hidden_up, axis=1, keepdims=True)
    normed = (
        hidden_up * lax.rsqrt(mean_square + NORM_EPS) * norm_gain.astype(jnp.float32)[None, :]
    ).astype(jnp.bfloat16)
    capacity = max(2, (rows_dev * TOPK + members - 1) // members)
    group_tokens = lax.all_gather(normed, "dp", axis=0, tiled=True)
    group_routes = lax.all_gather(routes, "dp", axis=0, tiled=True)
    routes_by_group = group_routes.reshape(groups, rows_dev, TOPK)
    slots_by_group = jax.vmap(partial(assign_slots, experts=members))(routes_by_group)
    tokens_by_group = group_tokens.reshape(groups, rows_dev, D)
    all_matrix = jax.vmap(partial(dispatch_matrix, experts=members, capacity=capacity))(
        routes_by_group, slots_by_group
    )
    all_matrix = all_matrix.reshape(groups, rows_dev, members, capacity)
    outgoing = jnp.einsum(
        "grxc,grd->xgcd", all_matrix, tokens_by_group, preferred_element_type=jnp.bfloat16
    )
    expert_rows = lax.all_to_all(outgoing, "expert", split_axis=0, concat_axis=0, tiled=True)
    expert_rows = expert_rows.reshape(-1, D)
    gate_score = jax.nn.sigmoid(
        jnp.dot(expert_rows, router[:, 0], preferred_element_type=jnp.float32)
    )
    gate_proj = jnp.dot(expert_rows, gate_weight[0], preferred_element_type=jnp.float32)
    up_proj = jnp.dot(expert_rows, up_weight[0], preferred_element_type=jnp.float32)
    expert_act = (jax.nn.silu(gate_proj) * up_proj).astype(jnp.bfloat16)
    shared_gate_full, shared_up_full, shared_down_full = (
        lax.all_gather(shared_gate, "expert", axis=0, tiled=True),
        lax.all_gather(shared_up, "expert", axis=0, tiled=True),
        lax.all_gather(shared_down, "expert", axis=0, tiled=True),
    )
    shared_act = (
        jax.nn.silu(jnp.dot(group_tokens, shared_gate_full, preferred_element_type=jnp.float32))
        * jnp.dot(group_tokens, shared_up_full, preferred_element_type=jnp.float32)
    ).astype(jnp.bfloat16)
    down_local = down_weight[0]
    col_width = down_local.shape[1]
    routed_piece = lax.all_gather(expert_act, "dp", axis=1, tiled=True)
    shared_piece = lax.all_gather(shared_act, "dp", axis=1, tiled=True)
    routed_cols = jnp.dot(routed_piece, down_local, preferred_element_type=jnp.float32)
    shared_cols = jnp.dot(shared_piece, shared_down_full, preferred_element_type=jnp.float32)
    expert_out = routed_cols.astype(jnp.bfloat16)
    shared_out = shared_cols.astype(jnp.bfloat16)
    returned = lax.all_to_all(
        expert_out.reshape(members, groups * capacity, col_width),
        "expert",
        split_axis=0,
        concat_axis=0,
        tiled=True,
    )
    returned_scores = lax.all_to_all(
        gate_score.reshape(members, groups * capacity),
        "expert",
        split_axis=0,
        concat_axis=0,
        tiled=True,
    )
    group_offset = (jnp.arange(groups, dtype=jnp.int32) * capacity)[:, None, None]
    lookup = (routes_by_group * (groups * capacity) + group_offset + slots_by_group).reshape(
        groups * rows_dev, TOPK
    )
    picked = jnp.take(returned.reshape(-1, col_width), lookup, axis=0)
    picked_scores = jnp.take(returned_scores.reshape(-1), lookup, axis=0)
    route_weight = ROUTE_SCALE * picked_scores / jnp.sum(picked_scores, axis=1, keepdims=True)
    moe_cols = shared_out.astype(jnp.float32) + jnp.sum(
        route_weight[:, :, None] * picked.astype(jnp.float32), axis=1
    )
    moe_home = lax.all_to_all(
        moe_cols.reshape(groups, rows_dev, col_width).astype(jnp.bfloat16),
        "dp",
        split_axis=0,
        concat_axis=2,
        tiled=True,
    ).astype(jnp.float32)
    final = (hidden_up + moe_home[0]).astype(jnp.bfloat16)
    return (final[:pre_rows], final[pre_rows:])


OUTER = 4
DEC_ROWS = 16


def fold_row(row):
    return row.reshape(row.shape[:-2] + (DEC_ROWS, row.shape[-1] // DEC_ROWS))


def unfold_row(block):
    return block.reshape(block.shape[:-2] + (block.shape[-2] * block.shape[-1],))


def swap(value, axis, bit):
    size = lax.axis_size(axis)
    return lax.ppermute(value, axis, [(i, i ^ bit) for i in range(size)])


def attention_rows(
    pre_query, pre_latent, dec_query, dec_latent, cache_lengths, latent_cache, sink_logits
):
    pre_rows = pre_query.shape[0]
    scale_qk = (QK_NOPE + ROPE) ** (-0.5)
    pre_scores = (
        jnp.einsum("thc,uc->thu", pre_query, pre_latent, preferred_element_type=jnp.float32)
        * scale_qk
    )
    places = jnp.arange(pre_rows, dtype=jnp.int32)
    allowed = (places[None, :] <= places[:, None])[:, None, :]
    masked = jnp.where(allowed, pre_scores, NEG_FILL)
    pre_max = jnp.maximum(jnp.max(masked, axis=2), sink_logits[None, :])
    exp_terms = jnp.where(allowed, jnp.exp(masked - pre_max[:, :, None]), 0.0)
    denominator = jnp.sum(exp_terms, axis=2) + jnp.exp(sink_logits[None, :] - pre_max)
    numerator = jnp.einsum(
        "thu,ul->thl",
        exp_terms.astype(jnp.bfloat16),
        pre_latent[:, :LATENT],
        preferred_element_type=jnp.float32,
    )
    pre_att = (numerator / denominator[:, :, None]).astype(jnp.bfloat16)
    window = latent_cache.shape[1]
    slot_ids = jnp.arange(window, dtype=jnp.int32)
    newest = cache_lengths - 1
    position = newest[:, None] - jnp.mod(newest[:, None] - slot_ids[None, :], window)
    usable = ((position >= 0) & (position > cache_lengths[:, None] - window))[:, None, :]
    cache_scores = (
        jnp.einsum("rhc,rsc->rhs", dec_query, latent_cache, preferred_element_type=jnp.float32)
        * scale_qk
    )
    own_scores = (
        jnp.einsum("rhc,rc->rh", dec_query, dec_latent, preferred_element_type=jnp.float32)
        * scale_qk
    )
    cache_masked = jnp.where(usable, cache_scores, NEG_FILL)
    top_score = jnp.maximum(
        jnp.maximum(jnp.max(cache_masked, axis=2), own_scores), sink_logits[None, :]
    )
    cache_exp = jnp.where(usable, jnp.exp(cache_masked - top_score[:, :, None]), 0.0)
    own_exp = jnp.exp(own_scores - top_score)
    dec_numer = jnp.einsum(
        "rhs,rsl->rhl",
        cache_exp.astype(jnp.bfloat16),
        latent_cache[:, :, :LATENT],
        preferred_element_type=jnp.float32,
    )
    dec_numer = dec_numer + own_exp.astype(jnp.bfloat16).astype(jnp.float32)[
        :, :, None
    ] * dec_latent[:, None, :LATENT].astype(jnp.float32)
    dec_total = jnp.sum(cache_exp, axis=2) + own_exp + jnp.exp(sink_logits[None, :] - top_score)
    dec_att = (dec_numer / dec_total[:, :, None]).astype(jnp.bfloat16)
    return pre_att, dec_att


def normalize(hidden, norm_gain):
    hidden_up = hidden.astype(jnp.float32)
    mean_square = jnp.mean(hidden_up * hidden_up, axis=1, keepdims=True)
    return (
        hidden_up * lax.rsqrt(mean_square + NORM_EPS) * norm_gain.astype(jnp.float32)[None, :]
    ).astype(jnp.bfloat16)


def token_shards(
    pre_query,
    pre_latent,
    pre_resid,
    dec_query,
    dec_latent,
    dec_resid,
    cache_lengths,
    latent_cache,
    sink_logits,
    uv_weight,
    out_weight,
    norm_gain,
    router,
    routes,
    gate_weight,
    up_weight,
    down_weight,
    shared_gate,
    shared_up,
    shared_down,
):
    groups = lax.axis_size("dp")
    members = lax.axis_size("expert")
    inner = members // OUTER
    homes = groups * members
    me = lax.axis_index("expert")
    my_group = lax.axis_index("dp")
    my_outer = me // inner
    pre_rows = pre_query.shape[0]
    rows_dev = pre_rows + 1
    capacity = max(2, (rows_dev * TOPK + members - 1) // members)

    heads_dev, latent_rows, value_dim = uv_weight.shape
    value_rows = out_weight.shape[1]
    heads_outer = heads_dev // OUTER
    out_blocks = out_weight.reshape(OUTER, heads_outer * value_rows, D)
    uv_tiles = heads_outer * latent_rows // DEC_ROWS
    uv_blocks = (
        uv_weight.reshape(OUTER, uv_tiles, DEC_ROWS, value_dim)
        .transpose(0, 2, 1, 3)
        .reshape(OUTER, DEC_ROWS, uv_tiles * value_dim)
    )
    router_block = router[:, 0].reshape(DEC_ROWS, D // DEC_ROWS)
    routes_low = routes.astype(jnp.bfloat16)
    routes_block = jnp.concatenate(
        [
            routes_low[:pre_rows],
            jnp.broadcast_to(routes_low[pre_rows:], (pre_rows, TOPK)),
            jnp.zeros((pre_rows, 128 - 2 * TOPK), jnp.bfloat16),
        ],
        axis=1,
    )
    side = jnp.concatenate([router_block, routes_block], axis=1)
    packed = jnp.concatenate(
        [out_blocks, uv_blocks, jnp.broadcast_to(side[None], (OUTER,) + side.shape)], axis=2
    )
    pieces = [lax.dynamic_index_in_dim(packed, my_outer, 0, keepdims=True)]
    for step in range(1, OUTER):
        block = lax.dynamic_index_in_dim(packed, my_outer ^ step, 0, keepdims=True)
        pieces.append(swap(block, "expert", step * inner))
    gathered = jnp.concatenate(pieces, axis=0)
    chain = [step * inner for step in range(OUTER)]
    bit = inner // 2
    while bit:
        gathered = jnp.concatenate([gathered, swap(gathered, "expert", bit)], axis=0)
        chain = chain + [offset | bit for offset in chain]
        bit //= 2
    chain_array = jnp.array(chain, jnp.int32)
    holders = me ^ chain_array
    out_rel = gathered[:, :, :D].reshape(heads_outer * members * value_rows, D)
    uv_rel = (
        gathered[:, :, D : D + uv_tiles * value_dim]
        .reshape(members, DEC_ROWS, heads_outer, latent_rows // DEC_ROWS, value_dim)
        .transpose(2, 0, 3, 1, 4)
        .reshape(heads_outer, members * latent_rows, value_dim)
    )
    side_all = gathered[:, :, D + uv_tiles * value_dim :]
    router_rel = side_all[:, :, : D // DEC_ROWS].reshape(members, D)
    routes_plane = side_all[:, :, D // DEC_ROWS :]
    routes_other = swap(routes_plane, "dp", 1)
    latent_abs = jnp.arange(members * latent_rows, dtype=jnp.int32)
    latent_rel_abs = (holders[:, None] * latent_rows + jnp.arange(latent_rows)[None, :]).reshape(-1)
    latent_order = (latent_abs[:, None] == latent_rel_abs[None, :]).astype(jnp.bfloat16)
    uv_full = jnp.einsum(
        "ab,hbv->hav", latent_order, uv_rel, preferred_element_type=jnp.float32
    ).astype(jnp.bfloat16)
    value_ids = jnp.arange(heads_outer * value_dim, dtype=jnp.int32)
    wanted = (
        jnp.arange(heads_outer)[None, :, None] * value_dim
        + holders[:, None, None] * value_rows
        + jnp.arange(value_rows)[None, None, :]
    ).reshape(-1)
    value_order = (value_ids[:, None] == wanted[None, :]).astype(jnp.bfloat16)

    units = shared_gate.shape[1] // members
    depth = shared_gate.shape[0]
    shared_cols = jnp.stack(
        [shared_gate.T.reshape(members, units, depth), shared_up.T.reshape(members, units, depth)],
        axis=1,
    )
    shared_got = lax.all_to_all(shared_cols, "expert", split_axis=0, concat_axis=0, tiled=True)
    shared_in = shared_got.transpose(1, 2, 0, 3).reshape(2, units, members * depth)
    half = members // 2
    low = me < half
    first, second = shared_down[:units], shared_down[units:]
    down_a = lax.ppermute(
        jnp.where(low, first, second),
        "expert",
        [(i, 2 * i if i < half else 2 * (i - half) + 1) for i in range(members)],
    )
    down_b = lax.ppermute(
        jnp.where(low, second, first),
        "expert",
        [(i, 2 * i + 1 if i < half else 2 * (i - half)) for i in range(members)],
    )
    mine_first = (me % 2) == my_group
    shared_down_own = jnp.where(mine_first, down_a, down_b)
    shared_down_other = jnp.where(mine_first, down_b, down_a)

    pre_att, dec_att = attention_rows(
        pre_query, pre_latent, dec_query, dec_latent, cache_lengths, latent_cache, sink_logits
    )
    peers = groups * OUTER
    heads_block = heads_outer * LATENT
    att_blocks = jnp.concatenate(
        [
            pre_att.reshape(pre_rows, peers, heads_block).transpose(1, 0, 2),
            fold_row(dec_att.reshape(peers, 1, heads_block)),
        ],
        axis=2,
    )
    lines = [
        [g * members + o * inner + i for g in range(groups) for o in range(OUTER)]
        for i in range(inner)
    ]
    both = ("dp", "expert")
    att_got = lax.all_to_all(
        att_blocks, both, split_axis=0, concat_axis=0, axis_index_groups=lines, tiled=True
    )
    att_rows = jnp.concatenate(
        [
            att_got[:, :, :heads_block].reshape(peers * pre_rows, heads_block),
            unfold_row(att_got[:, :, heads_block:]),
        ],
        axis=0,
    )
    head_values = jnp.concatenate(
        [
            jnp.dot(
                att_rows[:, h * LATENT : (h + 1) * LATENT],
                uv_full[h],
                preferred_element_type=jnp.float32,
            ).astype(jnp.bfloat16)
            for h in range(heads_outer)
        ],
        axis=1,
    )
    head_values = jnp.dot(
        head_values, value_order, preferred_element_type=jnp.float32
    ).astype(jnp.bfloat16)
    head_partial = jnp.dot(head_values, out_rel, preferred_element_type=jnp.float32).astype(
        jnp.bfloat16
    )
    split = peers * pre_rows
    partial_blocks = jnp.concatenate(
        [
            head_partial[:split].reshape(peers, pre_rows, D),
            fold_row(head_partial[split:].reshape(peers, 1, D)),
        ],
        axis=2,
    )
    partial_got = lax.all_to_all(
        partial_blocks, both, split_axis=0, concat_axis=0, axis_index_groups=lines, tiled=True
    )
    attn_out = jnp.sum(partial_got.astype(jnp.float32), axis=0)
    pre_hidden = (pre_resid.astype(jnp.float32) + attn_out[:, :D]).astype(jnp.bfloat16)
    dec_hidden = (
        dec_resid.astype(jnp.float32) + unfold_row(attn_out[:, D:])[None, :]
    ).astype(jnp.bfloat16)
    pre_hidden = lax.optimization_barrier(pre_hidden)
    dec_hidden = lax.optimization_barrier(dec_hidden)
    normed = jnp.concatenate(
        [normalize(pre_hidden, norm_gain), fold_row(normalize(dec_hidden, norm_gain))], axis=1
    )

    blocks = [normed] + [swap(normed, "expert", step * inner) for step in range(1, OUTER)]
    tags = [(0, step * inner) for step in range(OUTER)]
    middle = OUTER // 2
    bits = []
    bit = inner // 2
    while bit:
        bits.append(bit)
        bit //= 2

    def widen(value, names, group_bit, member_bit):
        if group_bit:
            other = swap(value, "dp", 1)
        else:
            other = swap(value, "expert", member_bit)
        return (
            jnp.concatenate([value, other], axis=0),
            names + [(g ^ group_bit, m ^ member_bit) for g, m in names],
        )

    half_a, tags_a = jnp.concatenate(blocks[:middle], axis=0), tags[:middle]
    half_b, tags_b = jnp.concatenate(blocks[middle:], axis=0), tags[middle:]
    half_a, tags_a = widen(half_a, tags_a, 0, bits[0])
    half_b, tags_b = widen(half_b, tags_b, 1, 0)
    half_a, tags_a = widen(half_a, tags_a, 1, 0)
    half_b, tags_b = widen(half_b, tags_b, 0, bits[0])
    rows_all, tags = jnp.concatenate([half_a, half_b], axis=0), tags_a + tags_b
    for bit in bits[1:]:
        rows_all, tags = widen(rows_all, tags, 0, bit)
    pre_total = homes * pre_rows
    tokens = jnp.concatenate(
        [
            rows_all[:, :D],
            unfold_row(rows_all[:, D:].reshape(homes, DEC_ROWS, D // DEC_ROWS)),
        ],
        axis=0,
    )
    total = pre_total + homes

    positions = [g * members + chain.index(m) for g, m in tags]
    routes_all = jnp.concatenate([routes_plane, routes_other], axis=0)
    routes_all = jnp.concatenate([routes_all[p : p + 1] for p in positions], axis=0)
    token_routes = jnp.concatenate(
        [
            routes_all[:, :, :TOPK].reshape(pre_total, TOPK),
            routes_all[:, 0, TOPK : 2 * TOPK],
        ],
        axis=0,
    ).astype(jnp.int32)
    chosen = jnp.sum(
        (token_routes[:, :, None] == holders[None, None, :]).astype(jnp.float32), axis=1
    )
    mine = chosen[:, 0]
    earlier = (
        jnp.arange(total, dtype=jnp.int32)[:, None] <= jnp.arange(total, dtype=jnp.int32)[None, :]
    ).astype(jnp.bfloat16)
    home_group = jnp.array([g for g, _ in tags], jnp.int32) ^ my_group
    home_member = jnp.array([m for _, m in tags], jnp.int32) ^ me
    home_place = (
        ((home_member ^ me) % 2) * (homes // 2) + home_group * (members // 2) + home_member // 2
    )
    place = jnp.concatenate(
        [
            (home_place[:, None] * pre_rows + jnp.arange(pre_rows)[None, :]).reshape(-1),
            pre_total + home_place,
        ]
    )
    reorder = (jnp.arange(total, dtype=jnp.int32)[:, None] == place[None, :]).astype(jnp.bfloat16)
    mine_placed = jnp.dot(reorder, mine.astype(jnp.bfloat16), preferred_element_type=jnp.float32)
    rank = jnp.dot(
        mine_placed.astype(jnp.bfloat16)[None, :], earlier, preferred_element_type=jnp.float32
    )
    slots = homes * capacity
    slot_ids = jnp.arange(1, slots + 1, dtype=jnp.float32)
    gather = ((rank == slot_ids[:, None]) & (mine_placed[None, :] > 0.0)).astype(jnp.bfloat16)
    scatter = gather.T
    select = jnp.dot(gather, reorder, preferred_element_type=jnp.float32).astype(jnp.bfloat16)

    shared_hidden = [
        lax.dot_general(
            tokens, shared_in[i], (((1,), (1,)), ((), ())), preferred_element_type=jnp.float32
        )
        for i in range(2)
    ]
    shared_act = (jax.nn.silu(shared_hidden[0]) * shared_hidden[1]).astype(jnp.bfloat16)
    shared_act = jnp.dot(reorder, shared_act, preferred_element_type=jnp.float32).astype(
        jnp.bfloat16
    )
    shared_act_other = swap(shared_act, "dp", 1)
    expert_rows = jnp.dot(select, tokens, preferred_element_type=jnp.float32).astype(jnp.bfloat16)
    scores = jax.nn.sigmoid(
        lax.dot_general(
            tokens, router_rel, (((1,), (1,)), ((), ())), preferred_element_type=jnp.float32
        )
    )
    token_weight = ROUTE_SCALE * scores[:, 0] / jnp.sum(scores * chosen, axis=1)
    slot_weight = jnp.sum(select.astype(jnp.float32) * token_weight[None, :], axis=1)
    gate_proj = jnp.dot(expert_rows, gate_weight[0], preferred_element_type=jnp.float32)
    up_proj = jnp.dot(expert_rows, up_weight[0], preferred_element_type=jnp.float32)
    expert_act = (jax.nn.silu(gate_proj) * up_proj * slot_weight[:, None]).astype(jnp.bfloat16)
    expert_act_other = swap(expert_act, "dp", 1)
    width = gate_weight.shape[2]
    down_own = lax.dynamic_slice_in_dim(down_weight[0], my_group * width, width, 0)
    down_other = lax.dynamic_slice_in_dim(down_weight[0], (1 - my_group) * width, width, 0)
    routed_cols = (
        jnp.dot(expert_act, down_own, preferred_element_type=jnp.float32)
        + jnp.dot(expert_act_other, down_other, preferred_element_type=jnp.float32)
    ).astype(jnp.bfloat16)
    cols = (
        jnp.dot(scatter, routed_cols, preferred_element_type=jnp.float32)
        + jnp.dot(shared_act, shared_down_own, preferred_element_type=jnp.float32)
        + jnp.dot(shared_act_other, shared_down_other, preferred_element_type=jnp.float32)
    )
    col_width = cols.shape[1]
    home_blocks = jnp.concatenate(
        [
            cols[:pre_total].reshape(homes, pre_rows, col_width),
            fold_row(cols[pre_total:].reshape(homes, 1, col_width)),
        ],
        axis=2,
    ).astype(jnp.bfloat16)
    kept, sent = home_blocks[: homes // 2], home_blocks[homes // 2 :]
    pair_sum = (kept.astype(jnp.float32) + swap(sent, "expert", 1).astype(jnp.float32)).astype(
        jnp.bfloat16
    )
    halves = [
        [g * members + 2 * i + b for g in range(groups) for i in range(members // 2)]
        for b in range(2)
    ]
    home_got = lax.all_to_all(
        pair_sum, both, split_axis=0, concat_axis=0, axis_index_groups=halves, tiled=True
    )
    home_sum = jnp.sum(
        home_got.reshape((groups, members // 2) + home_got.shape[1:]).astype(jnp.float32), axis=1
    )
    pre_moe = jnp.concatenate([home_sum[g, :, :col_width] for g in range(groups)], axis=1)
    dec_moe = unfold_row(home_sum[:, :, col_width:]).reshape(1, D)
    pre_out = (pre_hidden.astype(jnp.float32) + pre_moe).astype(jnp.bfloat16)
    dec_out = (dec_hidden.astype(jnp.float32) + dec_moe).astype(jnp.bfloat16)
    return (pre_out, dec_out)


def fits(mesh, heads, ff):
    groups, members = mesh.shape["dp"], mesh.shape["expert"]
    return (
        groups == 2
        and members % (2 * OUTER) == 0
        and (heads // groups) % OUTER == 0
        and ff % (groups * members) == 0
    )


def solution(mesh):
    in_specs = (
        P(("dp", "expert"), None, None),
        P(("dp", "expert"), None),
        P(("dp", "expert"), None),
        P(("dp", "expert"), None, None),
        P(("dp", "expert"), None),
        P(("dp", "expert"), None),
        P(("dp", "expert")),
        P(("dp", "expert"), None, None),
        P(),
        P("dp", "expert", None),
        P("dp", "expert", None),
        P(),
        P(None, "expert"),
        P(("dp", "expert"), None),
        P("expert", None, "dp"),
        P("expert", None, "dp"),
        P("expert", None, "dp"),
        P("expert", "dp"),
        P("expert", "dp"),
        P("expert", "dp"),
    )
    out_specs = (P(("dp", "expert"), None), P(("dp", "expert"), None))

    def layer(*args):
        plan = token_shards if fits(mesh, args[9].shape[0], args[17].shape[1]) else shards
        return jax.shard_map(
            plan, mesh=mesh, in_specs=in_specs, out_specs=out_specs, check_vma=False
        )(*args)

    return layer
```

```python
from functools import partial

import jax
import jax.numpy as jnp
from jax import lax
from jax.experimental import pallas as pl
from jax.experimental.pallas import tpu as pltpu
from jax.sharding import PartitionSpec as P

D = 2048
LATENT = 512
ROPE = 64
QK_NOPE = 128
TOPK = 6


ROUTE_SCALE = 2.446
NORM_EPS = 1e-06
NEG_FILL = -1e30


def assign_slots(route_rows, experts):
    flat_routes = route_rows.reshape(-1)
    one_hot = (flat_routes[:, None] == jnp.arange(experts, dtype=jnp.int32)[None, :]).astype(
        jnp.int32
    )
    running = jnp.cumsum(one_hot, axis=0)
    slot_rank = jnp.sum(running * one_hot, axis=1) - 1
    return slot_rank.reshape(route_rows.shape)


def dispatch_matrix(route_rows, slot_rows, experts, capacity):
    target = route_rows * capacity + slot_rows
    places = jnp.arange(experts * capacity, dtype=jnp.int32)
    total = jnp.zeros((route_rows.shape[0], experts * capacity), jnp.bfloat16)
    for column in range(route_rows.shape[1]):
        total = total + (target[:, column][:, None] == places[None, :]).astype(jnp.bfloat16)
    return total


def shards(
    pre_query,
    pre_latent,
    pre_resid,
    dec_query,
    dec_latent,
    dec_resid,
    cache_lengths,
    latent_cache,
    sink_logits,
    uv_weight,
    out_weight,
    norm_gain,
    router,
    routes,
    gate_weight,
    up_weight,
    down_weight,
    shared_gate,
    shared_up,
    shared_down,
):
    groups = lax.axis_size("dp")
    members = lax.axis_size("expert")
    pre_rows = pre_query.shape[0]
    rows_dev = pre_rows + 1
    scale_qk = (QK_NOPE + ROPE) ** (-0.5)
    pre_scores = (
        jnp.einsum("thc,uc->thu", pre_query, pre_latent, preferred_element_type=jnp.float32)
        * scale_qk
    )
    places = jnp.arange(pre_rows, dtype=jnp.int32)
    allowed = (places[None, :] <= places[:, None])[:, None, :]
    masked = jnp.where(allowed, pre_scores, NEG_FILL)
    pre_max = jnp.maximum(jnp.max(masked, axis=2), sink_logits[None, :])
    exp_terms = jnp.where(allowed, jnp.exp(masked - pre_max[:, :, None]), 0.0)
    denominator = jnp.sum(exp_terms, axis=2) + jnp.exp(sink_logits[None, :] - pre_max)
    numerator = jnp.einsum(
        "thu,ul->thl",
        exp_terms.astype(jnp.bfloat16),
        pre_latent[:, :LATENT],
        preferred_element_type=jnp.float32,
    )
    pre_att = (numerator / denominator[:, :, None]).astype(jnp.bfloat16)
    window = latent_cache.shape[1]
    slot_ids = jnp.arange(window, dtype=jnp.int32)
    newest = cache_lengths - 1
    position = newest[:, None] - jnp.mod(newest[:, None] - slot_ids[None, :], window)
    usable = ((position >= 0) & (position > cache_lengths[:, None] - window))[:, None, :]
    cache_scores = (
        jnp.einsum("rhc,rsc->rhs", dec_query, latent_cache, preferred_element_type=jnp.float32)
        * scale_qk
    )
    own_scores = (
        jnp.einsum("rhc,rc->rh", dec_query, dec_latent, preferred_element_type=jnp.float32)
        * scale_qk
    )
    cache_masked = jnp.where(usable, cache_scores, NEG_FILL)
    top_score = jnp.maximum(
        jnp.maximum(jnp.max(cache_masked, axis=2), own_scores), sink_logits[None, :]
    )
    cache_exp = jnp.where(usable, jnp.exp(cache_masked - top_score[:, :, None]), 0.0)
    own_exp = jnp.exp(own_scores - top_score)
    dec_numer = jnp.einsum(
        "rhs,rsl->rhl",
        cache_exp.astype(jnp.bfloat16),
        latent_cache[:, :, :LATENT],
        preferred_element_type=jnp.float32,
    )
    dec_numer = dec_numer + own_exp.astype(jnp.bfloat16).astype(jnp.float32)[
        :, :, None
    ] * dec_latent[:, None, :LATENT].astype(jnp.float32)
    dec_total = jnp.sum(cache_exp, axis=2) + own_exp + jnp.exp(sink_logits[None, :] - top_score)
    dec_att = (dec_numer / dec_total[:, :, None]).astype(jnp.bfloat16)
    attention = jnp.concatenate([pre_att, dec_att], axis=0)
    spread = lax.all_to_all(attention, "dp", split_axis=1, concat_axis=0, tiled=True)
    uv_full, out_full = (
        lax.all_gather(uv_weight, "expert", axis=1, tiled=True),
        lax.all_gather(out_weight, "expert", axis=1, tiled=True),
    )
    head_values = jnp.einsum(
        "thl,hlv->thv", spread, uv_full, preferred_element_type=jnp.float32
    ).astype(jnp.bfloat16)
    head_partial = jnp.einsum(
        "thv,hvd->td", head_values, out_full, preferred_element_type=jnp.float32
    )
    attn_out = lax.psum_scatter(
        head_partial.astype(jnp.bfloat16), "dp", scatter_dimension=0, tiled=True
    ).astype(jnp.float32)
    resid = jnp.concatenate([pre_resid, dec_resid], axis=0)
    hidden = (resid.astype(jnp.float32) + attn_out).astype(jnp.bfloat16)
    hidden_up = lax.optimization_barrier(hidden).astype(jnp.float32)
    mean_square = jnp.mean(hidden_up * hidden_up, axis=1, keepdims=True)
    normed = (
        hidden_up * lax.rsqrt(mean_square + NORM_EPS) * norm_gain.astype(jnp.float32)[None, :]
    ).astype(jnp.bfloat16)
    capacity = max(2, (rows_dev * TOPK + members - 1) // members)
    group_tokens = lax.all_gather(normed, "dp", axis=0, tiled=True)
    group_routes = lax.all_gather(routes, "dp", axis=0, tiled=True)
    routes_by_group = group_routes.reshape(groups, rows_dev, TOPK)
    slots_by_group = jax.vmap(partial(assign_slots, experts=members))(routes_by_group)
    tokens_by_group = group_tokens.reshape(groups, rows_dev, D)
    all_matrix = jax.vmap(partial(dispatch_matrix, experts=members, capacity=capacity))(
        routes_by_group, slots_by_group
    )
    all_matrix = all_matrix.reshape(groups, rows_dev, members, capacity)
    outgoing = jnp.einsum(
        "grxc,grd->xgcd", all_matrix, tokens_by_group, preferred_element_type=jnp.bfloat16
    )
    expert_rows = lax.all_to_all(outgoing, "expert", split_axis=0, concat_axis=0, tiled=True)
    expert_rows = expert_rows.reshape(-1, D)
    gate_score = jax.nn.sigmoid(
        jnp.dot(expert_rows, router[:, 0], preferred_element_type=jnp.float32)
    )
    gate_proj = jnp.dot(expert_rows, gate_weight[0], preferred_element_type=jnp.float32)
    up_proj = jnp.dot(expert_rows, up_weight[0], preferred_element_type=jnp.float32)
    expert_act = (jax.nn.silu(gate_proj) * up_proj).astype(jnp.bfloat16)
    shared_gate_full, shared_up_full, shared_down_full = (
        lax.all_gather(shared_gate, "expert", axis=0, tiled=True),
        lax.all_gather(shared_up, "expert", axis=0, tiled=True),
        lax.all_gather(shared_down, "expert", axis=0, tiled=True),
    )
    shared_act = (
        jax.nn.silu(jnp.dot(group_tokens, shared_gate_full, preferred_element_type=jnp.float32))
        * jnp.dot(group_tokens, shared_up_full, preferred_element_type=jnp.float32)
    ).astype(jnp.bfloat16)
    down_local = down_weight[0]
    col_width = down_local.shape[1]
    routed_piece = lax.all_gather(expert_act, "dp", axis=1, tiled=True)
    shared_piece = lax.all_gather(shared_act, "dp", axis=1, tiled=True)
    routed_cols = jnp.dot(routed_piece, down_local, preferred_element_type=jnp.float32)
    shared_cols = jnp.dot(shared_piece, shared_down_full, preferred_element_type=jnp.float32)
    expert_out = routed_cols.astype(jnp.bfloat16)
    shared_out = shared_cols.astype(jnp.bfloat16)
    returned = lax.all_to_all(
        expert_out.reshape(members, groups * capacity, col_width),
        "expert",
        split_axis=0,
        concat_axis=0,
        tiled=True,
    )
    returned_scores = lax.all_to_all(
        gate_score.reshape(members, groups * capacity),
        "expert",
        split_axis=0,
        concat_axis=0,
        tiled=True,
    )
    group_offset = (jnp.arange(groups, dtype=jnp.int32) * capacity)[:, None, None]
    lookup = (routes_by_group * (groups * capacity) + group_offset + slots_by_group).reshape(
        groups * rows_dev, TOPK
    )
    picked = jnp.take(returned.reshape(-1, col_width), lookup, axis=0)
    picked_scores = jnp.take(returned_scores.reshape(-1), lookup, axis=0)
    route_weight = ROUTE_SCALE * picked_scores / jnp.sum(picked_scores, axis=1, keepdims=True)
    moe_cols = shared_out.astype(jnp.float32) + jnp.sum(
        route_weight[:, :, None] * picked.astype(jnp.float32), axis=1
    )
    moe_home = lax.all_to_all(
        moe_cols.reshape(groups, rows_dev, col_width).astype(jnp.bfloat16),
        "dp",
        split_axis=0,
        concat_axis=2,
        tiled=True,
    ).astype(jnp.float32)
    final = (hidden_up + moe_home[0]).astype(jnp.bfloat16)
    return (final[:pre_rows], final[pre_rows:])


OUTER = 4
TILE = 16
LANES = 128
ROWS_CONTRACT = (((1,), (1,)), ((), ()))


def fold_row(row):
    return row.reshape(row.shape[:-2] + (TILE, row.shape[-1] // TILE))


def swap(value, axis, bit):
    size = lax.axis_size(axis)
    return lax.ppermute(value, axis, [(i, i ^ bit) for i in range(size)])


def call(kernel, out_shapes, args, scratch=(), scalars=0, flops=0, vmem=10):
    specs = [pl.BlockSpec(memory_space=pltpu.SMEM)] * scalars + [
        pl.BlockSpec(memory_space=pltpu.VMEM)
    ] * (len(args) - scalars)
    moved = sum(a.size * a.dtype.itemsize for a in args)
    single = not isinstance(out_shapes, (list, tuple))
    return pl.pallas_call(
        kernel,
        out_shape=out_shapes,
        in_specs=specs,
        out_specs=pl.BlockSpec(memory_space=pltpu.VMEM)
        if single
        else [pl.BlockSpec(memory_space=pltpu.VMEM)] * len(out_shapes),
        scratch_shapes=list(scratch),
        compiler_params=pltpu.CompilerParams(vmem_limit_bytes=vmem * 1024 * 1024),
        cost_estimate=pl.CostEstimate(flops=flops, bytes_accessed=moved, transcendentals=0),
    )(*args)


def low(shape):
    return jax.ShapeDtypeStruct(shape, jnp.bfloat16)


def pack_kernel(place_ref, out_ref, uv_ref, router_ref, routes_ref, *rest):
    block_refs, (side_ref,) = rest[:OUTER], rest[OUTER:]
    me = place_ref[0]
    outer = me // place_ref[2]
    heads = out_ref.shape[0] // OUTER
    tiles = heads * uv_ref.shape[1] // TILE
    side_ref[...] = jnp.zeros_like(side_ref)
    for part in range(TILE):
        side_ref[part : part + 1, :LANES] = router_ref[
            :, part * LANES : (part + 1) * LANES
        ].astype(jnp.float32)
    choices, rows = routes_ref.shape
    side_ref[:choices, LANES : LANES + rows] = routes_ref[...].astype(jnp.float32)
    side = side_ref[...].astype(jnp.bfloat16)
    for step in range(OUTER):
        target = outer ^ step
        block = block_refs[step]
        block[0, :, :D] = out_ref[pl.ds(target * heads, heads)].reshape(TILE, D)
        uv = uv_ref[pl.ds(target * heads, heads)].reshape(tiles * TILE, LANES)
        for tile in range(tiles):
            at = D + tile * LANES
            block[0, :, at : at + LANES] = uv[tile * TILE : (tile + 1) * TILE]
        block[0, :, D + tiles * LANES :] = side


def spread_kernel(units, place_ref, gate_ref, up_ref, *block_refs):
    me = place_ref[0]
    inner = block_refs[0].shape[0]
    padded = block_refs[0].shape[1] // 2
    for step in range(OUTER):
        block_refs[step][...] = jnp.zeros_like(block_refs[step])
    for member in range(inner * OUTER):
        offset = member ^ me
        step, near = offset // inner, offset % inner
        rows = slice(member * units, (member + 1) * units)
        for outer in range(OUTER):

            @pl.when(step == outer)
            def _():
                block_refs[outer][near, :units] = gate_ref[rows]
                block_refs[outer][near, padded : padded + units] = up_ref[rows]


def small_kernel(place_ref, kept_ref, far_ref, *rest):
    router_refs, (small_ref, fold_ref) = rest[:-2], rest[-2:]
    me = place_ref[0]
    members = kept_ref.shape[0] + far_ref.shape[0]
    small_ref[...] = jnp.zeros_like(small_ref)
    half = LANES // 2
    padded = kept_ref.shape[1] // 2
    for member in range(members):
        ref, i = (kept_ref, member) if member < members // 2 else (far_ref, member - members // 2)
        holder = me ^ chain_offset(member, members)
        lanes = pl.ds(pl.multiple_of(holder * LANES, LANES), LANES)
        small_ref[:padded, lanes] = ref[i, :padded]
        small_ref[half : half + padded, lanes] = ref[i, padded:]
    row = 0
    for ref in router_refs:
        count = ref.shape[0] * TILE
        fold_ref[row : row + count, :] = ref[...].reshape(count, LANES).astype(jnp.float32)
        row += count
    for part in range(TILE):
        small_ref[LANES - members :, part * LANES : (part + 1) * LANES] = fold_ref[
            pl.ds(part, members, stride=TILE), :
        ].astype(jnp.bfloat16)


def attend_kernel(
    length_ref, query_ref, latent_ref, dec_query_ref, dec_latent_ref, cache_ref, sink_ref,
    out_ref, rows_ref, dec_ref, fold_ref,
):
    span, heads, _ = query_ref.shape
    scale_qk = (QK_NOPE + ROPE) ** (-0.5)
    square = (heads, heads)
    diagonal = lax.broadcasted_iota(jnp.int32, square, 0) == lax.broadcasted_iota(
        jnp.int32, square, 1
    )
    sinks = jnp.sum(
        jnp.where(diagonal, jnp.broadcast_to(sink_ref[...], square), 0.0), axis=1, keepdims=True
    )
    latent = latent_ref[...]
    query = query_ref[...].reshape(span * heads, query_ref.shape[2])
    scores = (
        lax.dot_general(query, latent, ROWS_CONTRACT, preferred_element_type=jnp.float32) * scale_qk
    )
    token = lax.broadcasted_iota(jnp.int32, scores.shape, 0) // heads
    allowed = lax.broadcasted_iota(jnp.int32, scores.shape, 1) <= token
    masked = jnp.where(allowed, scores, NEG_FILL)
    sink_rows = jnp.broadcast_to(sinks[None], (span, heads, 1)).reshape(span * heads, 1)
    top = jnp.maximum(jnp.max(masked, axis=1, keepdims=True), sink_rows)
    terms = jnp.where(allowed, jnp.exp(masked - top), 0.0)
    total = jnp.sum(terms, axis=1, keepdims=True) + jnp.exp(sink_rows - top)
    numer = jnp.dot(
        terms.astype(jnp.bfloat16), latent[:, :LATENT], preferred_element_type=jnp.float32
    )
    attended = numer / total
    per_block = heads // out_ref.shape[0]
    parts = LATENT // LANES
    for part in range(parts):
        rows_ref[part] = attended[:, part * LANES : (part + 1) * LANES]
        for head in range(heads):
            at = (head % per_block) * LATENT + part * LANES
            out_ref[head // per_block, :, at : at + LANES] = rows_ref[
                part, pl.ds(head, span, stride=heads), :
            ].astype(jnp.bfloat16)

    window = cache_ref.shape[2]
    length = length_ref[0]
    slot = lax.broadcasted_iota(jnp.int32, (heads, window), 1)
    position = length - 1 - lax.rem(length - 1 - slot + window, window)
    usable = (position >= 0) & (position > length - window)
    dec_query = dec_query_ref[0]
    dec_latent = dec_latent_ref[...]
    cache = cache_ref[0]
    cache_scores = (
        jnp.dot(dec_query, cache, preferred_element_type=jnp.float32) * scale_qk
    )
    own = (
        jnp.sum(
            dec_query.astype(jnp.float32) * dec_latent.astype(jnp.float32), axis=1, keepdims=True
        )
        * scale_qk
    )
    cache_masked = jnp.where(usable, cache_scores, NEG_FILL)
    dec_top = jnp.maximum(
        jnp.maximum(jnp.max(cache_masked, axis=1, keepdims=True), own), sinks
    )
    cache_exp = jnp.where(usable, jnp.exp(cache_masked - dec_top), 0.0)
    own_exp = jnp.exp(own - dec_top)
    dec_numer = lax.dot_general(
        cache_exp.astype(jnp.bfloat16),
        cache[:LATENT, :],
        ROWS_CONTRACT,
        preferred_element_type=jnp.float32,
    )
    dec_numer = dec_numer + own_exp.astype(jnp.bfloat16).astype(jnp.float32) * dec_latent[
        :, :LATENT
    ].astype(jnp.float32)
    dec_total = jnp.sum(cache_exp, axis=1, keepdims=True) + own_exp + jnp.exp(sinks - dec_top)
    dec_attended = dec_numer / dec_total
    blocks = out_ref.shape[0]
    fold_ref[...] = jnp.zeros_like(fold_ref)
    for part in range(parts):
        dec_ref[part] = dec_attended[:, part * LANES : (part + 1) * LANES]
        for head in range(per_block):
            fold_ref[pl.ds(head * parts + part, blocks, stride=TILE), :] = dec_ref[
                part, pl.ds(head, blocks, stride=per_block), :
            ]
    out_ref[:, :, per_block * LATENT :] = (
        fold_ref[...].astype(jnp.bfloat16).reshape(blocks, TILE, LANES)
    )


def project_kernel(place_ref, att_ref, *rest):
    piece_refs, (out_ref, rows_ref, fold_ref, uv_ref) = rest[:-4], rest[-4:]
    pieces = [(ref, i) for ref in piece_refs for i in range(ref.shape[0])]
    me = place_ref[0]
    blocks, span, width = att_ref.shape
    width -= LANES
    members = len(pieces)
    heads = width // LATENT
    latent_rows = LATENT // members
    tiles = latent_rows // TILE
    value_rows = TILE // heads
    rows_ref[: blocks * span, :] = att_ref[:, :, :width].reshape(blocks * span, width)
    fold_ref[...] = att_ref[:, :, width:].reshape(blocks * TILE, LANES).astype(jnp.float32)
    dec_rows = jnp.concatenate(
        [fold_ref[pl.ds(i, blocks, stride=TILE), :] for i in range(width // LANES)], axis=1
    )
    dec_rows = jnp.concatenate([dec_rows, jnp.zeros((TILE - blocks, width), jnp.float32)], axis=0)
    rows_ref[blocks * span :, :] = dec_rows.astype(jnp.bfloat16)
    for step in range(members):
        holder = me ^ chain_offset(step, members)
        for head in range(heads):
            for tile in range(tiles):
                at = D + (head * tiles + tile) * LANES
                start = pl.multiple_of(head * LATENT + holder * latent_rows + tile * TILE, TILE)
                ref, i = pieces[step]
                uv_ref[pl.ds(start, TILE), :] = ref[i, :, at : at + LANES]
    value = lax.broadcasted_iota(jnp.int32, (LANES, members * TILE), 0)
    column = lax.broadcasted_iota(jnp.int32, (LANES, members * TILE), 1)
    step = column // TILE
    holder = chain_offset(step, members) ^ me
    wanted = holder * value_rows + column % value_rows
    column_head = (column % TILE) // value_rows
    spread = []
    for head in range(heads):
        order = jnp.where((value == wanted) & (column_head == head), 1.0, 0.0).astype(jnp.bfloat16)
        spread.append(
            jnp.dot(
                uv_ref[head * LATENT : (head + 1) * LATENT, :],
                order,
                preferred_element_type=jnp.float32,
            ).astype(jnp.bfloat16)
        )
    head_values = jnp.dot(
        rows_ref[...], jnp.concatenate(spread, axis=0), preferred_element_type=jnp.float32
    ).astype(jnp.bfloat16)
    out_rows = jnp.concatenate([ref[i, :, :D] for ref, i in pieces], axis=0)
    partial_rows = jnp.dot(head_values, out_rows, preferred_element_type=jnp.float32)
    split = blocks * span
    out_ref[:, :, :D] = partial_rows[:split].astype(jnp.bfloat16).reshape(blocks, span, D)
    for part in range(TILE):
        fold_ref[pl.ds(part, blocks, stride=TILE), :] = partial_rows[
            split : split + blocks, part * LANES : (part + 1) * LANES
        ]
    out_ref[:, :, D:] = fold_ref[...].astype(jnp.bfloat16).reshape(blocks, TILE, LANES)


def chain_offset(step, members):
    inner = members // OUTER
    offset = (step % OUTER) * inner
    rest = step // OUTER
    bit = inner // 2
    while bit:
        offset = offset + (rest % 2) * bit
        rest = rest // 2
        bit //= 2
    return offset


def norm_kernel(partial_ref, resid_ref, gain_ref, hidden_ref, normed_ref):
    summed = partial_ref[0].astype(jnp.float32)
    for i in range(1, partial_ref.shape[0]):
        summed = summed + partial_ref[i].astype(jnp.float32)
    hidden = (resid_ref[...].astype(jnp.float32) + summed).astype(jnp.bfloat16)
    hidden_ref[...] = hidden
    hidden = hidden.astype(jnp.float32)
    gain = gain_ref[...].astype(jnp.float32)
    pre, dec = hidden[:, :D], hidden[:, D:]
    pre_mean = jnp.sum(pre * pre, axis=1, keepdims=True) / D
    dec_mean = jnp.sum(jnp.sum(dec * dec, axis=1, keepdims=True), axis=0, keepdims=True) / D
    normed_ref[:, :D] = (pre * lax.rsqrt(pre_mean + NORM_EPS) * gain[:1, :D]).astype(jnp.bfloat16)
    normed_ref[:, D:] = (dec * lax.rsqrt(dec_mean + NORM_EPS) * gain[:, D:]).astype(jnp.bfloat16)


def expert_kernel(
    units, small_ref, select_ref, chosen_ref, reorder_ref, gate_ref, up_ref, *rest
):
    piece_refs, (act_ref, shared_ref, fold_ref, pre_ref, dec_ref) = rest[:-5], rest[-5:]
    pre_total = pre_ref.shape[0]
    homes = pre_total // TILE
    row = 0
    for ref in piece_refs:
        count = ref.shape[0]
        pre_ref[row : row + count, :] = ref[:, :D]
        fold_ref[row : row + count, :] = ref[:, D:].astype(jnp.float32)
        row += count
    for part in range(TILE):
        dec_ref[:, part * LANES : (part + 1) * LANES] = fold_ref[
            pl.ds(part, homes, stride=TILE), :
        ].astype(jnp.bfloat16)
    pre = pre_ref[...]
    dec = dec_ref[...]
    small = small_ref[...]
    first = jnp.concatenate(
        [
            lax.dot_general(pre, small, ROWS_CONTRACT, preferred_element_type=jnp.float32),
            lax.dot_general(dec, small, ROWS_CONTRACT, preferred_element_type=jnp.float32),
        ],
        axis=0,
    )
    half = LANES // 2
    members = len(piece_refs)
    gate_part = first[:, :units]
    up_part = first[:, half : half + units]
    shared_act = (gate_part / (1.0 + jnp.exp(-gate_part)) * up_part).astype(jnp.bfloat16)
    shared_act = jnp.dot(
        reorder_ref[...], shared_act, preferred_element_type=jnp.float32
    ).astype(jnp.bfloat16)
    total = shared_act.shape[0]
    shared_ref[...] = jnp.zeros_like(shared_ref)
    shared_ref[:, :units] = shared_act[: total // 2]
    shared_ref[:, half : half + units] = shared_act[total // 2 :]
    logits = first[:, LANES - members :]
    scores = 1.0 / (1.0 + jnp.exp(-logits))
    token_weight = (
        ROUTE_SCALE * scores[:, :1] / jnp.sum(scores * chosen_ref[:, LANES - members :], axis=1, keepdims=True)
    )
    high = token_weight.astype(jnp.bfloat16)
    rest = token_weight - high.astype(jnp.float32)
    middle = rest.astype(jnp.bfloat16)
    rest = (rest - middle.astype(jnp.float32)).astype(jnp.bfloat16)
    select = select_ref[...]
    weights = jnp.dot(
        select, jnp.concatenate([high, middle, rest], axis=1), preferred_element_type=jnp.float32
    )
    slot_weight = jnp.sum(weights, axis=1, keepdims=True)
    expert_rows = (
        jnp.dot(select[:, :pre_total], pre, preferred_element_type=jnp.float32)
        + jnp.dot(select[:, pre_total:], dec, preferred_element_type=jnp.float32)
    ).astype(jnp.bfloat16)
    gate = lax.dot_general(
        expert_rows, gate_ref[0], ROWS_CONTRACT, preferred_element_type=jnp.float32
    )
    up = lax.dot_general(expert_rows, up_ref[0], ROWS_CONTRACT, preferred_element_type=jnp.float32)
    act_ref[...] = (gate / (1.0 + jnp.exp(-gate)) * up * slot_weight).astype(jnp.bfloat16)


def down_kernel(
    place_ref, act_ref, act_other_ref, shared_ref, shared_other_ref, down_ref,
    shared_down_ref, shared_down_other_ref, scatter_ref, kept_ref, sent_ref, fold_ref,
):
    group = place_ref[1]
    width = act_ref.shape[1]
    columns = down_ref.shape[2]
    own = down_ref[0, pl.ds(pl.multiple_of(group * width, TILE), width), :]
    other = down_ref[0, pl.ds(pl.multiple_of((1 - group) * width, TILE), width), :]
    routed = (
        jnp.dot(act_ref[...], own, preferred_element_type=jnp.float32)
        + jnp.dot(act_other_ref[...], other, preferred_element_type=jnp.float32)
    ).astype(jnp.bfloat16)
    units = shared_down_ref.shape[0]

    def down(at):
        both = jnp.concatenate([shared_ref[:, at : at + units], shared_other_ref[:, at : at + units]], axis=1)
        return jnp.dot(both, jnp.concatenate([shared_down_ref[...], shared_down_other_ref[...]], axis=0), preferred_element_type=jnp.float32)

    total = (
        jnp.dot(scatter_ref[...], routed, preferred_element_type=jnp.float32)
        + jnp.concatenate([down(0), down(LANES // 2)], axis=0)
    )
    half = kept_ref.shape[0]
    homes = 2 * half
    split = homes * TILE
    kept_ref[:, :, :columns] = (
        total[: split // 2].astype(jnp.bfloat16).reshape(half, TILE, columns)
    )
    sent_ref[:, :, :columns] = (
        total[split // 2 : split].astype(jnp.bfloat16).reshape(half, TILE, columns)
    )
    fold_ref[...] = jnp.zeros_like(fold_ref)
    for part in range(columns // LANES):
        fold_ref[pl.ds(part, homes, stride=TILE), :] = total[
            split:, part * LANES : (part + 1) * LANES
        ]
    folded = fold_ref[...].astype(jnp.bfloat16)
    kept_ref[:, :, columns:] = folded[: split // 2].reshape(half, TILE, LANES)
    sent_ref[:, :, columns:] = folded[split // 2 :].reshape(half, TILE, LANES)


def finish_kernel(got_ref, hidden_ref, pre_ref, dec_ref):
    sources, _, width = got_ref.shape
    columns = width - LANES
    groups = D // columns
    each = sources // groups
    for group in range(groups):
        summed = got_ref[group * each].astype(jnp.float32)
        for i in range(1, each):
            summed = summed + got_ref[group * each + i].astype(jnp.float32)
        at = group * columns
        pre_ref[:, at : at + columns] = (
            hidden_ref[:, at : at + columns].astype(jnp.float32) + summed[:, :columns]
        ).astype(jnp.bfloat16)
        parts = columns // LANES
        for part in range(parts):
            row = group * parts + part
            dec_ref[:, row * LANES : (row + 1) * LANES] = (
                hidden_ref[row : row + 1, D:].astype(jnp.float32)
                + summed[part : part + 1, columns:]
            ).astype(jnp.bfloat16)


def token_shards(
    pre_query,
    pre_latent,
    pre_resid,
    dec_query,
    dec_latent,
    dec_resid,
    cache_lengths,
    latent_cache,
    sink_logits,
    uv_weight,
    out_weight,
    norm_gain,
    router,
    routes,
    gate_weight,
    up_weight,
    down_weight,
    shared_gate,
    shared_up,
    shared_down,
):
    groups = lax.axis_size("dp")
    members = lax.axis_size("expert")
    inner = members // OUTER
    homes = groups * members
    me = lax.axis_index("expert")
    my_group = lax.axis_index("dp")
    place_ids = jnp.stack([me, my_group, jnp.int32(inner)]).astype(jnp.int32)
    pre_rows = pre_query.shape[0]
    rows_dev = pre_rows + 1
    capacity = max(2, (rows_dev * TOPK + members - 1) // members)

    heads_dev, latent_rows, value_dim = uv_weight.shape
    heads_outer = heads_dev // OUTER
    uv_tiles = heads_outer * latent_rows // TILE
    block_width = D + uv_tiles * value_dim + 2 * LANES
    blocks = call(
        pack_kernel,
        [low((1, TILE, block_width))] * OUTER,
        [place_ids, out_weight, uv_weight, router.T, routes.T],
        scratch=[pltpu.VMEM((TILE, 2 * LANES), jnp.float32)],
        scalars=1,
    )
    pair_bit = inner // 2
    near = [blocks[0]] + [swap(blocks[i], "expert", i * inner) for i in range(1, OUTER)]
    own_pair = swap(blocks[0], "expert", pair_bit)
    line = jnp.concatenate(near, axis=0)
    far_pair = swap(line[1:], "expert", pair_bit)
    pieces = [line, own_pair, far_pair]
    pieces = pieces + [swap(piece, "expert", 1) for piece in pieces]
    chain = [chain_offset(step, members) for step in range(members)]
    holders = me ^ jnp.array(chain, jnp.int32)
    side_at = D + uv_tiles * value_dim
    router_blocks = [piece[:, :, side_at : side_at + LANES] for piece in pieces]
    routes_plane = jnp.concatenate(
        [piece[:, :TOPK, side_at + LANES : side_at + LANES + rows_dev] for piece in pieces], axis=0
    )
    routes_other = swap(routes_plane, "dp", 1)

    pre_query, blocks = lax.optimization_barrier((pre_query, blocks))
    peers = groups * OUTER
    heads_block = heads_outer * LATENT
    att_blocks = call(
        attend_kernel,
        low((peers, pre_rows, heads_block + LANES)),
        [
            cache_lengths, pre_query, pre_latent, dec_query, dec_latent,
            latent_cache.swapaxes(1, 2),
            sink_logits.reshape(1, -1),
        ],
        scratch=[
            pltpu.VMEM((LATENT // LANES, pre_rows * pre_query.shape[1], LANES), jnp.float32),
            pltpu.VMEM((LATENT // LANES, pre_query.shape[1], LANES), jnp.float32),
            pltpu.VMEM((peers * TILE, LANES), jnp.float32),
        ],
        scalars=1,
        flops=100_000_000,
    )
    lines = [
        [g * members + o * inner + i for g in range(groups) for o in range(OUTER)]
        for i in range(inner)
    ]
    both = ("dp", "expert")
    att_got = lax.all_to_all(
        att_blocks, both, split_axis=0, concat_axis=0, axis_index_groups=lines, tiled=True
    )
    partial_blocks = call(
        project_kernel,
        low((peers, pre_rows, D + LANES)),
        [place_ids, att_got, *pieces],
        scratch=[
            pltpu.VMEM((peers * pre_rows + TILE, heads_block), jnp.bfloat16),
            pltpu.VMEM((peers * TILE, LANES), jnp.float32),
            pltpu.VMEM((heads_block, value_dim), jnp.bfloat16),
        ],
        scalars=1,
        flops=300_000_000,
    )

    units = shared_gate.shape[1] // members
    padded = -(-units // TILE) * TILE
    depth = shared_gate.shape[0]
    shared_gate, shared_up, line = lax.optimization_barrier((shared_gate, shared_up, line))
    spread = call(
        partial(spread_kernel, units),
        [low((inner, 2 * padded, depth))] * OUTER,
        [place_ids, shared_gate.T, shared_up.T],
        scalars=1,
    )
    shared_got = [spread[0]] + [swap(spread[i], "expert", i * inner) for i in range(1, OUTER)]
    kept = jnp.concatenate([block[:pair_bit] for block in shared_got], axis=0)
    sent = jnp.concatenate([block[pair_bit:] for block in shared_got], axis=0)
    far = swap(sent, "expert", pair_bit)
    shared_kept = jnp.concatenate([kept[::pair_bit], far[::pair_bit]], axis=0)
    shared_sent = jnp.concatenate([kept[1::pair_bit], far[1::pair_bit]], axis=0)
    shared_far = swap(shared_sent, "expert", 1)
    small = call(
        small_kernel,
        low((LANES, D)),
        [place_ids, shared_kept, shared_far, *router_blocks],
        scratch=[pltpu.VMEM((members * TILE, LANES), jnp.float32)],
        scalars=1,
    )
    partial_got = lax.all_to_all(
        partial_blocks, both, split_axis=0, concat_axis=0, axis_index_groups=lines, tiled=True
    )
    shared_down, att_blocks = lax.optimization_barrier((shared_down, att_blocks))
    half = members // 2
    lower = me < half
    first, second = shared_down[:units], shared_down[units:]
    down_a = lax.ppermute(
        jnp.where(lower, first, second),
        "expert",
        [(i, 2 * i if i < half else 2 * (i - half) + 1) for i in range(members)],
    )
    down_b = lax.ppermute(
        jnp.where(lower, second, first),
        "expert",
        [(i, 2 * i + 1 if i < half else 2 * (i - half)) for i in range(members)],
    )
    mine_first = (me % 2) == my_group
    shared_down_own = jnp.where(mine_first, down_a, down_b)
    shared_down_other = jnp.where(mine_first, down_b, down_a)

    middle = OUTER // 2
    pair_bit = inner // 2
    tags_a = [(0, step * inner) for step in range(middle)]
    tags_b = [(0, step * inner) for step in range(middle, OUTER)]
    tags = []
    for last in range(2):
        for which, group_bit, member_bit in (
            (tags_a, 0, 0), (tags_b, 0, 0), (tags_a, 0, 1), (tags_b, 1, 0),
            (tags_a, 1, 0), (tags_b, 0, 1), (tags_a, 1, 1), (tags_b, 1, 1),
        ):
            tags += [(g ^ group_bit, m ^ (member_bit * pair_bit) ^ last) for g, m in which]
    pre_total = homes * pre_rows
    total = pre_total + homes

    positions = [g * members + chain.index(m) for g, m in tags]
    routes_all = jnp.concatenate([routes_plane, routes_other], axis=0)
    routes_all = jnp.stack([routes_all[p] for p in positions], axis=0)
    token_routes = jnp.concatenate(
        [
            routes_all[:, :, :pre_rows].transpose(0, 2, 1).reshape(pre_total, TOPK),
            routes_all[:, :, pre_rows],
        ],
        axis=0,
    ).astype(jnp.int32)
    lane_expert = jnp.concatenate([jnp.full((LANES - members,), -1, jnp.int32), holders])
    chosen = jnp.sum(
        (token_routes[:, :, None] == lane_expert[None, None, :]).astype(jnp.float32), axis=1
    )
    mine = jnp.sum((token_routes == me).astype(jnp.float32), axis=1)
    earlier = (
        jnp.arange(total, dtype=jnp.int32)[:, None] <= jnp.arange(total, dtype=jnp.int32)[None, :]
    ).astype(jnp.bfloat16)
    home_group = jnp.array([g for g, _ in tags], jnp.int32) ^ my_group
    home_member = jnp.array([m for _, m in tags], jnp.int32) ^ me
    home_place = (
        ((home_member ^ me) % 2) * (homes // 2) + home_group * (members // 2) + home_member // 2
    )
    place = jnp.concatenate(
        [
            (home_place[:, None] * pre_rows + jnp.arange(pre_rows)[None, :]).reshape(-1),
            pre_total + home_place,
        ]
    )
    reorder = (jnp.arange(total, dtype=jnp.int32)[:, None] == place[None, :]).astype(jnp.bfloat16)
    mine_placed = jnp.dot(reorder, mine.astype(jnp.bfloat16), preferred_element_type=jnp.float32)
    rank = jnp.dot(
        mine_placed.astype(jnp.bfloat16)[None, :], earlier, preferred_element_type=jnp.float32
    )
    slots = homes * capacity
    slot_ids = jnp.arange(1, slots + 1, dtype=jnp.float32)
    gather = ((rank == slot_ids[:, None]) & (mine_placed[None, :] > 0.0)).astype(jnp.bfloat16)
    scatter = gather.T
    select = jnp.dot(gather, reorder, preferred_element_type=jnp.float32).astype(jnp.bfloat16)

    (
        partial_got, select, scatter, reorder, chosen, small, shared_down_own, shared_down_other
    ) = lax.optimization_barrier(
        (
            partial_got, select, scatter, reorder, chosen, small, shared_down_own,
            shared_down_other,
        )
    )
    resid = jnp.concatenate([pre_resid, fold_row(dec_resid)], axis=1)
    gain = jnp.concatenate(
        [jnp.broadcast_to(norm_gain[None], (TILE, D)), norm_gain.reshape(TILE, LANES)], axis=1
    )
    hidden, normed = call(
        norm_kernel, [low(resid.shape)] * 2, [partial_got, resid, gain], flops=1_000_000
    )

    line = [normed] + [swap(normed, "expert", step * inner) for step in range(1, OUTER)]
    middle = OUTER // 2
    row_pieces = []
    for part in (line[:middle], line[middle:]):
        row_pieces.append(jnp.concatenate(part, axis=0))
    piece_a, piece_b = row_pieces
    a_pair, b_group = swap(piece_a, "expert", pair_bit), swap(piece_b, "dp", 1)
    a_group, b_pair = swap(piece_a, "dp", 1), swap(piece_b, "expert", pair_bit)
    a_both, b_both = swap(a_pair, "dp", 1), swap(b_group, "expert", pair_bit)
    row_pieces = [piece_a, piece_b, a_pair, b_group, a_group, b_pair, a_both, b_both]
    row_pieces = row_pieces + [swap(piece, "expert", 1) for piece in row_pieces]

    width = gate_weight.shape[2]
    expert_act, shared_act = call(
        partial(expert_kernel, units),
        [low((slots, width)), low((total // 2, LANES))],
        [
            small, select, chosen, reorder, gate_weight.swapaxes(1, 2), up_weight.swapaxes(1, 2),
            *row_pieces,
        ],
        scratch=[
            pltpu.VMEM((pre_total, LANES), jnp.float32),
            pltpu.VMEM((pre_total, D), jnp.bfloat16),
            pltpu.VMEM((homes, D), jnp.bfloat16),
        ],
        flops=3_000_000_000,
        vmem=20,
    )
    expert_act_other = swap(expert_act, "dp", 1)
    shared_act_other = swap(shared_act, "dp", 1)
    col_width = down_weight.shape[2]
    kept, sent = call(
        down_kernel,
        [low((homes // 2, TILE, col_width + LANES))] * 2,
        [
            place_ids, expert_act, expert_act_other, shared_act, shared_act_other, down_weight,
            shared_down_own, shared_down_other, scatter,
        ],
        scratch=[pltpu.VMEM((pre_total, LANES), jnp.float32)],
        scalars=1,
        flops=1_000_000_000,
        vmem=20,
    )
    pair_sum = (kept.astype(jnp.float32) + swap(sent, "expert", 1).astype(jnp.float32)).astype(
        jnp.bfloat16
    )
    halves = [
        [g * members + 2 * i + b for g in range(groups) for i in range(members // 2)]
        for b in range(2)
    ]
    home_got = lax.all_to_all(
        pair_sum, both, split_axis=0, concat_axis=0, axis_index_groups=halves, tiled=True
    )
    return tuple(
        call(finish_kernel, [low(pre_resid.shape), low(dec_resid.shape)], [home_got, hidden])
    )


def fits(mesh, heads, ff):
    groups, members = mesh.shape["dp"], mesh.shape["expert"]
    return (
        groups == 2
        and members % (2 * OUTER) == 0
        and (heads // groups) % OUTER == 0
        and ff % (groups * members) == 0
    )


def solution(mesh):
    in_specs = (
        P(("dp", "expert"), None, None),
        P(("dp", "expert"), None),
        P(("dp", "expert"), None),
        P(("dp", "expert"), None, None),
        P(("dp", "expert"), None),
        P(("dp", "expert"), None),
        P(("dp", "expert")),
        P(("dp", "expert"), None, None),
        P(),
        P("dp", "expert", None),
        P("dp", "expert", None),
        P(),
        P(None, "expert"),
        P(("dp", "expert"), None),
        P("expert", None, "dp"),
        P("expert", None, "dp"),
        P("expert", None, "dp"),
        P("expert", "dp"),
        P("expert", "dp"),
        P("expert", "dp"),
    )
    out_specs = (P(("dp", "expert"), None), P(("dp", "expert"), None))

    def layer(*args):
        plan = token_shards if fits(mesh, args[9].shape[0], args[17].shape[1]) else shards
        return jax.shard_map(
            plan, mesh=mesh, in_specs=in_specs, out_specs=out_specs, check_vma=False
        )(*args)

    return layer
```

```python
from functools import partial

import jax
import jax.numpy as jnp
from jax import lax
from jax.experimental import pallas as pl
from jax.experimental.pallas import tpu as pltpu
from jax.sharding import PartitionSpec as P

D = 2048
LATENT = 512
ROPE = 64
QK_NOPE = 128
TOPK = 6


ROUTE_SCALE = 2.446
NORM_EPS = 1e-06
NEG_FILL = -1e30


def assign_slots(route_rows, experts):
    flat_routes = route_rows.reshape(-1)
    one_hot = (flat_routes[:, None] == jnp.arange(experts, dtype=jnp.int32)[None, :]).astype(
        jnp.int32
    )
    running = jnp.cumsum(one_hot, axis=0)
    slot_rank = jnp.sum(running * one_hot, axis=1) - 1
    return slot_rank.reshape(route_rows.shape)


def dispatch_matrix(route_rows, slot_rows, experts, capacity):
    target = route_rows * capacity + slot_rows
    places = jnp.arange(experts * capacity, dtype=jnp.int32)
    total = jnp.zeros((route_rows.shape[0], experts * capacity), jnp.bfloat16)
    for column in range(route_rows.shape[1]):
        total = total + (target[:, column][:, None] == places[None, :]).astype(jnp.bfloat16)
    return total


def shards(
    pre_query,
    pre_latent,
    pre_resid,
    dec_query,
    dec_latent,
    dec_resid,
    cache_lengths,
    latent_cache,
    sink_logits,
    uv_weight,
    out_weight,
    norm_gain,
    router,
    routes,
    gate_weight,
    up_weight,
    down_weight,
    shared_gate,
    shared_up,
    shared_down,
):
    groups = lax.axis_size("dp")
    members = lax.axis_size("expert")
    pre_rows = pre_query.shape[0]
    rows_dev = pre_rows + 1
    scale_qk = (QK_NOPE + ROPE) ** (-0.5)
    pre_scores = (
        jnp.einsum("thc,uc->thu", pre_query, pre_latent, preferred_element_type=jnp.float32)
        * scale_qk
    )
    places = jnp.arange(pre_rows, dtype=jnp.int32)
    allowed = (places[None, :] <= places[:, None])[:, None, :]
    masked = jnp.where(allowed, pre_scores, NEG_FILL)
    pre_max = jnp.maximum(jnp.max(masked, axis=2), sink_logits[None, :])
    exp_terms = jnp.where(allowed, jnp.exp(masked - pre_max[:, :, None]), 0.0)
    denominator = jnp.sum(exp_terms, axis=2) + jnp.exp(sink_logits[None, :] - pre_max)
    numerator = jnp.einsum(
        "thu,ul->thl",
        exp_terms.astype(jnp.bfloat16),
        pre_latent[:, :LATENT],
        preferred_element_type=jnp.float32,
    )
    pre_att = (numerator / denominator[:, :, None]).astype(jnp.bfloat16)
    window = latent_cache.shape[1]
    slot_ids = jnp.arange(window, dtype=jnp.int32)
    newest = cache_lengths - 1
    position = newest[:, None] - jnp.mod(newest[:, None] - slot_ids[None, :], window)
    usable = ((position >= 0) & (position > cache_lengths[:, None] - window))[:, None, :]
    cache_scores = (
        jnp.einsum("rhc,rsc->rhs", dec_query, latent_cache, preferred_element_type=jnp.float32)
        * scale_qk
    )
    own_scores = (
        jnp.einsum("rhc,rc->rh", dec_query, dec_latent, preferred_element_type=jnp.float32)
        * scale_qk
    )
    cache_masked = jnp.where(usable, cache_scores, NEG_FILL)
    top_score = jnp.maximum(
        jnp.maximum(jnp.max(cache_masked, axis=2), own_scores), sink_logits[None, :]
    )
    cache_exp = jnp.where(usable, jnp.exp(cache_masked - top_score[:, :, None]), 0.0)
    own_exp = jnp.exp(own_scores - top_score)
    dec_numer = jnp.einsum(
        "rhs,rsl->rhl",
        cache_exp.astype(jnp.bfloat16),
        latent_cache[:, :, :LATENT],
        preferred_element_type=jnp.float32,
    )
    dec_numer = dec_numer + own_exp.astype(jnp.bfloat16).astype(jnp.float32)[
        :, :, None
    ] * dec_latent[:, None, :LATENT].astype(jnp.float32)
    dec_total = jnp.sum(cache_exp, axis=2) + own_exp + jnp.exp(sink_logits[None, :] - top_score)
    dec_att = (dec_numer / dec_total[:, :, None]).astype(jnp.bfloat16)
    attention = jnp.concatenate([pre_att, dec_att], axis=0)
    spread = lax.all_to_all(attention, "dp", split_axis=1, concat_axis=0, tiled=True)
    uv_full, out_full = (
        lax.all_gather(uv_weight, "expert", axis=1, tiled=True),
        lax.all_gather(out_weight, "expert", axis=1, tiled=True),
    )
    head_values = jnp.einsum(
        "thl,hlv->thv", spread, uv_full, preferred_element_type=jnp.float32
    ).astype(jnp.bfloat16)
    head_partial = jnp.einsum(
        "thv,hvd->td", head_values, out_full, preferred_element_type=jnp.float32
    )
    attn_out = lax.psum_scatter(
        head_partial.astype(jnp.bfloat16), "dp", scatter_dimension=0, tiled=True
    ).astype(jnp.float32)
    resid = jnp.concatenate([pre_resid, dec_resid], axis=0)
    hidden = (resid.astype(jnp.float32) + attn_out).astype(jnp.bfloat16)
    hidden_up = lax.optimization_barrier(hidden).astype(jnp.float32)
    mean_square = jnp.mean(hidden_up * hidden_up, axis=1, keepdims=True)
    normed = (
        hidden_up * lax.rsqrt(mean_square + NORM_EPS) * norm_gain.astype(jnp.float32)[None, :]
    ).astype(jnp.bfloat16)
    capacity = max(2, (rows_dev * TOPK + members - 1) // members)
    group_tokens = lax.all_gather(normed, "dp", axis=0, tiled=True)
    group_routes = lax.all_gather(routes, "dp", axis=0, tiled=True)
    routes_by_group = group_routes.reshape(groups, rows_dev, TOPK)
    slots_by_group = jax.vmap(partial(assign_slots, experts=members))(routes_by_group)
    tokens_by_group = group_tokens.reshape(groups, rows_dev, D)
    all_matrix = jax.vmap(partial(dispatch_matrix, experts=members, capacity=capacity))(
        routes_by_group, slots_by_group
    )
    all_matrix = all_matrix.reshape(groups, rows_dev, members, capacity)
    outgoing = jnp.einsum(
        "grxc,grd->xgcd", all_matrix, tokens_by_group, preferred_element_type=jnp.bfloat16
    )
    expert_rows = lax.all_to_all(outgoing, "expert", split_axis=0, concat_axis=0, tiled=True)
    expert_rows = expert_rows.reshape(-1, D)
    gate_score = jax.nn.sigmoid(
        jnp.dot(expert_rows, router[:, 0], preferred_element_type=jnp.float32)
    )
    gate_proj = jnp.dot(expert_rows, gate_weight[0], preferred_element_type=jnp.float32)
    up_proj = jnp.dot(expert_rows, up_weight[0], preferred_element_type=jnp.float32)
    expert_act = (jax.nn.silu(gate_proj) * up_proj).astype(jnp.bfloat16)
    shared_gate_full, shared_up_full, shared_down_full = (
        lax.all_gather(shared_gate, "expert", axis=0, tiled=True),
        lax.all_gather(shared_up, "expert", axis=0, tiled=True),
        lax.all_gather(shared_down, "expert", axis=0, tiled=True),
    )
    shared_act = (
        jax.nn.silu(jnp.dot(group_tokens, shared_gate_full, preferred_element_type=jnp.float32))
        * jnp.dot(group_tokens, shared_up_full, preferred_element_type=jnp.float32)
    ).astype(jnp.bfloat16)
    down_local = down_weight[0]
    col_width = down_local.shape[1]
    routed_piece = lax.all_gather(expert_act, "dp", axis=1, tiled=True)
    shared_piece = lax.all_gather(shared_act, "dp", axis=1, tiled=True)
    routed_cols = jnp.dot(routed_piece, down_local, preferred_element_type=jnp.float32)
    shared_cols = jnp.dot(shared_piece, shared_down_full, preferred_element_type=jnp.float32)
    expert_out = routed_cols.astype(jnp.bfloat16)
    shared_out = shared_cols.astype(jnp.bfloat16)
    returned = lax.all_to_all(
        expert_out.reshape(members, groups * capacity, col_width),
        "expert",
        split_axis=0,
        concat_axis=0,
        tiled=True,
    )
    returned_scores = lax.all_to_all(
        gate_score.reshape(members, groups * capacity),
        "expert",
        split_axis=0,
        concat_axis=0,
        tiled=True,
    )
    group_offset = (jnp.arange(groups, dtype=jnp.int32) * capacity)[:, None, None]
    lookup = (routes_by_group * (groups * capacity) + group_offset + slots_by_group).reshape(
        groups * rows_dev, TOPK
    )
    picked = jnp.take(returned.reshape(-1, col_width), lookup, axis=0)
    picked_scores = jnp.take(returned_scores.reshape(-1), lookup, axis=0)
    route_weight = ROUTE_SCALE * picked_scores / jnp.sum(picked_scores, axis=1, keepdims=True)
    moe_cols = shared_out.astype(jnp.float32) + jnp.sum(
        route_weight[:, :, None] * picked.astype(jnp.float32), axis=1
    )
    moe_home = lax.all_to_all(
        moe_cols.reshape(groups, rows_dev, col_width).astype(jnp.bfloat16),
        "dp",
        split_axis=0,
        concat_axis=2,
        tiled=True,
    ).astype(jnp.float32)
    final = (hidden_up + moe_home[0]).astype(jnp.bfloat16)
    return (final[:pre_rows], final[pre_rows:])


OUTER = 4
TILE = 16
LANES = 128
ROWS_CONTRACT = (((1,), (1,)), ((), ()))


def fold_row(row):
    return row.reshape(row.shape[:-2] + (TILE, row.shape[-1] // TILE))


def swap(value, axis, bit):
    size = lax.axis_size(axis)
    return lax.ppermute(value, axis, [(i, i ^ bit) for i in range(size)])


def call(kernel, out_shapes, args, scratch=(), scalars=0, flops=0, vmem=10, moved=(), late=(), rows=None):
    specs = []
    for i in range(len(args)):
        if i < scalars:
            specs.append(pl.BlockSpec(memory_space=pltpu.SMEM))
        elif i in moved:
            specs.append(pl.BlockSpec(memory_space=pl.ANY))
        else:
            specs.append(pl.BlockSpec(memory_space=pltpu.VMEM))
    scratch = list(scratch)
    body = kernel
    if moved:
        rows = dict(rows or {})
        shapes = {i: args[i].shape for i in moved}
        for i, (_, count) in rows.items():
            shapes[i] = (shapes[i][0], count) + shapes[i][2:]
        buffers = [pltpu.VMEM(shapes[i], args[i].dtype) for i in moved]
        scratch = scratch + buffers + [pltpu.SemaphoreType.DMA((len(moved),))]

        def body(*refs):
            rest, held, sem = refs[: -len(moved) - 1], refs[-len(moved) - 1 : -1], refs[-1]
            sources = {i: refs[i] for i in moved}
            for i, (start, count) in rows.items():
                sources[i] = refs[i].at[:, pl.ds(start, count)]
            copies = [
                pltpu.make_async_copy(sources[i], held[j], sem.at[j]) for j, i in enumerate(moved)
            ]
            for copy in copies:
                copy.start()
            for i, copy in zip(moved, copies):
                if i not in late:
                    copy.wait()
            inputs = [held[moved.index(i)] if i in moved else refs[i] for i in range(len(args))]
            if late:
                waits = [copies[moved.index(i)].wait for i in late]
                kernel(*inputs, *rest[len(args) :], waits=waits)
            else:
                kernel(*inputs, *rest[len(args) :])

    moved_bytes = sum(a.size * a.dtype.itemsize for a in args)
    single = not isinstance(out_shapes, (list, tuple))
    return pl.pallas_call(
        body,
        out_shape=out_shapes,
        in_specs=specs,
        out_specs=pl.BlockSpec(memory_space=pltpu.VMEM)
        if single
        else [pl.BlockSpec(memory_space=pltpu.VMEM)] * len(out_shapes),
        scratch_shapes=scratch,
        compiler_params=pltpu.CompilerParams(vmem_limit_bytes=vmem * 1024 * 1024),
        cost_estimate=pl.CostEstimate(flops=flops, bytes_accessed=moved_bytes, transcendentals=0),
    )(*args)


def low(shape):
    return jax.ShapeDtypeStruct(shape, jnp.bfloat16)


def pack_kernel(place_ref, out_ref, uv_ref, router_ref, routes_ref, *rest):
    block_refs, (side_ref,) = rest[:OUTER], rest[OUTER:]
    me = place_ref[0]
    outer = me // place_ref[2]
    heads = out_ref.shape[0] // OUTER
    tiles = heads * uv_ref.shape[1] // TILE
    side_ref[...] = jnp.zeros_like(side_ref)
    for part in range(TILE):
        side_ref[part : part + 1, :LANES] = router_ref[
            :, part * LANES : (part + 1) * LANES
        ].astype(jnp.float32)
    choices, rows = routes_ref.shape
    side_ref[:choices, LANES : LANES + rows] = routes_ref[...].astype(jnp.float32)
    side = side_ref[...].astype(jnp.bfloat16)
    for step in range(OUTER):
        target = outer ^ step
        block = block_refs[step]
        block[0, :, :D] = out_ref[pl.ds(target * heads, heads)].reshape(TILE, D)
        uv = uv_ref[pl.ds(target * heads, heads)].reshape(tiles * TILE, LANES)
        for tile in range(tiles):
            at = D + tile * LANES
            block[0, :, at : at + LANES] = uv[tile * TILE : (tile + 1) * TILE]
        block[0, :, D + tiles * LANES :] = side


def spread_kernel(units, place_ref, gate_ref, up_ref, down_ref, *out_refs):
    block_refs, (down_a_ref, down_b_ref) = out_refs[:-2], out_refs[-2:]
    me = place_ref[0]
    lower = me < block_refs[0].shape[0] * OUTER // 2
    first, second = down_ref[:units], down_ref[units:]
    down_a_ref[...] = jnp.where(lower, first, second)
    down_b_ref[...] = jnp.where(lower, second, first)
    inner = block_refs[0].shape[0]
    padded = block_refs[0].shape[1] // 2
    for step in range(OUTER):
        block_refs[step][...] = jnp.zeros_like(block_refs[step])
    for member in range(inner * OUTER):
        offset = member ^ me
        step, near = offset // inner, offset % inner
        rows = slice(member * units, (member + 1) * units)
        for outer in range(OUTER):

            @pl.when(step == outer)
            def _():
                block_refs[outer][near, :units] = gate_ref[rows]
                block_refs[outer][near, padded : padded + units] = up_ref[rows]


def small_kernel(place_ref, kept_ref, far_ref, router_ref, small_ref, fold_ref):
    me = place_ref[0]
    members = kept_ref.shape[0] + far_ref.shape[0]
    small_ref[...] = jnp.zeros_like(small_ref)
    half = LANES // 2
    padded = kept_ref.shape[1] // 2
    for member in range(members):
        ref, i = (kept_ref, member) if member < members // 2 else (far_ref, member - members // 2)
        holder = me ^ chain_offset(member, members)
        lanes = pl.ds(pl.multiple_of(holder * LANES, LANES), LANES)
        small_ref[:padded, lanes] = ref[i, :padded]
        small_ref[half : half + padded, lanes] = ref[i, padded:]
    fold_ref[...] = router_ref[...].reshape(members * TILE, LANES).astype(jnp.float32)
    for part in range(TILE):
        small_ref[LANES - members :, part * LANES : (part + 1) * LANES] = fold_ref[
            pl.ds(part, members, stride=TILE), :
        ].astype(jnp.bfloat16)


def attend_kernel(
    length_ref, query_ref, latent_ref, dec_query_ref, dec_latent_ref, cache_ref, sink_ref,
    out_ref, rows_ref, dec_ref, fold_ref,
):
    span, heads, _ = query_ref.shape
    scale_qk = (QK_NOPE + ROPE) ** (-0.5)
    square = (heads, heads)
    diagonal = lax.broadcasted_iota(jnp.int32, square, 0) == lax.broadcasted_iota(
        jnp.int32, square, 1
    )
    sinks = jnp.sum(
        jnp.where(diagonal, jnp.broadcast_to(sink_ref[...], square), 0.0), axis=1, keepdims=True
    )
    latent = latent_ref[...]
    query = query_ref[...].reshape(span * heads, query_ref.shape[2])
    scores = (
        lax.dot_general(query, latent, ROWS_CONTRACT, preferred_element_type=jnp.float32) * scale_qk
    )
    token = lax.broadcasted_iota(jnp.int32, scores.shape, 0) // heads
    allowed = lax.broadcasted_iota(jnp.int32, scores.shape, 1) <= token
    masked = jnp.where(allowed, scores, NEG_FILL)
    sink_rows = jnp.broadcast_to(sinks[None], (span, heads, 1)).reshape(span * heads, 1)
    top = jnp.maximum(jnp.max(masked, axis=1, keepdims=True), sink_rows)
    terms = jnp.where(allowed, jnp.exp(masked - top), 0.0)
    total = jnp.sum(terms, axis=1, keepdims=True) + jnp.exp(sink_rows - top)
    numer = jnp.dot(
        terms.astype(jnp.bfloat16), latent[:, :LATENT], preferred_element_type=jnp.float32
    )
    attended = numer / total
    per_block = heads // out_ref.shape[0]
    parts = LATENT // LANES
    for part in range(parts):
        rows_ref[part] = attended[:, part * LANES : (part + 1) * LANES]
        for head in range(heads):
            at = (head % per_block) * LATENT + part * LANES
            out_ref[head // per_block, :, at : at + LANES] = rows_ref[
                part, pl.ds(head, span, stride=heads), :
            ].astype(jnp.bfloat16)

    window = cache_ref.shape[2]
    length = length_ref[0]
    slot = lax.broadcasted_iota(jnp.int32, (heads, window), 1)
    position = length - 1 - lax.rem(length - 1 - slot + window, window)
    usable = (position >= 0) & (position > length - window)
    dec_query = dec_query_ref[0]
    dec_latent = dec_latent_ref[...]
    cache = cache_ref[0]
    cache_scores = (
        jnp.dot(dec_query, cache, preferred_element_type=jnp.float32) * scale_qk
    )
    own = (
        jnp.sum(
            dec_query.astype(jnp.float32) * dec_latent.astype(jnp.float32), axis=1, keepdims=True
        )
        * scale_qk
    )
    cache_masked = jnp.where(usable, cache_scores, NEG_FILL)
    dec_top = jnp.maximum(
        jnp.maximum(jnp.max(cache_masked, axis=1, keepdims=True), own), sinks
    )
    cache_exp = jnp.where(usable, jnp.exp(cache_masked - dec_top), 0.0)
    own_exp = jnp.exp(own - dec_top)
    dec_numer = lax.dot_general(
        cache_exp.astype(jnp.bfloat16),
        cache[:LATENT, :],
        ROWS_CONTRACT,
        preferred_element_type=jnp.float32,
    )
    dec_numer = dec_numer + own_exp.astype(jnp.bfloat16).astype(jnp.float32) * dec_latent[
        :, :LATENT
    ].astype(jnp.float32)
    dec_total = jnp.sum(cache_exp, axis=1, keepdims=True) + own_exp + jnp.exp(sinks - dec_top)
    dec_attended = dec_numer / dec_total
    blocks = out_ref.shape[0]
    fold_ref[...] = jnp.zeros_like(fold_ref)
    for part in range(parts):
        dec_ref[part] = dec_attended[:, part * LANES : (part + 1) * LANES]
        for head in range(per_block):
            fold_ref[pl.ds(head * parts + part, blocks, stride=TILE), :] = dec_ref[
                part, pl.ds(head, blocks, stride=per_block), :
            ]
    out_ref[:, :, per_block * LATENT :] = (
        fold_ref[...].astype(jnp.bfloat16).reshape(blocks, TILE, LANES)
    )


def project_kernel(place_ref, att_ref, *rest):
    piece_refs, (out_ref, router_ref, routes_ref, rows_ref, fold_ref, uv_ref) = rest[:-6], rest[-6:]
    pieces = [(ref, i) for ref in piece_refs for i in range(ref.shape[0])]
    for step, (ref, i) in enumerate(pieces):
        router_ref[step] = ref[i, :, -2 * LANES : -LANES]
        routes_ref[step] = ref[i, :, -LANES:]
    me = place_ref[0]
    blocks, span, width = att_ref.shape
    width -= LANES
    members = len(pieces)
    heads = width // LATENT
    latent_rows = LATENT // members
    tiles = latent_rows // TILE
    value_rows = TILE // heads
    rows_ref[: blocks * span, :] = att_ref[:, :, :width].reshape(blocks * span, width)
    fold_ref[...] = att_ref[:, :, width:].reshape(blocks * TILE, LANES).astype(jnp.float32)
    dec_rows = jnp.concatenate(
        [fold_ref[pl.ds(i, blocks, stride=TILE), :] for i in range(width // LANES)], axis=1
    )
    dec_rows = jnp.concatenate([dec_rows, jnp.zeros((TILE - blocks, width), jnp.float32)], axis=0)
    rows_ref[blocks * span :, :] = dec_rows.astype(jnp.bfloat16)
    for step in range(members):
        holder = me ^ chain_offset(step, members)
        for head in range(heads):
            for tile in range(tiles):
                at = D + (head * tiles + tile) * LANES
                start = pl.multiple_of(head * LATENT + holder * latent_rows + tile * TILE, TILE)
                ref, i = pieces[step]
                uv_ref[pl.ds(start, TILE), :] = ref[i, :, at : at + LANES]
    value = lax.broadcasted_iota(jnp.int32, (LANES, members * TILE), 0)
    column = lax.broadcasted_iota(jnp.int32, (LANES, members * TILE), 1)
    step = column // TILE
    holder = chain_offset(step, members) ^ me
    wanted = holder * value_rows + column % value_rows
    column_head = (column % TILE) // value_rows
    spread = []
    for head in range(heads):
        order = jnp.where((value == wanted) & (column_head == head), 1.0, 0.0).astype(jnp.bfloat16)
        spread.append(
            jnp.dot(
                uv_ref[head * LATENT : (head + 1) * LATENT, :],
                order,
                preferred_element_type=jnp.float32,
            ).astype(jnp.bfloat16)
        )
    head_values = jnp.dot(
        rows_ref[...], jnp.concatenate(spread, axis=0), preferred_element_type=jnp.float32
    ).astype(jnp.bfloat16)
    out_rows = jnp.concatenate([ref[i, :, :D] for ref, i in pieces], axis=0)
    partial_rows = jnp.dot(head_values, out_rows, preferred_element_type=jnp.float32)
    split = blocks * span
    out_ref[:, :, :D] = partial_rows[:split].astype(jnp.bfloat16).reshape(blocks, span, D)
    for part in range(TILE):
        fold_ref[pl.ds(part, blocks, stride=TILE), :] = partial_rows[
            split : split + blocks, part * LANES : (part + 1) * LANES
        ]
    out_ref[:, :, D:] = fold_ref[...].astype(jnp.bfloat16).reshape(blocks, TILE, LANES)


def chain_offset(step, members):
    inner = members // OUTER
    offset = (step % OUTER) * inner
    rest = step // OUTER
    bit = inner // 2
    while bit:
        offset = offset + (rest % 2) * bit
        rest = rest // 2
        bit //= 2
    return offset


def route_kernel(
    place_ref, plane_ref, other_ref, select_ref, scatter_ref, chosen_ref
):
    me, group = place_ref[0], place_ref[1]
    members = plane_ref.shape[0]
    homes = 2 * members
    total = chosen_ref.shape[0]
    pre_total = homes * TILE
    slots = select_ref.shape[0]

    def home_of(token):
        return jnp.where(token < pre_total, token // TILE, token - pre_total)

    def row_of(token):
        return jnp.where(token < pre_total, token % TILE, TILE)

    def place_of(token):
        place = home_place(home_of(token), me, group, members)
        return jnp.where(token < pre_total, place * TILE + token % TILE, pre_total + place)

    def iota(shape, axis):
        return lax.broadcasted_iota(jnp.int32, shape, axis)

    token = iota((total, homes), 0)
    home = home_of(token)
    held = ((home // (members // 2)) % 2) * members + (home // members) * (members // 2) + home % (
        members // 2
    )
    pick = jnp.where(held == iota((total, homes), 1), 1.0, 0.0).astype(jnp.bfloat16)
    own_row = iota((total, LANES), 1) == row_of(iota((total, LANES), 0))
    lane = iota((total, LANES), 1)
    lane_expert = jnp.where(
        lane >= LANES - members,
        chain_offset(lane - jnp.where(lane >= LANES - members, LANES - members, 0), members) ^ me,
        -1,
    ).astype(jnp.float32)
    chosen = jnp.zeros((total, LANES), jnp.float32)
    mine = jnp.zeros((total, LANES), jnp.float32)
    for k in range(TOPK):
        table = jnp.concatenate([plane_ref[:, k, :], other_ref[:, k, :]], axis=0)
        spread = jnp.dot(pick, table, preferred_element_type=jnp.float32)
        expert = jnp.sum(jnp.where(own_row, spread, 0.0), axis=1, keepdims=True)
        chosen = chosen + jnp.where(expert == lane_expert, 1.0, 0.0)
        mine = mine + jnp.where(own_row & (spread == me.astype(jnp.float32)), 1.0, 0.0)
    chosen_ref[...] = chosen.astype(jnp.bfloat16)
    mine_row = lax.dot_general(
        jnp.ones((8, LANES), jnp.bfloat16),
        mine.astype(jnp.bfloat16),
        ROWS_CONTRACT,
        preferred_element_type=jnp.float32,
    )
    square = (total, total)
    place_row = place_of(iota((8, total), 1))[:1]
    place_column = place_of(iota((total, LANES), 0))[:, :1]
    earlier = jnp.where(place_column <= place_row, 1.0, 0.0).astype(jnp.bfloat16)
    rank_row = jnp.dot(
        mine_row.astype(jnp.bfloat16), earlier, preferred_element_type=jnp.float32
    )[:1]
    slot = (iota((slots, total), 0) + 1).astype(jnp.float32)
    select = jnp.where((slot == rank_row) & (mine_row[:1] > 0.0), 1.0, 0.0).astype(jnp.bfloat16)
    same = jnp.where(iota(square, 0) == iota(square, 1), 1.0, 0.0).astype(jnp.bfloat16)
    select_ref[...] = select
    scatter_ref[...] = lax.dot_general(
        same, select, ROWS_CONTRACT, preferred_element_type=jnp.float32
    ).astype(jnp.bfloat16)


def home_place(index, me, group, members):
    half = members // 2
    last, home_group = index // members, (index // half) % 2
    member = chain_offset(index % half + last * half, members) ^ me
    return last * members + (home_group ^ group) * half + member // 2


def norm_kernel(partial_ref, resid_ref, gain_ref, hidden_ref, normed_ref):
    summed = partial_ref[0].astype(jnp.float32)
    for i in range(1, partial_ref.shape[0]):
        summed = summed + partial_ref[i].astype(jnp.float32)
    hidden = (resid_ref[...].astype(jnp.float32) + summed).astype(jnp.bfloat16)
    hidden_ref[...] = hidden
    hidden = hidden.astype(jnp.float32)
    gain = gain_ref[...].astype(jnp.float32)
    pre, dec = hidden[:, :D], hidden[:, D:]
    pre_mean = jnp.sum(pre * pre, axis=1, keepdims=True) / D
    dec_mean = jnp.sum(jnp.sum(dec * dec, axis=1, keepdims=True), axis=0, keepdims=True) / D
    normed_ref[:, :D] = (pre * lax.rsqrt(pre_mean + NORM_EPS) * gain[:1, :D]).astype(jnp.bfloat16)
    normed_ref[:, D:] = (dec * lax.rsqrt(dec_mean + NORM_EPS) * gain[:, D:]).astype(jnp.bfloat16)


def expert_kernel(units, small_ref, select_ref, chosen_ref, gate_ref, up_ref, *rest):
    piece_refs, outs = rest[:-7], rest[-7:]
    act_ref, shared_ref, rows_ref, weight_ref, fold_ref, pre_ref, dec_ref = outs
    pre_total = pre_ref.shape[0]
    homes = pre_total // TILE
    row = 0
    for ref in piece_refs:
        count = ref.shape[0]
        pre_ref[row : row + count, :] = ref[:, :D]
        fold_ref[row : row + count, :] = ref[:, D:].astype(jnp.float32)
        row += count
    for part in range(TILE):
        dec_ref[:, part * LANES : (part + 1) * LANES] = fold_ref[
            pl.ds(part, homes, stride=TILE), :
        ].astype(jnp.bfloat16)
    pre = pre_ref[...]
    dec = dec_ref[...]
    small = small_ref[...]
    first = jnp.concatenate(
        [
            lax.dot_general(pre, small, ROWS_CONTRACT, preferred_element_type=jnp.float32),
            lax.dot_general(dec, small, ROWS_CONTRACT, preferred_element_type=jnp.float32),
        ],
        axis=0,
    )
    half = LANES // 2
    members = len(piece_refs)
    gate_part = first[:, :units]
    up_part = first[:, half : half + units]
    shared_act = (gate_part / (1.0 + jnp.exp(-gate_part)) * up_part).astype(jnp.bfloat16)
    shared_ref[...] = jnp.zeros_like(shared_ref)
    split = pre_total // 2
    middle = pre_total + homes // 2
    shared_ref[:split, :units] = shared_act[:split]
    shared_ref[:split, half : half + units] = shared_act[split:pre_total]
    shared_ref[split:, :units] = shared_act[pre_total:middle]
    shared_ref[split:, half : half + units] = shared_act[middle:]
    logits = first[:, LANES - members :]
    scores = 1.0 / (1.0 + jnp.exp(-logits))
    token_weight = (
        ROUTE_SCALE
        * scores[:, :1]
        / jnp.sum(scores * chosen_ref[:, LANES - members :], axis=1, keepdims=True)
    )
    high = token_weight.astype(jnp.bfloat16)
    rest = token_weight - high.astype(jnp.float32)
    middle = rest.astype(jnp.bfloat16)
    rest = (rest - middle.astype(jnp.float32)).astype(jnp.bfloat16)
    select = select_ref[...]
    weights = jnp.dot(
        select, jnp.concatenate([high, middle, rest], axis=1), preferred_element_type=jnp.float32
    )
    weight_ref[...] = jnp.broadcast_to(jnp.sum(weights, axis=1, keepdims=True), weight_ref.shape)
    rows_ref[...] = (
        jnp.dot(select[:, :pre_total], pre, preferred_element_type=jnp.float32)
        + jnp.dot(select[:, pre_total:], dec, preferred_element_type=jnp.float32)
    ).astype(jnp.bfloat16)
    hidden_kernel(0, rows_ref, weight_ref, gate_ref, up_ref, act_ref)


def hidden_kernel(start, rows_ref, weight_ref, gate_ref, up_ref, act_ref):
    rows = rows_ref[...]
    count = act_ref.shape[1]
    gate = lax.dot_general(
        rows, gate_ref[0, start : start + count], ROWS_CONTRACT, preferred_element_type=jnp.float32
    )
    up = lax.dot_general(
        rows, up_ref[0, start : start + count], ROWS_CONTRACT, preferred_element_type=jnp.float32
    )
    act_ref[...] = (gate / (1.0 + jnp.exp(-gate)) * up * weight_ref[:, :1]).astype(jnp.bfloat16)


def down_kernel(
    place_ref, act_a_ref, act_b_ref, other_a_ref, other_b_ref, shared_ref, shared_other_ref,
    down_ref, down_a_ref, down_b_ref, scatter_ref, kept_ref, sent_ref, fold_ref,
):
    me, group = place_ref[0], place_ref[1]
    columns = down_ref.shape[2]
    units = down_a_ref.shape[0]
    width = down_ref.shape[1] // 2
    routed = jnp.zeros((act_a_ref.shape[0], columns), jnp.float32)
    for refs, which in (((act_a_ref, act_b_ref), group), ((other_a_ref, other_b_ref), 1 - group)):
        row = which * width
        for ref in refs:
            rows = down_ref[0, pl.ds(pl.multiple_of(row, TILE), ref.shape[1]), :]
            routed = routed + jnp.dot(ref[...], rows, preferred_element_type=jnp.float32)
            row = row + ref.shape[1]
    routed = routed.astype(jnp.bfloat16)
    mine_first = lax.rem(me, 2) == group
    own_down = jnp.where(mine_first, down_a_ref[...], down_b_ref[...])
    other_down = jnp.where(mine_first, down_b_ref[...], down_a_ref[...])
    both_down = jnp.concatenate([own_down, other_down], axis=0)
    half = kept_ref.shape[0]
    homes = 2 * half
    split = homes * TILE
    other = shared_other_ref[...]
    middle, decs = split // 4, other[split // 2 :].astype(jnp.float32)
    eighth = homes // 4
    other = jnp.concatenate(
        [
            other[middle : 2 * middle],
            other[:middle],
            jnp.concatenate([decs[eighth:], decs[:eighth]], axis=0).astype(jnp.bfloat16),
        ],
        axis=0,
    )
    shared = shared_ref[...]

    def down(at):
        acts = jnp.concatenate([shared[:, at : at + units], other[:, at : at + units]], axis=1)
        return jnp.dot(acts, both_down, preferred_element_type=jnp.float32)

    low_half, high_half = down(0), down(LANES // 2)
    total = jnp.dot(scatter_ref[...], routed, preferred_element_type=jnp.float32) + jnp.concatenate(
        [
            low_half[: split // 2], high_half[: split // 2], low_half[split // 2 :],
            high_half[split // 2 :],
        ],
        axis=0,
    )
    fold_ref[...] = jnp.zeros_like(fold_ref)
    for part in range(columns // LANES):
        fold_ref[pl.ds(part, homes, stride=TILE), :] = total[
            split:, part * LANES : (part + 1) * LANES
        ]
    for home in range(homes):
        place = home_place(home, me, group, half)
        ref = kept_ref if home < half else sent_ref
        at = place if home < half else place - half
        rows = slice(home * TILE, (home + 1) * TILE)
        ref[at, :, :columns] = total[rows].astype(jnp.bfloat16)
        ref[at, :, columns:] = fold_ref[rows].astype(jnp.bfloat16)


def finish_kernel(got_ref, hidden_ref, pre_ref, dec_ref):
    sources, _, width = got_ref.shape
    columns = width - LANES
    groups = D // columns
    each = sources // groups
    for group in range(groups):
        summed = got_ref[group * each].astype(jnp.float32)
        for i in range(1, each):
            summed = summed + got_ref[group * each + i].astype(jnp.float32)
        at = group * columns
        pre_ref[:, at : at + columns] = (
            hidden_ref[:, at : at + columns].astype(jnp.float32) + summed[:, :columns]
        ).astype(jnp.bfloat16)
        parts = columns // LANES
        for part in range(parts):
            row = group * parts + part
            dec_ref[:, row * LANES : (row + 1) * LANES] = (
                hidden_ref[row : row + 1, D:].astype(jnp.float32)
                + summed[part : part + 1, columns:]
            ).astype(jnp.bfloat16)


def token_shards(
    pre_query,
    pre_latent,
    pre_resid,
    dec_query,
    dec_latent,
    dec_resid,
    cache_lengths,
    latent_cache,
    sink_logits,
    uv_weight,
    out_weight,
    norm_gain,
    router,
    routes,
    gate_weight,
    up_weight,
    down_weight,
    shared_gate,
    shared_up,
    shared_down,
):
    groups = lax.axis_size("dp")
    members = lax.axis_size("expert")
    inner = members // OUTER
    homes = groups * members
    me = lax.axis_index("expert")
    my_group = lax.axis_index("dp")
    place_ids = jnp.stack([me, my_group, jnp.int32(inner)]).astype(jnp.int32)
    pre_rows = pre_query.shape[0]
    rows_dev = pre_rows + 1
    capacity = max(2, (rows_dev * TOPK + members - 1) // members)

    heads_dev, latent_rows, value_dim = uv_weight.shape
    heads_outer = heads_dev // OUTER
    uv_tiles = heads_outer * latent_rows // TILE
    block_width = D + uv_tiles * value_dim + 2 * LANES
    blocks = call(
        pack_kernel,
        [low((1, TILE, block_width))] * OUTER,
        [place_ids, out_weight, uv_weight, router.T, routes.T],
        scratch=[pltpu.VMEM((TILE, 2 * LANES), jnp.float32)],
        scalars=1,
        moved=(1, 2, 3, 4),
        vmem=60,
    )
    pair_bit = inner // 2
    near = [blocks[0]] + [swap(blocks[i], "expert", i * inner) for i in range(1, OUTER)]
    own_pair = swap(blocks[0], "expert", pair_bit)
    line = jnp.concatenate(near, axis=0)
    far_in, own_pair = lax.optimization_barrier((line[1:], own_pair))
    far_pair = swap(far_in, "expert", pair_bit)
    units = shared_gate.shape[1] // members
    padded = -(-units // TILE) * TILE
    depth = shared_gate.shape[0]
    line, line_gate = lax.optimization_barrier((line, shared_gate))
    *spread, down_a, down_b = call(
        partial(spread_kernel, units),
        [low((inner, 2 * padded, depth))] * OUTER + [low((units, shared_down.shape[1]))] * 2,
        [place_ids, line_gate.T, shared_up.T, shared_down],
        scalars=1,
    )
    far_pair, *spread = lax.optimization_barrier((far_pair, *spread))
    pieces = [line, own_pair, far_pair]
    pieces = pieces + [swap(piece, "expert", 1) for piece in pieces]

    pre_query, blocks = lax.optimization_barrier((pre_query, blocks))
    peers = groups * OUTER
    heads_block = heads_outer * LATENT
    att_blocks = call(
        attend_kernel,
        low((peers, pre_rows, heads_block + LANES)),
        [
            cache_lengths, pre_query, pre_latent, dec_query, dec_latent,
            latent_cache.swapaxes(1, 2),
            sink_logits.reshape(1, -1),
        ],
        scratch=[
            pltpu.VMEM((LATENT // LANES, pre_rows * pre_query.shape[1], LANES), jnp.float32),
            pltpu.VMEM((LATENT // LANES, pre_query.shape[1], LANES), jnp.float32),
            pltpu.VMEM((peers * TILE, LANES), jnp.float32),
        ],
        scalars=1,
        flops=100_000_000,
        moved=(1, 2, 3, 4, 5),
        vmem=60,
    )
    lines = [
        [g * members + o * inner + i for g in range(groups) for o in range(OUTER)]
        for i in range(inner)
    ]
    both = ("dp", "expert")
    att_got = lax.all_to_all(
        att_blocks, both, split_axis=0, concat_axis=0, axis_index_groups=lines, tiled=True
    )
    partial_blocks, router_blocks, routes_plane = call(
        project_kernel,
        [low((peers, pre_rows, D + LANES))] + [low((members, TILE, LANES))] * 2,
        [place_ids, att_got, *pieces],
        scratch=[
            pltpu.VMEM((peers * pre_rows + TILE, heads_block), jnp.bfloat16),
            pltpu.VMEM((peers * TILE, LANES), jnp.float32),
            pltpu.VMEM((heads_block, value_dim), jnp.bfloat16),
        ],
        scalars=1,
        flops=300_000_000,
        moved=tuple(range(2, 2 + len(pieces))),
    )
    routes_other = swap(routes_plane, "dp", 1)

    shared_got = [spread[0]] + [swap(spread[i], "expert", i * inner) for i in range(1, OUTER)]
    _, *shared_got = lax.optimization_barrier((partial_blocks, *shared_got))
    kept = jnp.concatenate([block[:pair_bit] for block in shared_got], axis=0)
    sent = jnp.concatenate([block[pair_bit:] for block in shared_got], axis=0)
    far = swap(sent, "expert", pair_bit)
    pre_total = homes * pre_rows
    total = pre_total + homes
    slots = homes * capacity
    select, scatter, chosen = call(
        route_kernel,
        [low((slots, total)), low((total, slots)), low((total, LANES))],
        [place_ids, routes_plane, routes_other],
        scalars=1,
        vmem=16,
    )
    far, select = lax.optimization_barrier((far, select))
    shared_kept = jnp.concatenate([kept[::pair_bit], far[::pair_bit]], axis=0)
    shared_sent = jnp.concatenate([kept[1::pair_bit], far[1::pair_bit]], axis=0)
    shared_far = swap(shared_sent, "expert", 1)
    small = call(
        small_kernel,
        low((LANES, D)),
        [place_ids, shared_kept, shared_far, router_blocks],
        scratch=[pltpu.VMEM((members * TILE, LANES), jnp.float32)],
        scalars=1,
    )
    partial_got = lax.all_to_all(
        partial_blocks, both, split_axis=0, concat_axis=0, axis_index_groups=lines, tiled=True
    )
    middle = OUTER // 2
    partial_got, select, scatter, chosen, small = lax.optimization_barrier(
        (partial_got, select, scatter, chosen, small)
    )
    resid = jnp.concatenate([pre_resid, fold_row(dec_resid)], axis=1)
    gain = jnp.concatenate(
        [jnp.broadcast_to(norm_gain[None], (TILE, D)), norm_gain.reshape(TILE, LANES)], axis=1
    )
    hidden, normed = call(
        norm_kernel, [low(resid.shape)] * 2, [partial_got, resid, gain], flops=20_000_000_000
    )

    line = [normed] + [swap(normed, "expert", step * inner) for step in range(1, OUTER)]
    middle = OUTER // 2
    row_pieces = []
    for part in (line[:middle], line[middle:]):
        row_pieces.append(jnp.concatenate(part, axis=0))
    piece_a, piece_b = row_pieces
    a_pair, b_group = swap(piece_a, "expert", pair_bit), swap(piece_b, "dp", 1)
    a_group, b_pair = swap(piece_a, "dp", 1), swap(piece_b, "expert", pair_bit)
    a_both, b_both = swap(a_pair, "dp", 1), swap(b_group, "expert", pair_bit)
    row_pieces = [piece_a, piece_b, a_pair, b_pair, a_group, b_group, a_both, b_both]
    row_pieces = row_pieces + [swap(piece, "expert", 1) for piece in row_pieces]

    width = gate_weight.shape[2]
    first_width = -(-width // (2 * LANES)) * LANES
    gate_rows, up_rows = gate_weight.swapaxes(1, 2), up_weight.swapaxes(1, 2)
    act_a, shared_act, expert_rows, slot_weight = call(
        partial(expert_kernel, units),
        [
            low((slots, first_width)), low((total // 2, LANES)), low((slots, D)),
            jax.ShapeDtypeStruct((slots, LANES), jnp.float32),
        ],
        [small, select, chosen, gate_rows, up_rows, *row_pieces],
        scratch=[
            pltpu.VMEM((pre_total, LANES), jnp.float32),
            pltpu.VMEM((pre_total, D), jnp.bfloat16),
            pltpu.VMEM((homes, D), jnp.bfloat16),
        ],
        flops=2_000_000_000,
        vmem=20,
    )
    act_a_other = swap(act_a, "dp", 1)
    act_b = call(
        partial(hidden_kernel, first_width),
        low((slots, width - first_width)),
        [expert_rows, slot_weight, gate_rows, up_rows],
        flops=1_000_000_000,
        vmem=12,
    )
    act_b_other = swap(act_b, "dp", 1)
    shared_act_other = swap(shared_act, "dp", 1)
    act_a, down_a, down_b = lax.optimization_barrier((act_a, down_a, down_b))
    half = members // 2
    down_a = lax.ppermute(
        down_a,
        "expert",
        [(i, 2 * i if i < half else 2 * (i - half) + 1) for i in range(members)],
    )
    down_b = lax.ppermute(
        down_b,
        "expert",
        [(i, 2 * i + 1 if i < half else 2 * (i - half)) for i in range(members)],
    )
    col_width = down_weight.shape[2]
    kept, sent = call(
        down_kernel,
        [low((homes // 2, TILE, col_width + LANES))] * 2,
        [
            place_ids, act_a, act_b, act_a_other, act_b_other, shared_act, shared_act_other,
            down_weight, down_a, down_b, scatter,
        ],
        scratch=[pltpu.VMEM((pre_total, LANES), jnp.float32)],
        scalars=1,
        flops=1_000_000_000,
        vmem=20,
    )
    pair_sum = (kept.astype(jnp.float32) + swap(sent, "expert", 1).astype(jnp.float32)).astype(
        jnp.bfloat16
    )
    halves = [
        [g * members + 2 * i + b for g in range(groups) for i in range(members // 2)]
        for b in range(2)
    ]
    home_got = lax.all_to_all(
        pair_sum, both, split_axis=0, concat_axis=0, axis_index_groups=halves, tiled=True
    )
    return tuple(
        call(finish_kernel, [low(pre_resid.shape), low(dec_resid.shape)], [home_got, hidden])
    )


def fits(mesh, heads, ff):
    groups, members = mesh.shape["dp"], mesh.shape["expert"]
    return (
        groups == 2
        and members % (2 * OUTER) == 0
        and (heads // groups) % OUTER == 0
        and ff % (groups * members) == 0
    )


def solution(mesh):
    in_specs = (
        P(("dp", "expert"), None, None),
        P(("dp", "expert"), None),
        P(("dp", "expert"), None),
        P(("dp", "expert"), None, None),
        P(("dp", "expert"), None),
        P(("dp", "expert"), None),
        P(("dp", "expert")),
        P(("dp", "expert"), None, None),
        P(),
        P("dp", "expert", None),
        P("dp", "expert", None),
        P(),
        P(None, "expert"),
        P(("dp", "expert"), None),
        P("expert", None, "dp"),
        P("expert", None, "dp"),
        P("expert", None, "dp"),
        P("expert", "dp"),
        P("expert", "dp"),
        P("expert", "dp"),
    )
    out_specs = (P(("dp", "expert"), None), P(("dp", "expert"), None))

    def layer(*args):
        plan = token_shards if fits(mesh, args[9].shape[0], args[17].shape[1]) else shards
        return jax.shard_map(
            plan, mesh=mesh, in_specs=in_specs, out_specs=out_specs, check_vma=False
        )(*args)

    return layer
```

```python
from functools import partial

import jax
import jax.numpy as jnp
from jax import lax
from jax.experimental import pallas as pl
from jax.experimental.pallas import tpu as pltpu
from jax.sharding import PartitionSpec as P

D = 2048
LATENT = 512
ROPE = 64
QK_NOPE = 128
TOPK = 6


ROUTE_SCALE = 2.446
NORM_EPS = 1e-06
NEG_FILL = -1e30


def assign_slots(route_rows, experts):
    flat_routes = route_rows.reshape(-1)
    one_hot = (flat_routes[:, None] == jnp.arange(experts, dtype=jnp.int32)[None, :]).astype(
        jnp.int32
    )
    running = jnp.cumsum(one_hot, axis=0)
    slot_rank = jnp.sum(running * one_hot, axis=1) - 1
    return slot_rank.reshape(route_rows.shape)


def dispatch_matrix(route_rows, slot_rows, experts, capacity):
    target = route_rows * capacity + slot_rows
    places = jnp.arange(experts * capacity, dtype=jnp.int32)
    total = jnp.zeros((route_rows.shape[0], experts * capacity), jnp.bfloat16)
    for column in range(route_rows.shape[1]):
        total = total + (target[:, column][:, None] == places[None, :]).astype(jnp.bfloat16)
    return total


def shards(
    pre_query,
    pre_latent,
    pre_resid,
    dec_query,
    dec_latent,
    dec_resid,
    cache_lengths,
    latent_cache,
    sink_logits,
    uv_weight,
    out_weight,
    norm_gain,
    router,
    routes,
    gate_weight,
    up_weight,
    down_weight,
    shared_gate,
    shared_up,
    shared_down,
):
    groups = lax.axis_size("dp")
    members = lax.axis_size("expert")
    pre_rows = pre_query.shape[0]
    rows_dev = pre_rows + 1
    scale_qk = (QK_NOPE + ROPE) ** (-0.5)
    pre_scores = (
        jnp.einsum("thc,uc->thu", pre_query, pre_latent, preferred_element_type=jnp.float32)
        * scale_qk
    )
    places = jnp.arange(pre_rows, dtype=jnp.int32)
    allowed = (places[None, :] <= places[:, None])[:, None, :]
    masked = jnp.where(allowed, pre_scores, NEG_FILL)
    pre_max = jnp.maximum(jnp.max(masked, axis=2), sink_logits[None, :])
    exp_terms = jnp.where(allowed, jnp.exp(masked - pre_max[:, :, None]), 0.0)
    denominator = jnp.sum(exp_terms, axis=2) + jnp.exp(sink_logits[None, :] - pre_max)
    numerator = jnp.einsum(
        "thu,ul->thl",
        exp_terms.astype(jnp.bfloat16),
        pre_latent[:, :LATENT],
        preferred_element_type=jnp.float32,
    )
    pre_att = (numerator / denominator[:, :, None]).astype(jnp.bfloat16)
    window = latent_cache.shape[1]
    slot_ids = jnp.arange(window, dtype=jnp.int32)
    newest = cache_lengths - 1
    position = newest[:, None] - jnp.mod(newest[:, None] - slot_ids[None, :], window)
    usable = ((position >= 0) & (position > cache_lengths[:, None] - window))[:, None, :]
    cache_scores = (
        jnp.einsum("rhc,rsc->rhs", dec_query, latent_cache, preferred_element_type=jnp.float32)
        * scale_qk
    )
    own_scores = (
        jnp.einsum("rhc,rc->rh", dec_query, dec_latent, preferred_element_type=jnp.float32)
        * scale_qk
    )
    cache_masked = jnp.where(usable, cache_scores, NEG_FILL)
    top_score = jnp.maximum(
        jnp.maximum(jnp.max(cache_masked, axis=2), own_scores), sink_logits[None, :]
    )
    cache_exp = jnp.where(usable, jnp.exp(cache_masked - top_score[:, :, None]), 0.0)
    own_exp = jnp.exp(own_scores - top_score)
    dec_numer = jnp.einsum(
        "rhs,rsl->rhl",
        cache_exp.astype(jnp.bfloat16),
        latent_cache[:, :, :LATENT],
        preferred_element_type=jnp.float32,
    )
    dec_numer = dec_numer + own_exp.astype(jnp.bfloat16).astype(jnp.float32)[
        :, :, None
    ] * dec_latent[:, None, :LATENT].astype(jnp.float32)
    dec_total = jnp.sum(cache_exp, axis=2) + own_exp + jnp.exp(sink_logits[None, :] - top_score)
    dec_att = (dec_numer / dec_total[:, :, None]).astype(jnp.bfloat16)
    attention = jnp.concatenate([pre_att, dec_att], axis=0)
    spread = lax.all_to_all(attention, "dp", split_axis=1, concat_axis=0, tiled=True)
    uv_full, out_full = (
        lax.all_gather(uv_weight, "expert", axis=1, tiled=True),
        lax.all_gather(out_weight, "expert", axis=1, tiled=True),
    )
    head_values = jnp.einsum(
        "thl,hlv->thv", spread, uv_full, preferred_element_type=jnp.float32
    ).astype(jnp.bfloat16)
    head_partial = jnp.einsum(
        "thv,hvd->td", head_values, out_full, preferred_element_type=jnp.float32
    )
    attn_out = lax.psum_scatter(
        head_partial.astype(jnp.bfloat16), "dp", scatter_dimension=0, tiled=True
    ).astype(jnp.float32)
    resid = jnp.concatenate([pre_resid, dec_resid], axis=0)
    hidden = (resid.astype(jnp.float32) + attn_out).astype(jnp.bfloat16)
    hidden_up = lax.optimization_barrier(hidden).astype(jnp.float32)
    mean_square = jnp.mean(hidden_up * hidden_up, axis=1, keepdims=True)
    normed = (
        hidden_up * lax.rsqrt(mean_square + NORM_EPS) * norm_gain.astype(jnp.float32)[None, :]
    ).astype(jnp.bfloat16)
    capacity = max(2, (rows_dev * TOPK + members - 1) // members)
    group_tokens = lax.all_gather(normed, "dp", axis=0, tiled=True)
    group_routes = lax.all_gather(routes, "dp", axis=0, tiled=True)
    routes_by_group = group_routes.reshape(groups, rows_dev, TOPK)
    slots_by_group = jax.vmap(partial(assign_slots, experts=members))(routes_by_group)
    tokens_by_group = group_tokens.reshape(groups, rows_dev, D)
    all_matrix = jax.vmap(partial(dispatch_matrix, experts=members, capacity=capacity))(
        routes_by_group, slots_by_group
    )
    all_matrix = all_matrix.reshape(groups, rows_dev, members, capacity)
    outgoing = jnp.einsum(
        "grxc,grd->xgcd", all_matrix, tokens_by_group, preferred_element_type=jnp.bfloat16
    )
    expert_rows = lax.all_to_all(outgoing, "expert", split_axis=0, concat_axis=0, tiled=True)
    expert_rows = expert_rows.reshape(-1, D)
    gate_score = jax.nn.sigmoid(
        jnp.dot(expert_rows, router[:, 0], preferred_element_type=jnp.float32)
    )
    gate_proj = jnp.dot(expert_rows, gate_weight[0], preferred_element_type=jnp.float32)
    up_proj = jnp.dot(expert_rows, up_weight[0], preferred_element_type=jnp.float32)
    expert_act = (jax.nn.silu(gate_proj) * up_proj).astype(jnp.bfloat16)
    shared_gate_full, shared_up_full, shared_down_full = (
        lax.all_gather(shared_gate, "expert", axis=0, tiled=True),
        lax.all_gather(shared_up, "expert", axis=0, tiled=True),
        lax.all_gather(shared_down, "expert", axis=0, tiled=True),
    )
    shared_act = (
        jax.nn.silu(jnp.dot(group_tokens, shared_gate_full, preferred_element_type=jnp.float32))
        * jnp.dot(group_tokens, shared_up_full, preferred_element_type=jnp.float32)
    ).astype(jnp.bfloat16)
    down_local = down_weight[0]
    col_width = down_local.shape[1]
    routed_piece = lax.all_gather(expert_act, "dp", axis=1, tiled=True)
    shared_piece = lax.all_gather(shared_act, "dp", axis=1, tiled=True)
    routed_cols = jnp.dot(routed_piece, down_local, preferred_element_type=jnp.float32)
    shared_cols = jnp.dot(shared_piece, shared_down_full, preferred_element_type=jnp.float32)
    expert_out = routed_cols.astype(jnp.bfloat16)
    shared_out = shared_cols.astype(jnp.bfloat16)
    returned = lax.all_to_all(
        expert_out.reshape(members, groups * capacity, col_width),
        "expert",
        split_axis=0,
        concat_axis=0,
        tiled=True,
    )
    returned_scores = lax.all_to_all(
        gate_score.reshape(members, groups * capacity),
        "expert",
        split_axis=0,
        concat_axis=0,
        tiled=True,
    )
    group_offset = (jnp.arange(groups, dtype=jnp.int32) * capacity)[:, None, None]
    lookup = (routes_by_group * (groups * capacity) + group_offset + slots_by_group).reshape(
        groups * rows_dev, TOPK
    )
    picked = jnp.take(returned.reshape(-1, col_width), lookup, axis=0)
    picked_scores = jnp.take(returned_scores.reshape(-1), lookup, axis=0)
    route_weight = ROUTE_SCALE * picked_scores / jnp.sum(picked_scores, axis=1, keepdims=True)
    moe_cols = shared_out.astype(jnp.float32) + jnp.sum(
        route_weight[:, :, None] * picked.astype(jnp.float32), axis=1
    )
    moe_home = lax.all_to_all(
        moe_cols.reshape(groups, rows_dev, col_width).astype(jnp.bfloat16),
        "dp",
        split_axis=0,
        concat_axis=2,
        tiled=True,
    ).astype(jnp.float32)
    final = (hidden_up + moe_home[0]).astype(jnp.bfloat16)
    return (final[:pre_rows], final[pre_rows:])


OUTER = 4
TILE = 16
LANES = 128
ROWS_CONTRACT = (((1,), (1,)), ((), ()))


def fold_row(row):
    return row.reshape(row.shape[:-2] + (TILE, row.shape[-1] // TILE))


def swap(value, axis, bit):
    size = lax.axis_size(axis)
    return lax.ppermute(value, axis, [(i, i ^ bit) for i in range(size)])


def line_swaps(blocks, inner):
    got = {i: swap(blocks[i], "expert", i * inner) for i in reversed(range(1, len(blocks)))}
    return [blocks[0]] + [got[i] for i in range(1, len(blocks))]


def call(kernel, out_shapes, args, scratch=(), scalars=0, flops=0, vmem=10, moved=(), late=(), rows=None):
    specs = []
    for i in range(len(args)):
        if i < scalars:
            specs.append(pl.BlockSpec(memory_space=pltpu.SMEM))
        elif i in moved:
            specs.append(pl.BlockSpec(memory_space=pl.ANY))
        else:
            specs.append(pl.BlockSpec(memory_space=pltpu.VMEM))
    scratch = list(scratch)
    body = kernel
    if moved:
        rows = dict(rows or {})
        shapes = {i: args[i].shape for i in moved}
        for i, (_, count) in rows.items():
            shapes[i] = (shapes[i][0], count) + shapes[i][2:]
        buffers = [pltpu.VMEM(shapes[i], args[i].dtype) for i in moved]
        scratch = scratch + buffers + [pltpu.SemaphoreType.DMA((len(moved),))]

        def body(*refs):
            rest, held, sem = refs[: -len(moved) - 1], refs[-len(moved) - 1 : -1], refs[-1]
            sources = {i: refs[i] for i in moved}
            for i, (start, count) in rows.items():
                sources[i] = refs[i].at[:, pl.ds(start, count)]
            copies = [
                pltpu.make_async_copy(sources[i], held[j], sem.at[j]) for j, i in enumerate(moved)
            ]
            for copy in copies:
                copy.start()
            for i, copy in zip(moved, copies):
                if i not in late:
                    copy.wait()
            inputs = [held[moved.index(i)] if i in moved else refs[i] for i in range(len(args))]
            if late:
                waits = [copies[moved.index(i)].wait for i in late]
                kernel(*inputs, *rest[len(args) :], waits=waits)
            else:
                kernel(*inputs, *rest[len(args) :])

    moved_bytes = sum(a.size * a.dtype.itemsize for a in args)
    single = not isinstance(out_shapes, (list, tuple))
    return pl.pallas_call(
        body,
        out_shape=out_shapes,
        in_specs=specs,
        out_specs=pl.BlockSpec(memory_space=pltpu.VMEM)
        if single
        else [pl.BlockSpec(memory_space=pltpu.VMEM)] * len(out_shapes),
        scratch_shapes=scratch,
        compiler_params=pltpu.CompilerParams(vmem_limit_bytes=vmem * 1024 * 1024),
        cost_estimate=pl.CostEstimate(flops=flops, bytes_accessed=moved_bytes, transcendentals=0),
    )(*args)


def low(shape):
    return jax.ShapeDtypeStruct(shape, jnp.bfloat16)


def pack_kernel(place_ref, out_ref, uv_ref, router_ref, routes_ref, *rest):
    block_refs, (side_ref,) = rest[:OUTER], rest[OUTER:]
    me = place_ref[0]
    outer = me // place_ref[2]
    heads = out_ref.shape[0] // OUTER
    tiles = heads * uv_ref.shape[1] // TILE
    side_ref[...] = jnp.zeros_like(side_ref)
    for part in range(TILE):
        side_ref[part : part + 1, :LANES] = router_ref[
            :, part * LANES : (part + 1) * LANES
        ].astype(jnp.float32)
    choices, rows = routes_ref.shape
    side_ref[:choices, LANES : LANES + rows] = routes_ref[...].astype(jnp.float32)
    side = side_ref[...].astype(jnp.bfloat16)
    for step in range(OUTER):
        target = outer ^ step
        block = block_refs[step]
        block[0, :, :D] = out_ref[pl.ds(target * heads, heads)].reshape(TILE, D)
        uv = uv_ref[pl.ds(target * heads, heads)].reshape(tiles * TILE, LANES)
        for tile in range(tiles):
            at = D + tile * LANES
            block[0, :, at : at + LANES] = uv[tile * TILE : (tile + 1) * TILE]
        block[0, :, D + tiles * LANES :] = side


def spread_kernel(units, place_ref, gate_ref, up_ref, down_ref, *out_refs):
    block_refs, (down_a_ref, down_b_ref) = out_refs[:-2], out_refs[-2:]
    me = place_ref[0]
    lower = me < block_refs[0].shape[0] * OUTER // 2
    first, second = down_ref[:units], down_ref[units:]
    down_a_ref[...] = jnp.where(lower, first, second)
    down_b_ref[...] = jnp.where(lower, second, first)
    inner = block_refs[0].shape[0]
    padded = block_refs[0].shape[1] // 2
    for step in range(OUTER):
        block_refs[step][...] = jnp.zeros_like(block_refs[step])
    for member in range(inner * OUTER):
        offset = member ^ me
        step, near = offset // inner, offset % inner
        rows = slice(member * units, (member + 1) * units)
        for outer in range(OUTER):

            @pl.when(step == outer)
            def _():
                block_refs[outer][near, :units] = gate_ref[rows]
                block_refs[outer][near, padded : padded + units] = up_ref[rows]


def small_kernel(place_ref, kept_ref, far_ref, router_ref, small_ref, fold_ref):
    me = place_ref[0]
    members = kept_ref.shape[0] + far_ref.shape[0]
    small_ref[...] = jnp.zeros_like(small_ref)
    half = LANES // 2
    padded = kept_ref.shape[1] // 2
    for member in range(members):
        ref, i = (kept_ref, member) if member < members // 2 else (far_ref, member - members // 2)
        holder = me ^ chain_offset(member, members)
        lanes = pl.ds(pl.multiple_of(holder * LANES, LANES), LANES)
        small_ref[:padded, lanes] = ref[i, :padded]
        small_ref[half : half + padded, lanes] = ref[i, padded:]
    fold_ref[...] = router_ref[...].reshape(members * TILE, LANES).astype(jnp.float32)
    for part in range(TILE):
        small_ref[LANES - members :, part * LANES : (part + 1) * LANES] = fold_ref[
            pl.ds(part, members, stride=TILE), :
        ].astype(jnp.bfloat16)


def attend_kernel(
    length_ref, query_ref, latent_ref, dec_query_ref, dec_latent_ref, cache_ref, sink_ref,
    out_ref, rows_ref, dec_ref, fold_ref,
):
    span, heads, _ = query_ref.shape
    scale_qk = (QK_NOPE + ROPE) ** (-0.5)
    square = (heads, heads)
    diagonal = lax.broadcasted_iota(jnp.int32, square, 0) == lax.broadcasted_iota(
        jnp.int32, square, 1
    )
    sinks = jnp.sum(
        jnp.where(diagonal, jnp.broadcast_to(sink_ref[...], square), 0.0), axis=1, keepdims=True
    )
    latent = latent_ref[...]
    query = query_ref[...].reshape(span * heads, query_ref.shape[2])
    scores = (
        lax.dot_general(query, latent, ROWS_CONTRACT, preferred_element_type=jnp.float32) * scale_qk
    )
    token = lax.broadcasted_iota(jnp.int32, scores.shape, 0) // heads
    allowed = lax.broadcasted_iota(jnp.int32, scores.shape, 1) <= token
    masked = jnp.where(allowed, scores, NEG_FILL)
    sink_rows = jnp.broadcast_to(sinks[None], (span, heads, 1)).reshape(span * heads, 1)
    top = jnp.maximum(jnp.max(masked, axis=1, keepdims=True), sink_rows)
    terms = jnp.where(allowed, jnp.exp(masked - top), 0.0)
    total = jnp.sum(terms, axis=1, keepdims=True) + jnp.exp(sink_rows - top)
    numer = jnp.dot(
        terms.astype(jnp.bfloat16), latent[:, :LATENT], preferred_element_type=jnp.float32
    )
    attended = numer / total
    per_block = heads // out_ref.shape[0]
    parts = LATENT // LANES
    for part in range(parts):
        rows_ref[part] = attended[:, part * LANES : (part + 1) * LANES]
        for head in range(heads):
            at = (head % per_block) * LATENT + part * LANES
            out_ref[head // per_block, :, at : at + LANES] = rows_ref[
                part, pl.ds(head, span, stride=heads), :
            ].astype(jnp.bfloat16)

    window = cache_ref.shape[2]
    length = length_ref[0]
    slot = lax.broadcasted_iota(jnp.int32, (heads, window), 1)
    position = length - 1 - lax.rem(length - 1 - slot + window, window)
    usable = (position >= 0) & (position > length - window)
    dec_query = dec_query_ref[0]
    dec_latent = dec_latent_ref[...]
    cache = cache_ref[0]
    cache_scores = (
        jnp.dot(dec_query, cache, preferred_element_type=jnp.float32) * scale_qk
    )
    own = (
        jnp.sum(
            dec_query.astype(jnp.float32) * dec_latent.astype(jnp.float32), axis=1, keepdims=True
        )
        * scale_qk
    )
    cache_masked = jnp.where(usable, cache_scores, NEG_FILL)
    dec_top = jnp.maximum(
        jnp.maximum(jnp.max(cache_masked, axis=1, keepdims=True), own), sinks
    )
    cache_exp = jnp.where(usable, jnp.exp(cache_masked - dec_top), 0.0)
    own_exp = jnp.exp(own - dec_top)
    dec_numer = lax.dot_general(
        cache_exp.astype(jnp.bfloat16),
        cache[:LATENT, :],
        ROWS_CONTRACT,
        preferred_element_type=jnp.float32,
    )
    dec_numer = dec_numer + own_exp.astype(jnp.bfloat16).astype(jnp.float32) * dec_latent[
        :, :LATENT
    ].astype(jnp.float32)
    dec_total = jnp.sum(cache_exp, axis=1, keepdims=True) + own_exp + jnp.exp(sinks - dec_top)
    dec_attended = dec_numer / dec_total
    blocks = out_ref.shape[0]
    fold_ref[...] = jnp.zeros_like(fold_ref)
    for part in range(parts):
        dec_ref[part] = dec_attended[:, part * LANES : (part + 1) * LANES]
        for head in range(per_block):
            fold_ref[pl.ds(head * parts + part, blocks, stride=TILE), :] = dec_ref[
                part, pl.ds(head, blocks, stride=per_block), :
            ]
    out_ref[:, :, per_block * LATENT :] = (
        fold_ref[...].astype(jnp.bfloat16).reshape(blocks, TILE, LANES)
    )


def project_kernel(place_ref, att_ref, *rest):
    piece_refs, outs = rest[:-7], rest[-7:]
    kept_ref, sent_ref, router_ref, routes_ref, rows_ref, fold_ref, uv_ref = outs
    group, outer = place_ref[1], place_ref[0] // place_ref[2]
    pieces = [(ref, i) for ref in piece_refs for i in range(ref.shape[0])]
    for step, (ref, i) in enumerate(pieces):
        router_ref[step] = ref[i, :, -2 * LANES : -LANES]
        routes_ref[step] = ref[i, :, -LANES:]
    me = place_ref[0]
    blocks, span, width = att_ref.shape
    width -= LANES
    members = len(pieces)
    heads = width // LATENT
    latent_rows = LATENT // members
    tiles = latent_rows // TILE
    value_rows = TILE // heads
    rows_ref[: blocks * span, :] = att_ref[:, :, :width].reshape(blocks * span, width)
    fold_ref[...] = att_ref[:, :, width:].reshape(blocks * TILE, LANES).astype(jnp.float32)
    dec_rows = jnp.concatenate(
        [fold_ref[pl.ds(i, blocks, stride=TILE), :] for i in range(width // LANES)], axis=1
    )
    dec_rows = jnp.concatenate([dec_rows, jnp.zeros((TILE - blocks, width), jnp.float32)], axis=0)
    rows_ref[blocks * span :, :] = dec_rows.astype(jnp.bfloat16)
    for step in range(members):
        holder = me ^ chain_offset(step, members)
        for head in range(heads):
            for tile in range(tiles):
                at = D + (head * tiles + tile) * LANES
                start = pl.multiple_of(head * LATENT + holder * latent_rows + tile * TILE, TILE)
                ref, i = pieces[step]
                uv_ref[pl.ds(start, TILE), :] = ref[i, :, at : at + LANES]
    value = lax.broadcasted_iota(jnp.int32, (LANES, members * TILE), 0)
    column = lax.broadcasted_iota(jnp.int32, (LANES, members * TILE), 1)
    step = column // TILE
    holder = chain_offset(step, members) ^ me
    wanted = holder * value_rows + column % value_rows
    column_head = (column % TILE) // value_rows
    spread = []
    for head in range(heads):
        order = jnp.where((value == wanted) & (column_head == head), 1.0, 0.0).astype(jnp.bfloat16)
        spread.append(
            jnp.dot(
                uv_ref[head * LATENT : (head + 1) * LATENT, :],
                order,
                preferred_element_type=jnp.float32,
            ).astype(jnp.bfloat16)
        )
    head_values = jnp.dot(
        rows_ref[...], jnp.concatenate(spread, axis=0), preferred_element_type=jnp.float32
    ).astype(jnp.bfloat16)
    out_rows = jnp.concatenate([ref[i, :, :D] for ref, i in pieces], axis=0)
    partial_rows = jnp.dot(head_values, out_rows, preferred_element_type=jnp.float32)
    split = blocks * span
    for part in range(TILE):
        fold_ref[pl.ds(part, blocks, stride=TILE), :] = partial_rows[
            split : split + blocks, part * LANES : (part + 1) * LANES
        ]
    for block in range(blocks):
        rows = slice(block * TILE, (block + 1) * TILE)
        step = (block % OUTER) ^ outer

        def store(ref):
            ref[step, :, :D] = partial_rows[rows].astype(jnp.bfloat16)
            ref[step, :, D:] = fold_ref[rows].astype(jnp.bfloat16)

        pl.when(group == block // OUTER)(partial(store, kept_ref))
        pl.when(group != block // OUTER)(partial(store, sent_ref))


def pair_kernel(kept_ref, other_ref, *out_refs):
    for step, out_ref in enumerate(out_refs):
        out_ref[...] = (
            kept_ref[step].astype(jnp.float32) + other_ref[step].astype(jnp.float32)
        ).astype(jnp.bfloat16)


def chain_offset(step, members):
    inner = members // OUTER
    offset = (step % OUTER) * inner
    rest = step // OUTER
    bit = inner // 2
    while bit:
        offset = offset + (rest % 2) * bit
        rest = rest // 2
        bit //= 2
    return offset


def route_kernel(
    place_ref, plane_ref, other_ref, select_ref, scatter_ref, chosen_ref
):
    me, group = place_ref[0], place_ref[1]
    members = plane_ref.shape[0]
    homes = 2 * members
    total = chosen_ref.shape[0]
    pre_total = homes * TILE
    slots = select_ref.shape[0]

    def home_of(token):
        return jnp.where(token < pre_total, token // TILE, token - pre_total)

    def row_of(token):
        return jnp.where(token < pre_total, token % TILE, TILE)

    def place_of(token):
        place = home_place(home_of(token), me, group, members)
        return jnp.where(token < pre_total, place * TILE + token % TILE, pre_total + place)

    def iota(shape, axis):
        return lax.broadcasted_iota(jnp.int32, shape, axis)

    token = iota((total, homes), 0)
    home = home_of(token)
    held = ((home // (members // 2)) % 2) * members + (home // members) * (members // 2) + home % (
        members // 2
    )
    pick = jnp.where(held == iota((total, homes), 1), 1.0, 0.0).astype(jnp.bfloat16)
    own_row = iota((total, LANES), 1) == row_of(iota((total, LANES), 0))
    lane = iota((total, LANES), 1)
    lane_expert = jnp.where(
        lane >= LANES - members,
        chain_offset(lane - jnp.where(lane >= LANES - members, LANES - members, 0), members) ^ me,
        -1,
    ).astype(jnp.float32)
    chosen = jnp.zeros((total, LANES), jnp.float32)
    mine = jnp.zeros((total, LANES), jnp.float32)
    for k in range(TOPK):
        table = jnp.concatenate([plane_ref[:, k, :], other_ref[:, k, :]], axis=0)
        spread = jnp.dot(pick, table, preferred_element_type=jnp.float32)
        expert = jnp.sum(jnp.where(own_row, spread, 0.0), axis=1, keepdims=True)
        chosen = chosen + jnp.where(expert == lane_expert, 1.0, 0.0)
        mine = mine + jnp.where(own_row & (spread == me.astype(jnp.float32)), 1.0, 0.0)
    chosen_ref[...] = chosen.astype(jnp.bfloat16)
    mine_row = lax.dot_general(
        jnp.ones((8, LANES), jnp.bfloat16),
        mine.astype(jnp.bfloat16),
        ROWS_CONTRACT,
        preferred_element_type=jnp.float32,
    )
    square = (total, total)
    place_row = place_of(iota((8, total), 1))[:1]
    place_column = place_of(iota((total, LANES), 0))[:, :1]
    earlier = jnp.where(place_column <= place_row, 1.0, 0.0).astype(jnp.bfloat16)
    rank_row = jnp.dot(
        mine_row.astype(jnp.bfloat16), earlier, preferred_element_type=jnp.float32
    )[:1]
    slot = (iota((slots, total), 0) + 1).astype(jnp.float32)
    select = jnp.where((slot == rank_row) & (mine_row[:1] > 0.0), 1.0, 0.0).astype(jnp.bfloat16)
    same = jnp.where(iota(square, 0) == iota(square, 1), 1.0, 0.0).astype(jnp.bfloat16)
    select_ref[...] = select
    scatter_ref[...] = lax.dot_general(
        same, select, ROWS_CONTRACT, preferred_element_type=jnp.float32
    ).astype(jnp.bfloat16)


def home_place(index, me, group, members):
    half = members // 2
    last, home_group = index // members, (index // half) % 2
    member = chain_offset(index % half + last * half, members) ^ me
    return last * members + (home_group ^ group) * half + member // 2


def norm_kernel(resid_ref, gain_ref, *rest):
    partial_refs, (hidden_ref, normed_ref) = rest[:-2], rest[-2:]
    summed = partial_refs[0][...].astype(jnp.float32)
    for ref in partial_refs[1:]:
        summed = summed + ref[...].astype(jnp.float32)
    hidden = (resid_ref[...].astype(jnp.float32) + summed).astype(jnp.bfloat16)
    hidden_ref[...] = hidden
    hidden = hidden.astype(jnp.float32)
    gain = gain_ref[...].astype(jnp.float32)
    pre, dec = hidden[:, :D], hidden[:, D:]
    pre_mean = jnp.sum(pre * pre, axis=1, keepdims=True) / D
    dec_mean = jnp.sum(jnp.sum(dec * dec, axis=1, keepdims=True), axis=0, keepdims=True) / D
    normed_ref[:, :D] = (pre * lax.rsqrt(pre_mean + NORM_EPS) * gain[:1, :D]).astype(jnp.bfloat16)
    normed_ref[:, D:] = (dec * lax.rsqrt(dec_mean + NORM_EPS) * gain[:, D:]).astype(jnp.bfloat16)


def expert_kernel(select_ref, gate_ref, up_ref, *rest):
    piece_refs, (act_ref, pre_ref, dec_ref, fold_ref) = rest[:-4], rest[-4:]
    pre_total = pre_ref.shape[0]
    homes = pre_total // TILE
    row = 0
    for ref in piece_refs:
        count = ref.shape[0]
        pre_ref[row : row + count, :] = ref[:, :D]
        fold_ref[row : row + count, :] = ref[:, D:].astype(jnp.float32)
        row += count
    for part in range(TILE):
        dec_ref[:, part * LANES : (part + 1) * LANES] = fold_ref[
            pl.ds(part, homes, stride=TILE), :
        ].astype(jnp.bfloat16)
    select = select_ref[...]
    rows = (
        jnp.dot(select[:, :pre_total], pre_ref[...], preferred_element_type=jnp.float32)
        + jnp.dot(select[:, pre_total:], dec_ref[...], preferred_element_type=jnp.float32)
    ).astype(jnp.bfloat16)
    gate = lax.dot_general(rows, gate_ref[0], ROWS_CONTRACT, preferred_element_type=jnp.float32)
    up = lax.dot_general(rows, up_ref[0], ROWS_CONTRACT, preferred_element_type=jnp.float32)
    act_ref[...] = (gate / (1.0 + jnp.exp(-gate)) * up).astype(jnp.bfloat16)


def shared_kernel(
    units, members, small_ref, select_ref, chosen_ref, pre_ref, dec_ref, shared_ref, weight_ref
):
    pre_total = pre_ref.shape[0]
    homes = pre_total // TILE
    small = small_ref[...]
    first = jnp.concatenate(
        [
            lax.dot_general(
                ref[...], small, ROWS_CONTRACT, preferred_element_type=jnp.float32
            )
            for ref in (pre_ref, dec_ref)
        ],
        axis=0,
    )
    half = LANES // 2
    gate_part = first[:, :units]
    up_part = first[:, half : half + units]
    shared_act = (gate_part / (1.0 + jnp.exp(-gate_part)) * up_part).astype(jnp.bfloat16)
    shared_ref[...] = jnp.zeros_like(shared_ref)
    split = pre_total // 2
    middle = pre_total + homes // 2
    shared_ref[:split, :units] = shared_act[:split]
    shared_ref[:split, half : half + units] = shared_act[split:pre_total]
    shared_ref[split:, :units] = shared_act[pre_total:middle]
    shared_ref[split:, half : half + units] = shared_act[middle:]
    logits = first[:, LANES - members :]
    scores = 1.0 / (1.0 + jnp.exp(-logits))
    token_weight = (
        ROUTE_SCALE
        * scores[:, :1]
        / jnp.sum(scores * chosen_ref[:, LANES - members :], axis=1, keepdims=True)
    )
    high = token_weight.astype(jnp.bfloat16)
    rest = token_weight - high.astype(jnp.float32)
    middle = rest.astype(jnp.bfloat16)
    rest = (rest - middle.astype(jnp.float32)).astype(jnp.bfloat16)
    weights = jnp.dot(
        select_ref[...],
        jnp.concatenate([high, middle, rest], axis=1),
        preferred_element_type=jnp.float32,
    )
    weight_ref[...] = jnp.broadcast_to(jnp.sum(weights, axis=1, keepdims=True), weight_ref.shape)


def down_kernel(
    place_ref, act_ref, act_other_ref, shared_ref, shared_other_ref,
    down_ref, down_a_ref, down_b_ref, scatter_ref, weight_ref, kept_ref, sent_ref, fold_ref,
):
    me, group = place_ref[0], place_ref[1]
    columns = down_ref.shape[2]
    units = down_a_ref.shape[0]
    width = down_ref.shape[1] // 2
    own = down_ref[0, pl.ds(pl.multiple_of(group * width, TILE), width), :]
    other = down_ref[0, pl.ds(pl.multiple_of((1 - group) * width, TILE), width), :]
    routed = jnp.dot(act_ref[...], own, preferred_element_type=jnp.float32) + jnp.dot(
        act_other_ref[...], other, preferred_element_type=jnp.float32
    )
    routed = (routed * weight_ref[:, :1]).astype(jnp.bfloat16)
    mine_first = lax.rem(me, 2) == group
    own_down = jnp.where(mine_first, down_a_ref[...], down_b_ref[...])
    other_down = jnp.where(mine_first, down_b_ref[...], down_a_ref[...])
    both_down = jnp.concatenate([own_down, other_down], axis=0)
    half = kept_ref.shape[0]
    homes = 2 * half
    split = homes * TILE
    other = shared_other_ref[...]
    middle, decs = split // 4, other[split // 2 :].astype(jnp.float32)
    eighth = homes // 4
    other = jnp.concatenate(
        [
            other[middle : 2 * middle],
            other[:middle],
            jnp.concatenate([decs[eighth:], decs[:eighth]], axis=0).astype(jnp.bfloat16),
        ],
        axis=0,
    )
    shared = shared_ref[...]

    def down(at):
        acts = jnp.concatenate([shared[:, at : at + units], other[:, at : at + units]], axis=1)
        return jnp.dot(acts, both_down, preferred_element_type=jnp.float32)

    low_half, high_half = down(0), down(LANES // 2)
    total = jnp.dot(scatter_ref[...], routed, preferred_element_type=jnp.float32) + jnp.concatenate(
        [
            low_half[: split // 2], high_half[: split // 2], low_half[split // 2 :],
            high_half[split // 2 :],
        ],
        axis=0,
    )
    fold_ref[...] = jnp.zeros_like(fold_ref)
    for part in range(columns // LANES):
        fold_ref[pl.ds(part, homes, stride=TILE), :] = total[
            split:, part * LANES : (part + 1) * LANES
        ]
    for home in range(homes):
        place = home_place(home, me, group, half)
        ref = kept_ref if home < half else sent_ref
        at = place if home < half else place - half
        rows = slice(home * TILE, (home + 1) * TILE)
        ref[at, :, :columns] = total[rows].astype(jnp.bfloat16)
        ref[at, :, columns:] = fold_ref[rows].astype(jnp.bfloat16)


def finish_kernel(got_ref, hidden_ref, pre_ref, dec_ref):
    sources, _, width = got_ref.shape
    columns = width - LANES
    groups = D // columns
    each = sources // groups
    for group in range(groups):
        summed = got_ref[group * each].astype(jnp.float32)
        for i in range(1, each):
            summed = summed + got_ref[group * each + i].astype(jnp.float32)
        at = group * columns
        pre_ref[:, at : at + columns] = (
            hidden_ref[:, at : at + columns].astype(jnp.float32) + summed[:, :columns]
        ).astype(jnp.bfloat16)
        parts = columns // LANES
        for part in range(parts):
            row = group * parts + part
            dec_ref[:, row * LANES : (row + 1) * LANES] = (
                hidden_ref[row : row + 1, D:].astype(jnp.float32)
                + summed[part : part + 1, columns:]
            ).astype(jnp.bfloat16)


def token_shards(
    pre_query,
    pre_latent,
    pre_resid,
    dec_query,
    dec_latent,
    dec_resid,
    cache_lengths,
    latent_cache,
    sink_logits,
    uv_weight,
    out_weight,
    norm_gain,
    router,
    routes,
    gate_weight,
    up_weight,
    down_weight,
    shared_gate,
    shared_up,
    shared_down,
):
    groups = lax.axis_size("dp")
    members = lax.axis_size("expert")
    inner = members // OUTER
    homes = groups * members
    me = lax.axis_index("expert")
    my_group = lax.axis_index("dp")
    place_ids = jnp.stack([me, my_group, jnp.int32(inner)]).astype(jnp.int32)
    pre_rows = pre_query.shape[0]
    rows_dev = pre_rows + 1
    capacity = max(2, (rows_dev * TOPK + members - 1) // members)

    heads_dev, latent_rows, value_dim = uv_weight.shape
    heads_outer = heads_dev // OUTER
    uv_tiles = heads_outer * latent_rows // TILE
    block_width = D + uv_tiles * value_dim + 2 * LANES
    blocks = call(
        pack_kernel,
        [low((1, TILE, block_width))] * OUTER,
        [place_ids, out_weight, uv_weight, router.T, routes.T],
        scratch=[pltpu.VMEM((TILE, 2 * LANES), jnp.float32)],
        scalars=1,
        moved=(1, 2, 3, 4),
        flops=10_000_000_000,
    )
    pair_bit = inner // 2
    near = line_swaps(blocks, inner)
    own_pair = swap(blocks[0], "expert", pair_bit)
    line = jnp.concatenate(near, axis=0)
    far_in, own_pair = lax.optimization_barrier((line[1:], own_pair))

    pre_query, blocks = lax.optimization_barrier((pre_query, blocks))
    peers = groups * OUTER
    heads_block = heads_outer * LATENT
    att_blocks = call(
        attend_kernel,
        low((peers, pre_rows, heads_block + LANES)),
        [
            cache_lengths, pre_query, pre_latent, dec_query, dec_latent,
            latent_cache.swapaxes(1, 2),
            sink_logits.reshape(1, -1),
        ],
        scratch=[
            pltpu.VMEM((LATENT // LANES, pre_rows * pre_query.shape[1], LANES), jnp.float32),
            pltpu.VMEM((LATENT // LANES, pre_query.shape[1], LANES), jnp.float32),
            pltpu.VMEM((peers * TILE, LANES), jnp.float32),
        ],
        scalars=1,
        flops=100_000_000,
    )
    lines = [
        [g * members + o * inner + i for g in range(groups) for o in range(OUTER)]
        for i in range(inner)
    ]
    both = ("dp", "expert")
    far_pair = swap(far_in, "expert", pair_bit)
    att_got = lax.all_to_all(
        att_blocks, both, split_axis=0, concat_axis=0, axis_index_groups=lines, tiled=True
    )
    units = shared_gate.shape[1] // members
    padded = -(-units // TILE) * TILE
    depth = shared_gate.shape[0]
    line, line_gate = lax.optimization_barrier((line, shared_gate))
    *spread, down_a, down_b = call(
        partial(spread_kernel, units),
        [low((inner, 2 * padded, depth))] * OUTER + [low((units, shared_down.shape[1]))] * 2,
        [place_ids, line_gate.T, shared_up.T, shared_down],
        scalars=1,
    )
    far_pair, *spread = lax.optimization_barrier((far_pair, *spread))
    pieces = [line, own_pair, far_pair]
    pieces = pieces + [swap(piece, "expert", 1) for piece in pieces]
    kept_sums, sent_sums, router_blocks, routes_plane = call(
        project_kernel,
        [low((OUTER, pre_rows, D + LANES))] * 2 + [low((members, TILE, LANES))] * 2,
        [place_ids, att_got, *pieces],
        scratch=[
            pltpu.VMEM((peers * pre_rows + TILE, heads_block), jnp.bfloat16),
            pltpu.VMEM((peers * TILE, LANES), jnp.float32),
            pltpu.VMEM((heads_block, value_dim), jnp.bfloat16),
        ],
        scalars=1,
        flops=300_000_000,
        moved=tuple(range(2, 2 + len(pieces))),
    )
    other_sums = swap(sent_sums, "dp", 1)
    routes_other = swap(routes_plane, "dp", 1)

    _, *spread = lax.optimization_barrier((kept_sums, *spread))
    shared_got = line_swaps(spread, inner)
    pre_total = homes * pre_rows
    total = pre_total + homes
    slots = homes * capacity
    select, scatter, chosen = call(
        route_kernel,
        [low((slots, total)), low((total, slots)), low((total, LANES))],
        [place_ids, routes_plane, routes_other],
        scalars=1,
        vmem=16,
    )
    resid = jnp.concatenate([pre_resid, fold_row(dec_resid)], axis=1)
    gain = jnp.concatenate(
        [jnp.broadcast_to(norm_gain[None], (TILE, D)), norm_gain.reshape(TILE, LANES)], axis=1
    )
    other_sums, select, scatter, chosen = lax.optimization_barrier(
        (other_sums, select, scatter, chosen)
    )
    sums = call(pair_kernel, [low(resid.shape)] * OUTER, [kept_sums, other_sums], flops=1_000_000)
    sums_got = line_swaps(sums, inner)
    _, *shared_got = lax.optimization_barrier((sums[0], *shared_got))
    kept = jnp.concatenate([block[:pair_bit] for block in shared_got], axis=0)
    sent = jnp.concatenate([block[pair_bit:] for block in shared_got], axis=0)
    far = swap(sent, "expert", pair_bit)
    shared_kept = jnp.concatenate([kept[::pair_bit], far[::pair_bit]], axis=0)
    shared_sent = jnp.concatenate([kept[1::pair_bit], far[1::pair_bit]], axis=0)
    shared_far = swap(shared_sent, "expert", 1)
    small = call(
        small_kernel,
        low((LANES, D)),
        [place_ids, shared_kept, shared_far, router_blocks],
        scratch=[pltpu.VMEM((members * TILE, LANES), jnp.float32)],
        scalars=1,
    )
    middle = OUTER // 2
    hidden, normed = call(
        norm_kernel, [low(resid.shape)] * 2, [resid, gain, *sums_got], flops=20_000_000_000
    )

    line = line_swaps([normed] * OUTER, inner)
    middle = OUTER // 2
    row_pieces = []
    for part in (line[:middle], line[middle:]):
        row_pieces.append(jnp.concatenate(part, axis=0))
    piece_a, piece_b = row_pieces
    a_pair, b_group = swap(piece_a, "expert", pair_bit), swap(piece_b, "dp", 1)
    a_group, b_pair = swap(piece_a, "dp", 1), swap(piece_b, "expert", pair_bit)
    a_both, b_both = swap(a_pair, "dp", 1), swap(b_group, "expert", pair_bit)
    row_pieces = [piece_a, piece_b, a_pair, b_pair, a_group, b_group, a_both, b_both]
    row_pieces = row_pieces + [swap(piece, "expert", 1) for piece in row_pieces]

    width = gate_weight.shape[2]
    gate_rows, up_rows = gate_weight.swapaxes(1, 2), up_weight.swapaxes(1, 2)
    expert_act, pre_tokens, dec_tokens = call(
        expert_kernel,
        [low((slots, width)), low((pre_total, D)), low((homes, D))],
        [select, gate_rows, up_rows, *row_pieces],
        scratch=[pltpu.VMEM((pre_total, LANES), jnp.float32)],
        flops=2_000_000_000,
        vmem=20,
    )
    expert_act_other = swap(expert_act, "dp", 1)
    shared_act, slot_weight = call(
        partial(shared_kernel, units, members),
        [low((total // 2, LANES)), jax.ShapeDtypeStruct((slots, LANES), jnp.float32)],
        [small, select, chosen, pre_tokens, dec_tokens],
        flops=500_000_000,
        vmem=12,
    )
    shared_act_other = swap(shared_act, "dp", 1)
    shared_act, down_a, down_b = lax.optimization_barrier((shared_act, down_a, down_b))
    half = members // 2
    down_a = lax.ppermute(
        down_a,
        "expert",
        [(i, 2 * i if i < half else 2 * (i - half) + 1) for i in range(members)],
    )
    down_b = lax.ppermute(
        down_b,
        "expert",
        [(i, 2 * i + 1 if i < half else 2 * (i - half)) for i in range(members)],
    )
    col_width = down_weight.shape[2]
    kept, sent = call(
        down_kernel,
        [low((homes // 2, TILE, col_width + LANES))] * 2,
        [
            place_ids, expert_act, expert_act_other, shared_act, shared_act_other,
            down_weight, down_a, down_b, scatter, slot_weight,
        ],
        scratch=[pltpu.VMEM((pre_total, LANES), jnp.float32)],
        scalars=1,
        flops=1_000_000_000,
        vmem=20,
    )
    pair_sum = (kept.astype(jnp.float32) + swap(sent, "expert", 1).astype(jnp.float32)).astype(
        jnp.bfloat16
    )
    halves = [
        [g * members + 2 * i + b for g in range(groups) for i in range(members // 2)]
        for b in range(2)
    ]
    home_got = lax.all_to_all(
        pair_sum, both, split_axis=0, concat_axis=0, axis_index_groups=halves, tiled=True
    )
    return tuple(
        call(finish_kernel, [low(pre_resid.shape), low(dec_resid.shape)], [home_got, hidden])
    )


def fits(mesh, heads, ff):
    groups, members = mesh.shape["dp"], mesh.shape["expert"]
    return (
        groups == 2
        and members % (2 * OUTER) == 0
        and (heads // groups) % OUTER == 0
        and ff % (groups * members) == 0
    )


def solution(mesh):
    in_specs = (
        P(("dp", "expert"), None, None),
        P(("dp", "expert"), None),
        P(("dp", "expert"), None),
        P(("dp", "expert"), None, None),
        P(("dp", "expert"), None),
        P(("dp", "expert"), None),
        P(("dp", "expert")),
        P(("dp", "expert"), None, None),
        P(),
        P("dp", "expert", None),
        P("dp", "expert", None),
        P(),
        P(None, "expert"),
        P(("dp", "expert"), None),
        P("expert", None, "dp"),
        P("expert", None, "dp"),
        P("expert", None, "dp"),
        P("expert", "dp"),
        P("expert", "dp"),
        P("expert", "dp"),
    )
    out_specs = (P(("dp", "expert"), None), P(("dp", "expert"), None))

    def layer(*args):
        plan = token_shards if fits(mesh, args[9].shape[0], args[17].shape[1]) else shards
        return jax.shard_map(
            plan, mesh=mesh, in_specs=in_specs, out_specs=out_specs, check_vma=False
        )(*args)

    return layer
```

```python
from functools import partial

import jax
import jax.numpy as jnp
from jax import lax
from jax.experimental import pallas as pl
from jax.experimental.pallas import tpu as pltpu
from jax.sharding import PartitionSpec as P

D = 2048
LATENT = 512
ROPE = 64
QK_NOPE = 128
TOPK = 6


ROUTE_SCALE = 2.446
NORM_EPS = 1e-06
NEG_FILL = -1e30


def assign_slots(route_rows, experts):
    flat_routes = route_rows.reshape(-1)
    one_hot = (flat_routes[:, None] == jnp.arange(experts, dtype=jnp.int32)[None, :]).astype(
        jnp.int32
    )
    running = jnp.cumsum(one_hot, axis=0)
    slot_rank = jnp.sum(running * one_hot, axis=1) - 1
    return slot_rank.reshape(route_rows.shape)


def dispatch_matrix(route_rows, slot_rows, experts, capacity):
    target = route_rows * capacity + slot_rows
    places = jnp.arange(experts * capacity, dtype=jnp.int32)
    total = jnp.zeros((route_rows.shape[0], experts * capacity), jnp.bfloat16)
    for column in range(route_rows.shape[1]):
        total = total + (target[:, column][:, None] == places[None, :]).astype(jnp.bfloat16)
    return total


def shards(
    pre_query,
    pre_latent,
    pre_resid,
    dec_query,
    dec_latent,
    dec_resid,
    cache_lengths,
    latent_cache,
    sink_logits,
    uv_weight,
    out_weight,
    norm_gain,
    router,
    routes,
    gate_weight,
    up_weight,
    down_weight,
    shared_gate,
    shared_up,
    shared_down,
):
    groups = lax.axis_size("dp")
    members = lax.axis_size("expert")
    pre_rows = pre_query.shape[0]
    rows_dev = pre_rows + 1
    scale_qk = (QK_NOPE + ROPE) ** (-0.5)
    pre_scores = (
        jnp.einsum("thc,uc->thu", pre_query, pre_latent, preferred_element_type=jnp.float32)
        * scale_qk
    )
    places = jnp.arange(pre_rows, dtype=jnp.int32)
    allowed = (places[None, :] <= places[:, None])[:, None, :]
    masked = jnp.where(allowed, pre_scores, NEG_FILL)
    pre_max = jnp.maximum(jnp.max(masked, axis=2), sink_logits[None, :])
    exp_terms = jnp.where(allowed, jnp.exp(masked - pre_max[:, :, None]), 0.0)
    denominator = jnp.sum(exp_terms, axis=2) + jnp.exp(sink_logits[None, :] - pre_max)
    numerator = jnp.einsum(
        "thu,ul->thl",
        exp_terms.astype(jnp.bfloat16),
        pre_latent[:, :LATENT],
        preferred_element_type=jnp.float32,
    )
    pre_att = (numerator / denominator[:, :, None]).astype(jnp.bfloat16)
    window = latent_cache.shape[1]
    slot_ids = jnp.arange(window, dtype=jnp.int32)
    newest = cache_lengths - 1
    position = newest[:, None] - jnp.mod(newest[:, None] - slot_ids[None, :], window)
    usable = ((position >= 0) & (position > cache_lengths[:, None] - window))[:, None, :]
    cache_scores = (
        jnp.einsum("rhc,rsc->rhs", dec_query, latent_cache, preferred_element_type=jnp.float32)
        * scale_qk
    )
    own_scores = (
        jnp.einsum("rhc,rc->rh", dec_query, dec_latent, preferred_element_type=jnp.float32)
        * scale_qk
    )
    cache_masked = jnp.where(usable, cache_scores, NEG_FILL)
    top_score = jnp.maximum(
        jnp.maximum(jnp.max(cache_masked, axis=2), own_scores), sink_logits[None, :]
    )
    cache_exp = jnp.where(usable, jnp.exp(cache_masked - top_score[:, :, None]), 0.0)
    own_exp = jnp.exp(own_scores - top_score)
    dec_numer = jnp.einsum(
        "rhs,rsl->rhl",
        cache_exp.astype(jnp.bfloat16),
        latent_cache[:, :, :LATENT],
        preferred_element_type=jnp.float32,
    )
    dec_numer = dec_numer + own_exp.astype(jnp.bfloat16).astype(jnp.float32)[
        :, :, None
    ] * dec_latent[:, None, :LATENT].astype(jnp.float32)
    dec_total = jnp.sum(cache_exp, axis=2) + own_exp + jnp.exp(sink_logits[None, :] - top_score)
    dec_att = (dec_numer / dec_total[:, :, None]).astype(jnp.bfloat16)
    attention = jnp.concatenate([pre_att, dec_att], axis=0)
    spread = lax.all_to_all(attention, "dp", split_axis=1, concat_axis=0, tiled=True)
    uv_full, out_full = (
        lax.all_gather(uv_weight, "expert", axis=1, tiled=True),
        lax.all_gather(out_weight, "expert", axis=1, tiled=True),
    )
    head_values = jnp.einsum(
        "thl,hlv->thv", spread, uv_full, preferred_element_type=jnp.float32
    ).astype(jnp.bfloat16)
    head_partial = jnp.einsum(
        "thv,hvd->td", head_values, out_full, preferred_element_type=jnp.float32
    )
    attn_out = lax.psum_scatter(
        head_partial.astype(jnp.bfloat16), "dp", scatter_dimension=0, tiled=True
    ).astype(jnp.float32)
    resid = jnp.concatenate([pre_resid, dec_resid], axis=0)
    hidden = (resid.astype(jnp.float32) + attn_out).astype(jnp.bfloat16)
    hidden_up = lax.optimization_barrier(hidden).astype(jnp.float32)
    mean_square = jnp.mean(hidden_up * hidden_up, axis=1, keepdims=True)
    normed = (
        hidden_up * lax.rsqrt(mean_square + NORM_EPS) * norm_gain.astype(jnp.float32)[None, :]
    ).astype(jnp.bfloat16)
    capacity = max(2, (rows_dev * TOPK + members - 1) // members)
    group_tokens = lax.all_gather(normed, "dp", axis=0, tiled=True)
    group_routes = lax.all_gather(routes, "dp", axis=0, tiled=True)
    routes_by_group = group_routes.reshape(groups, rows_dev, TOPK)
    slots_by_group = jax.vmap(partial(assign_slots, experts=members))(routes_by_group)
    tokens_by_group = group_tokens.reshape(groups, rows_dev, D)
    all_matrix = jax.vmap(partial(dispatch_matrix, experts=members, capacity=capacity))(
        routes_by_group, slots_by_group
    )
    all_matrix = all_matrix.reshape(groups, rows_dev, members, capacity)
    outgoing = jnp.einsum(
        "grxc,grd->xgcd", all_matrix, tokens_by_group, preferred_element_type=jnp.bfloat16
    )
    expert_rows = lax.all_to_all(outgoing, "expert", split_axis=0, concat_axis=0, tiled=True)
    expert_rows = expert_rows.reshape(-1, D)
    gate_score = jax.nn.sigmoid(
        jnp.dot(expert_rows, router[:, 0], preferred_element_type=jnp.float32)
    )
    gate_proj = jnp.dot(expert_rows, gate_weight[0], preferred_element_type=jnp.float32)
    up_proj = jnp.dot(expert_rows, up_weight[0], preferred_element_type=jnp.float32)
    expert_act = (jax.nn.silu(gate_proj) * up_proj).astype(jnp.bfloat16)
    shared_gate_full, shared_up_full, shared_down_full = (
        lax.all_gather(shared_gate, "expert", axis=0, tiled=True),
        lax.all_gather(shared_up, "expert", axis=0, tiled=True),
        lax.all_gather(shared_down, "expert", axis=0, tiled=True),
    )
    shared_act = (
        jax.nn.silu(jnp.dot(group_tokens, shared_gate_full, preferred_element_type=jnp.float32))
        * jnp.dot(group_tokens, shared_up_full, preferred_element_type=jnp.float32)
    ).astype(jnp.bfloat16)
    down_local = down_weight[0]
    col_width = down_local.shape[1]
    routed_piece = lax.all_gather(expert_act, "dp", axis=1, tiled=True)
    shared_piece = lax.all_gather(shared_act, "dp", axis=1, tiled=True)
    routed_cols = jnp.dot(routed_piece, down_local, preferred_element_type=jnp.float32)
    shared_cols = jnp.dot(shared_piece, shared_down_full, preferred_element_type=jnp.float32)
    expert_out = routed_cols.astype(jnp.bfloat16)
    shared_out = shared_cols.astype(jnp.bfloat16)
    returned = lax.all_to_all(
        expert_out.reshape(members, groups * capacity, col_width),
        "expert",
        split_axis=0,
        concat_axis=0,
        tiled=True,
    )
    returned_scores = lax.all_to_all(
        gate_score.reshape(members, groups * capacity),
        "expert",
        split_axis=0,
        concat_axis=0,
        tiled=True,
    )
    group_offset = (jnp.arange(groups, dtype=jnp.int32) * capacity)[:, None, None]
    lookup = (routes_by_group * (groups * capacity) + group_offset + slots_by_group).reshape(
        groups * rows_dev, TOPK
    )
    picked = jnp.take(returned.reshape(-1, col_width), lookup, axis=0)
    picked_scores = jnp.take(returned_scores.reshape(-1), lookup, axis=0)
    route_weight = ROUTE_SCALE * picked_scores / jnp.sum(picked_scores, axis=1, keepdims=True)
    moe_cols = shared_out.astype(jnp.float32) + jnp.sum(
        route_weight[:, :, None] * picked.astype(jnp.float32), axis=1
    )
    moe_home = lax.all_to_all(
        moe_cols.reshape(groups, rows_dev, col_width).astype(jnp.bfloat16),
        "dp",
        split_axis=0,
        concat_axis=2,
        tiled=True,
    ).astype(jnp.float32)
    final = (hidden_up + moe_home[0]).astype(jnp.bfloat16)
    return (final[:pre_rows], final[pre_rows:])


OUTER = 4
TILE = 16
LANES = 128
ROWS_CONTRACT = (((1,), (1,)), ((), ()))


def fold_row(row):
    return row.reshape(row.shape[:-2] + (TILE, row.shape[-1] // TILE))


def swap(value, axis, bit):
    size = lax.axis_size(axis)
    return lax.ppermute(value, axis, [(i, i ^ bit) for i in range(size)])


def line_swaps(blocks, inner):
    got = {i: swap(blocks[i], "expert", i * inner) for i in reversed(range(1, len(blocks)))}
    return [blocks[0]] + [got[i] for i in range(1, len(blocks))]


def call(kernel, out_shapes, args, scratch=(), scalars=0, flops=0, vmem=10, moved=(), late=(), rows=None):
    specs = []
    for i in range(len(args)):
        if i < scalars:
            specs.append(pl.BlockSpec(memory_space=pltpu.SMEM))
        elif i in moved:
            specs.append(pl.BlockSpec(memory_space=pl.ANY))
        else:
            specs.append(pl.BlockSpec(memory_space=pltpu.VMEM))
    scratch = list(scratch)
    body = kernel
    if moved:
        rows = dict(rows or {})
        shapes = {i: args[i].shape for i in moved}
        for i, (_, count) in rows.items():
            shapes[i] = (shapes[i][0], count) + shapes[i][2:]
        buffers = [pltpu.VMEM(shapes[i], args[i].dtype) for i in moved]
        scratch = scratch + buffers + [pltpu.SemaphoreType.DMA((len(moved),))]

        def body(*refs):
            rest, held, sem = refs[: -len(moved) - 1], refs[-len(moved) - 1 : -1], refs[-1]
            sources = {i: refs[i] for i in moved}
            for i, (start, count) in rows.items():
                sources[i] = refs[i].at[:, pl.ds(start, count)]
            copies = [
                pltpu.make_async_copy(sources[i], held[j], sem.at[j]) for j, i in enumerate(moved)
            ]
            for copy in copies:
                copy.start()
            for i, copy in zip(moved, copies):
                if i not in late:
                    copy.wait()
            inputs = [held[moved.index(i)] if i in moved else refs[i] for i in range(len(args))]
            if late:
                waits = [copies[moved.index(i)].wait for i in late]
                kernel(*inputs, *rest[len(args) :], waits=waits)
            else:
                kernel(*inputs, *rest[len(args) :])

    moved_bytes = sum(a.size * a.dtype.itemsize for a in args)
    single = not isinstance(out_shapes, (list, tuple))
    return pl.pallas_call(
        body,
        out_shape=out_shapes,
        in_specs=specs,
        out_specs=pl.BlockSpec(memory_space=pltpu.VMEM)
        if single
        else [pl.BlockSpec(memory_space=pltpu.VMEM)] * len(out_shapes),
        scratch_shapes=scratch,
        compiler_params=pltpu.CompilerParams(vmem_limit_bytes=vmem * 1024 * 1024),
        cost_estimate=pl.CostEstimate(flops=flops, bytes_accessed=moved_bytes, transcendentals=0),
    )(*args)


def low(shape):
    return jax.ShapeDtypeStruct(shape, jnp.bfloat16)


def pack_kernel(place_ref, out_ref, uv_ref, router_ref, routes_ref, *rest):
    block_refs, (side_ref,) = rest[:OUTER], rest[OUTER:]
    me = place_ref[0]
    outer = me // place_ref[2]
    heads = out_ref.shape[0] // OUTER
    tiles = heads * uv_ref.shape[1] // TILE
    side_ref[...] = jnp.zeros_like(side_ref)
    for part in range(TILE):
        side_ref[part : part + 1, :LANES] = router_ref[
            :, part * LANES : (part + 1) * LANES
        ].astype(jnp.float32)
    choices, rows = routes_ref.shape
    side_ref[:choices, LANES : LANES + rows] = routes_ref[...].astype(jnp.float32)
    side = side_ref[...].astype(jnp.bfloat16)
    for step in range(OUTER):
        target = outer ^ step
        block = block_refs[step]
        block[0, :, :D] = out_ref[pl.ds(target * heads, heads)].reshape(TILE, D)
        uv = uv_ref[pl.ds(target * heads, heads)].reshape(tiles * TILE, LANES)
        for tile in range(tiles):
            at = D + tile * LANES
            block[0, :, at : at + LANES] = uv[tile * TILE : (tile + 1) * TILE]
        block[0, :, D + tiles * LANES :] = side


def spread_kernel(units, place_ref, gate_ref, up_ref, down_ref, *out_refs):
    block_refs, (down_a_ref, down_b_ref) = out_refs[:-2], out_refs[-2:]
    me = place_ref[0]
    lower = me < block_refs[0].shape[0] * OUTER // 2
    first, second = down_ref[:units], down_ref[units:]
    down_a_ref[...] = jnp.where(lower, first, second)
    down_b_ref[...] = jnp.where(lower, second, first)
    inner = block_refs[0].shape[0]
    padded = block_refs[0].shape[1] // 2
    for step in range(OUTER):
        block_refs[step][...] = jnp.zeros_like(block_refs[step])
    for member in range(inner * OUTER):
        offset = member ^ me
        step, near = offset // inner, offset % inner
        rows = slice(member * units, (member + 1) * units)
        for outer in range(OUTER):

            @pl.when(step == outer)
            def _():
                block_refs[outer][near, :units] = gate_ref[rows]
                block_refs[outer][near, padded : padded + units] = up_ref[rows]


def small_kernel(place_ref, kept_ref, far_ref, router_ref, small_ref, fold_ref):
    me = place_ref[0]
    members = kept_ref.shape[0] + far_ref.shape[0]
    small_ref[...] = jnp.zeros_like(small_ref)
    half = LANES // 2
    padded = kept_ref.shape[1] // 2
    for member in range(members):
        ref, i = (kept_ref, member) if member < members // 2 else (far_ref, member - members // 2)
        holder = me ^ chain_offset(member, members)
        lanes = pl.ds(pl.multiple_of(holder * LANES, LANES), LANES)
        small_ref[:padded, lanes] = ref[i, :padded]
        small_ref[half : half + padded, lanes] = ref[i, padded:]
    fold_ref[...] = router_ref[...].reshape(members * TILE, LANES).astype(jnp.float32)
    for part in range(TILE):
        small_ref[LANES - members :, part * LANES : (part + 1) * LANES] = fold_ref[
            pl.ds(part, members, stride=TILE), :
        ].astype(jnp.bfloat16)


def attend_kernel(
    length_ref, query_ref, latent_ref, dec_query_ref, dec_latent_ref, cache_ref, sink_ref,
    out_ref, rows_ref, dec_ref, fold_ref,
):
    span, heads, _ = query_ref.shape
    scale_qk = (QK_NOPE + ROPE) ** (-0.5)
    square = (heads, heads)
    diagonal = lax.broadcasted_iota(jnp.int32, square, 0) == lax.broadcasted_iota(
        jnp.int32, square, 1
    )
    sinks = jnp.sum(
        jnp.where(diagonal, jnp.broadcast_to(sink_ref[...], square), 0.0), axis=1, keepdims=True
    )
    latent = latent_ref[...]
    query = query_ref[...].reshape(span * heads, query_ref.shape[2])
    scores = (
        lax.dot_general(query, latent, ROWS_CONTRACT, preferred_element_type=jnp.float32) * scale_qk
    )
    token = lax.broadcasted_iota(jnp.int32, scores.shape, 0) // heads
    allowed = lax.broadcasted_iota(jnp.int32, scores.shape, 1) <= token
    masked = jnp.where(allowed, scores, NEG_FILL)
    sink_rows = jnp.broadcast_to(sinks[None], (span, heads, 1)).reshape(span * heads, 1)
    top = jnp.maximum(jnp.max(masked, axis=1, keepdims=True), sink_rows)
    terms = jnp.where(allowed, jnp.exp(masked - top), 0.0)
    total = jnp.sum(terms, axis=1, keepdims=True) + jnp.exp(sink_rows - top)
    numer = jnp.dot(
        terms.astype(jnp.bfloat16), latent[:, :LATENT], preferred_element_type=jnp.float32
    )
    attended = numer / total
    per_block = heads // out_ref.shape[0]
    parts = LATENT // LANES
    for part in range(parts):
        rows_ref[part] = attended[:, part * LANES : (part + 1) * LANES]
        for head in range(heads):
            at = (head % per_block) * LATENT + part * LANES
            out_ref[head // per_block, :, at : at + LANES] = rows_ref[
                part, pl.ds(head, span, stride=heads), :
            ].astype(jnp.bfloat16)

    window = cache_ref.shape[2]
    length = length_ref[0]
    slot = lax.broadcasted_iota(jnp.int32, (heads, window), 1)
    position = length - 1 - lax.rem(length - 1 - slot + window, window)
    usable = (position >= 0) & (position > length - window)
    dec_query = dec_query_ref[0]
    dec_latent = dec_latent_ref[...]
    cache = cache_ref[0]
    cache_scores = (
        jnp.dot(dec_query, cache, preferred_element_type=jnp.float32) * scale_qk
    )
    own = (
        jnp.sum(
            dec_query.astype(jnp.float32) * dec_latent.astype(jnp.float32), axis=1, keepdims=True
        )
        * scale_qk
    )
    cache_masked = jnp.where(usable, cache_scores, NEG_FILL)
    dec_top = jnp.maximum(
        jnp.maximum(jnp.max(cache_masked, axis=1, keepdims=True), own), sinks
    )
    cache_exp = jnp.where(usable, jnp.exp(cache_masked - dec_top), 0.0)
    own_exp = jnp.exp(own - dec_top)
    dec_numer = lax.dot_general(
        cache_exp.astype(jnp.bfloat16),
        cache[:LATENT, :],
        ROWS_CONTRACT,
        preferred_element_type=jnp.float32,
    )
    dec_numer = dec_numer + own_exp.astype(jnp.bfloat16).astype(jnp.float32) * dec_latent[
        :, :LATENT
    ].astype(jnp.float32)
    dec_total = jnp.sum(cache_exp, axis=1, keepdims=True) + own_exp + jnp.exp(sinks - dec_top)
    dec_attended = dec_numer / dec_total
    blocks = out_ref.shape[0]
    fold_ref[...] = jnp.zeros_like(fold_ref)
    for part in range(parts):
        dec_ref[part] = dec_attended[:, part * LANES : (part + 1) * LANES]
        for head in range(per_block):
            fold_ref[pl.ds(head * parts + part, blocks, stride=TILE), :] = dec_ref[
                part, pl.ds(head, blocks, stride=per_block), :
            ]
    out_ref[:, :, per_block * LATENT :] = (
        fold_ref[...].astype(jnp.bfloat16).reshape(blocks, TILE, LANES)
    )


def project_kernel(place_ref, att_ref, *rest):
    piece_refs, outs = rest[:-7], rest[-7:]
    kept_ref, sent_ref, router_ref, routes_ref, rows_ref, fold_ref, uv_ref = outs
    group, outer = place_ref[1], place_ref[0] // place_ref[2]
    pieces = [(ref, i) for ref in piece_refs for i in range(ref.shape[0])]
    for step, (ref, i) in enumerate(pieces):
        router_ref[step] = ref[i, :, -2 * LANES : -LANES]
        routes_ref[step] = ref[i, :, -LANES:]
        near, row = step // OUTER, (step // OUTER % 2) * (TILE // 2)
        at = D + LANES + near // 2 * LANES
        sent_ref[step % OUTER, row : row + TILE // 2, at : at + LANES] = ref[
            i, : TILE // 2, -LANES:
        ]
    me = place_ref[0]
    blocks, span, width = att_ref.shape
    width -= LANES
    members = len(pieces)
    heads = width // LATENT
    latent_rows = LATENT // members
    tiles = latent_rows // TILE
    value_rows = TILE // heads
    rows_ref[: blocks * span, :] = att_ref[:, :, :width].reshape(blocks * span, width)
    fold_ref[...] = att_ref[:, :, width:].reshape(blocks * TILE, LANES).astype(jnp.float32)
    dec_rows = jnp.concatenate(
        [fold_ref[pl.ds(i, blocks, stride=TILE), :] for i in range(width // LANES)], axis=1
    )
    dec_rows = jnp.concatenate([dec_rows, jnp.zeros((TILE - blocks, width), jnp.float32)], axis=0)
    rows_ref[blocks * span :, :] = dec_rows.astype(jnp.bfloat16)
    for step in range(members):
        holder = me ^ chain_offset(step, members)
        for head in range(heads):
            for tile in range(tiles):
                at = D + (head * tiles + tile) * LANES
                start = pl.multiple_of(head * LATENT + holder * latent_rows + tile * TILE, TILE)
                ref, i = pieces[step]
                uv_ref[pl.ds(start, TILE), :] = ref[i, :, at : at + LANES]
    value = lax.broadcasted_iota(jnp.int32, (LANES, members * TILE), 0)
    column = lax.broadcasted_iota(jnp.int32, (LANES, members * TILE), 1)
    step = column // TILE
    holder = chain_offset(step, members) ^ me
    wanted = holder * value_rows + column % value_rows
    column_head = (column % TILE) // value_rows
    spread = []
    for head in range(heads):
        order = jnp.where((value == wanted) & (column_head == head), 1.0, 0.0).astype(jnp.bfloat16)
        spread.append(
            jnp.dot(
                uv_ref[head * LATENT : (head + 1) * LATENT, :],
                order,
                preferred_element_type=jnp.float32,
            ).astype(jnp.bfloat16)
        )
    head_values = jnp.dot(
        rows_ref[...], jnp.concatenate(spread, axis=0), preferred_element_type=jnp.float32
    ).astype(jnp.bfloat16)
    out_rows = jnp.concatenate([ref[i, :, :D] for ref, i in pieces], axis=0)
    partial_rows = jnp.dot(head_values, out_rows, preferred_element_type=jnp.float32)
    split = blocks * span
    for part in range(TILE):
        fold_ref[pl.ds(part, blocks, stride=TILE), :] = partial_rows[
            split : split + blocks, part * LANES : (part + 1) * LANES
        ]
    for block in range(blocks):
        rows = slice(block * TILE, (block + 1) * TILE)
        step = (block % OUTER) ^ outer

        def store(ref):
            ref[step, :, :D] = partial_rows[rows].astype(jnp.bfloat16)
            ref[step, :, D : D + LANES] = fold_ref[rows].astype(jnp.bfloat16)

        pl.when(group == block // OUTER)(partial(store, kept_ref))
        pl.when(group != block // OUTER)(partial(store, sent_ref))


def pair_kernel(kept_ref, other_ref, *out_refs):
    for step, out_ref in enumerate(out_refs):
        out_ref[...] = (
            kept_ref[step].astype(jnp.float32)
            + other_ref[step, :, : D + LANES].astype(jnp.float32)
        ).astype(jnp.bfloat16)


def chain_offset(step, members):
    inner = members // OUTER
    offset = (step % OUTER) * inner
    rest = step // OUTER
    bit = inner // 2
    while bit:
        offset = offset + (rest % 2) * bit
        rest = rest // 2
        bit //= 2
    return offset


def route_kernel(
    place_ref, plane_ref, other_ref, select_ref, scatter_ref, chosen_ref
):
    me, group = place_ref[0], place_ref[1]
    members = plane_ref.shape[0]
    homes = 2 * members
    total = chosen_ref.shape[0]
    pre_total = homes * TILE
    slots = select_ref.shape[0]

    def home_of(token):
        return jnp.where(token < pre_total, token // TILE, token - pre_total)

    def row_of(token):
        return jnp.where(token < pre_total, token % TILE, TILE)

    def place_of(token):
        place = home_place(home_of(token), me, group, members)
        return jnp.where(token < pre_total, place * TILE + token % TILE, pre_total + place)

    def iota(shape, axis):
        return lax.broadcasted_iota(jnp.int32, shape, axis)

    token = iota((total, homes), 0)
    home = home_of(token)
    held = ((home // (members // 2)) % 2) * members + (home // members) * (members // 2) + home % (
        members // 2
    )
    pick = jnp.where(held == iota((total, homes), 1), 1.0, 0.0).astype(jnp.bfloat16)
    own_row = iota((total, LANES), 1) == row_of(iota((total, LANES), 0))
    lane = iota((total, LANES), 1)
    lane_expert = jnp.where(
        lane >= LANES - members,
        chain_offset(lane - jnp.where(lane >= LANES - members, LANES - members, 0), members) ^ me,
        -1,
    ).astype(jnp.float32)
    chosen = jnp.zeros((total, LANES), jnp.float32)
    mine = jnp.zeros((total, LANES), jnp.float32)
    for k in range(TOPK):
        parts = [plane_ref[:, k, :].astype(jnp.float32)]
        for near in range(members // OUTER):
            at = D + LANES + near // 2 * LANES
            parts.append(other_ref[:, (near % 2) * (TILE // 2) + k, at : at + LANES].astype(jnp.float32))
        table = jnp.concatenate(parts, axis=0).astype(jnp.bfloat16)
        spread = jnp.dot(pick, table, preferred_element_type=jnp.float32)
        expert = jnp.sum(jnp.where(own_row, spread, 0.0), axis=1, keepdims=True)
        chosen = chosen + jnp.where(expert == lane_expert, 1.0, 0.0)
        mine = mine + jnp.where(own_row & (spread == me.astype(jnp.float32)), 1.0, 0.0)
    chosen_ref[...] = chosen.astype(jnp.bfloat16)
    mine_row = lax.dot_general(
        jnp.ones((8, LANES), jnp.bfloat16),
        mine.astype(jnp.bfloat16),
        ROWS_CONTRACT,
        preferred_element_type=jnp.float32,
    )
    square = (total, total)
    place_row = place_of(iota((8, total), 1))[:1]
    place_column = place_of(iota((total, LANES), 0))[:, :1]
    earlier = jnp.where(place_column <= place_row, 1.0, 0.0).astype(jnp.bfloat16)
    rank_row = jnp.dot(
        mine_row.astype(jnp.bfloat16), earlier, preferred_element_type=jnp.float32
    )[:1]
    slot = (iota((slots, total), 0) + 1).astype(jnp.float32)
    select = jnp.where((slot == rank_row) & (mine_row[:1] > 0.0), 1.0, 0.0).astype(jnp.bfloat16)
    same = jnp.where(iota(square, 0) == iota(square, 1), 1.0, 0.0).astype(jnp.bfloat16)
    select_ref[...] = select
    scatter_ref[...] = lax.dot_general(
        same, select, ROWS_CONTRACT, preferred_element_type=jnp.float32
    ).astype(jnp.bfloat16)


def home_place(index, me, group, members):
    half = members // 2
    last, home_group = index // members, (index // half) % 2
    member = chain_offset(index % half + last * half, members) ^ me
    return last * members + (home_group ^ group) * half + member // 2


def norm_kernel(resid_ref, gain_ref, *rest):
    partial_refs, (hidden_ref, normed_ref) = rest[:-2], rest[-2:]
    summed = partial_refs[0][...].astype(jnp.float32)
    for ref in partial_refs[1:]:
        summed = summed + ref[...].astype(jnp.float32)
    hidden = (resid_ref[...].astype(jnp.float32) + summed).astype(jnp.bfloat16)
    hidden_ref[...] = hidden
    hidden = hidden.astype(jnp.float32)
    gain = gain_ref[...].astype(jnp.float32)
    pre, dec = hidden[:, :D], hidden[:, D:]
    pre_mean = jnp.sum(pre * pre, axis=1, keepdims=True) / D
    dec_mean = jnp.sum(jnp.sum(dec * dec, axis=1, keepdims=True), axis=0, keepdims=True) / D
    normed_ref[:, :D] = (pre * lax.rsqrt(pre_mean + NORM_EPS) * gain[:1, :D]).astype(jnp.bfloat16)
    normed_ref[:, D:] = (dec * lax.rsqrt(dec_mean + NORM_EPS) * gain[:, D:]).astype(jnp.bfloat16)


def expert_kernel(select_ref, gate_ref, up_ref, *rest):
    piece_refs, (act_ref, pre_ref, dec_ref, fold_ref) = rest[:-4], rest[-4:]
    pre_total = pre_ref.shape[0]
    homes = pre_total // TILE
    row = 0
    for ref in piece_refs:
        count = ref.shape[0]
        pre_ref[row : row + count, :] = ref[:, :D]
        fold_ref[row : row + count, :] = ref[:, D:].astype(jnp.float32)
        row += count
    for part in range(TILE):
        dec_ref[:, part * LANES : (part + 1) * LANES] = fold_ref[
            pl.ds(part, homes, stride=TILE), :
        ].astype(jnp.bfloat16)
    select = select_ref[...]
    rows = (
        jnp.dot(select[:, :pre_total], pre_ref[...], preferred_element_type=jnp.float32)
        + jnp.dot(select[:, pre_total:], dec_ref[...], preferred_element_type=jnp.float32)
    ).astype(jnp.bfloat16)
    gate = lax.dot_general(rows, gate_ref[0], ROWS_CONTRACT, preferred_element_type=jnp.float32)
    up = lax.dot_general(rows, up_ref[0], ROWS_CONTRACT, preferred_element_type=jnp.float32)
    act_ref[...] = (gate / (1.0 + jnp.exp(-gate)) * up).astype(jnp.bfloat16)


def shared_kernel(
    units, members, place_ref, kept_ref, far_ref, router_ref, select_ref, chosen_ref, pre_ref,
    dec_ref, shared_ref, weight_ref, small_ref, fold_ref,
):
    small_kernel(place_ref, kept_ref, far_ref, router_ref, small_ref, fold_ref)
    pre_total = pre_ref.shape[0]
    homes = pre_total // TILE
    small = small_ref[...]
    first = jnp.concatenate(
        [
            lax.dot_general(
                ref[...], small, ROWS_CONTRACT, preferred_element_type=jnp.float32
            )
            for ref in (pre_ref, dec_ref)
        ],
        axis=0,
    )
    half = LANES // 2
    gate_part = first[:, :units]
    up_part = first[:, half : half + units]
    shared_act = (gate_part / (1.0 + jnp.exp(-gate_part)) * up_part).astype(jnp.bfloat16)
    shared_ref[...] = jnp.zeros_like(shared_ref)
    split = pre_total // 2
    middle = pre_total + homes // 2
    shared_ref[:split, :units] = shared_act[:split]
    shared_ref[:split, half : half + units] = shared_act[split:pre_total]
    shared_ref[split:, :units] = shared_act[pre_total:middle]
    shared_ref[split:, half : half + units] = shared_act[middle:]
    logits = first[:, LANES - members :]
    scores = 1.0 / (1.0 + jnp.exp(-logits))
    token_weight = (
        ROUTE_SCALE
        * scores[:, :1]
        / jnp.sum(scores * chosen_ref[:, LANES - members :], axis=1, keepdims=True)
    )
    high = token_weight.astype(jnp.bfloat16)
    rest = token_weight - high.astype(jnp.float32)
    middle = rest.astype(jnp.bfloat16)
    rest = (rest - middle.astype(jnp.float32)).astype(jnp.bfloat16)
    weights = jnp.dot(
        select_ref[...],
        jnp.concatenate([high, middle, rest], axis=1),
        preferred_element_type=jnp.float32,
    )
    weight_ref[...] = jnp.broadcast_to(jnp.sum(weights, axis=1, keepdims=True), weight_ref.shape)


def down_kernel(
    place_ref, act_ref, act_other_ref, shared_ref, shared_other_ref,
    down_ref, down_a_ref, down_b_ref, scatter_ref, weight_ref, kept_ref, sent_ref, fold_ref,
):
    me, group = place_ref[0], place_ref[1]
    columns = down_ref.shape[2]
    units = down_a_ref.shape[0]
    width = down_ref.shape[1] // 2
    own = down_ref[0, pl.ds(pl.multiple_of(group * width, TILE), width), :]
    other = down_ref[0, pl.ds(pl.multiple_of((1 - group) * width, TILE), width), :]
    routed = jnp.dot(act_ref[...], own, preferred_element_type=jnp.float32) + jnp.dot(
        act_other_ref[...], other, preferred_element_type=jnp.float32
    )
    routed = (routed * weight_ref[:, :1]).astype(jnp.bfloat16)
    mine_first = lax.rem(me, 2) == group
    own_down = jnp.where(mine_first, down_a_ref[...], down_b_ref[...])
    other_down = jnp.where(mine_first, down_b_ref[...], down_a_ref[...])
    both_down = jnp.concatenate([own_down, other_down], axis=0)
    half = kept_ref.shape[0]
    homes = 2 * half
    split = homes * TILE
    other = shared_other_ref[...]
    middle, decs = split // 4, other[split // 2 :].astype(jnp.float32)
    eighth = homes // 4
    other = jnp.concatenate(
        [
            other[middle : 2 * middle],
            other[:middle],
            jnp.concatenate([decs[eighth:], decs[:eighth]], axis=0).astype(jnp.bfloat16),
        ],
        axis=0,
    )
    shared = shared_ref[...]

    def down(at):
        acts = jnp.concatenate([shared[:, at : at + units], other[:, at : at + units]], axis=1)
        return jnp.dot(acts, both_down, preferred_element_type=jnp.float32)

    low_half, high_half = down(0), down(LANES // 2)
    total = jnp.dot(scatter_ref[...], routed, preferred_element_type=jnp.float32) + jnp.concatenate(
        [
            low_half[: split // 2], high_half[: split // 2], low_half[split // 2 :],
            high_half[split // 2 :],
        ],
        axis=0,
    )
    fold_ref[...] = jnp.zeros_like(fold_ref)
    for part in range(columns // LANES):
        fold_ref[pl.ds(part, homes, stride=TILE), :] = total[
            split:, part * LANES : (part + 1) * LANES
        ]
    for home in range(homes):
        place = home_place(home, me, group, half)
        ref = kept_ref if home < half else sent_ref
        at = place if home < half else place - half
        rows = slice(home * TILE, (home + 1) * TILE)
        ref[at, :, :columns] = total[rows].astype(jnp.bfloat16)
        ref[at, :, columns:] = fold_ref[rows].astype(jnp.bfloat16)


def finish_kernel(got_ref, hidden_ref, pre_ref, dec_ref):
    sources, _, width = got_ref.shape
    columns = width - LANES
    groups = D // columns
    each = sources // groups
    for group in range(groups):
        summed = got_ref[group * each].astype(jnp.float32)
        for i in range(1, each):
            summed = summed + got_ref[group * each + i].astype(jnp.float32)
        at = group * columns
        pre_ref[:, at : at + columns] = (
            hidden_ref[:, at : at + columns].astype(jnp.float32) + summed[:, :columns]
        ).astype(jnp.bfloat16)
        parts = columns // LANES
        for part in range(parts):
            row = group * parts + part
            dec_ref[:, row * LANES : (row + 1) * LANES] = (
                hidden_ref[row : row + 1, D:].astype(jnp.float32)
                + summed[part : part + 1, columns:]
            ).astype(jnp.bfloat16)


def token_shards(
    pre_query,
    pre_latent,
    pre_resid,
    dec_query,
    dec_latent,
    dec_resid,
    cache_lengths,
    latent_cache,
    sink_logits,
    uv_weight,
    out_weight,
    norm_gain,
    router,
    routes,
    gate_weight,
    up_weight,
    down_weight,
    shared_gate,
    shared_up,
    shared_down,
):
    groups = lax.axis_size("dp")
    members = lax.axis_size("expert")
    inner = members // OUTER
    homes = groups * members
    me = lax.axis_index("expert")
    my_group = lax.axis_index("dp")
    place_ids = jnp.stack([me, my_group, jnp.int32(inner)]).astype(jnp.int32)
    pre_rows = pre_query.shape[0]
    rows_dev = pre_rows + 1
    capacity = max(2, (rows_dev * TOPK + members - 1) // members)

    heads_dev, latent_rows, value_dim = uv_weight.shape
    heads_outer = heads_dev // OUTER
    uv_tiles = heads_outer * latent_rows // TILE
    block_width = D + uv_tiles * value_dim + 2 * LANES
    blocks = call(
        pack_kernel,
        [low((1, TILE, block_width))] * OUTER,
        [place_ids, out_weight, uv_weight, router.T, routes.T],
        scratch=[pltpu.VMEM((TILE, 2 * LANES), jnp.float32)],
        scalars=1,
        moved=(1, 2, 3, 4),
        flops=10_000_000_000,
    )
    pair_bit = inner // 2
    near = line_swaps(blocks, inner)
    own_pair = swap(blocks[0], "expert", pair_bit)
    line = jnp.concatenate(near, axis=0)
    far_in, own_pair = lax.optimization_barrier((line[1:], own_pair))

    pre_query, blocks = lax.optimization_barrier((pre_query, blocks))
    peers = groups * OUTER
    heads_block = heads_outer * LATENT
    att_blocks = call(
        attend_kernel,
        low((peers, pre_rows, heads_block + LANES)),
        [
            cache_lengths, pre_query, pre_latent, dec_query, dec_latent,
            latent_cache.swapaxes(1, 2),
            sink_logits.reshape(1, -1),
        ],
        scratch=[
            pltpu.VMEM((LATENT // LANES, pre_rows * pre_query.shape[1], LANES), jnp.float32),
            pltpu.VMEM((LATENT // LANES, pre_query.shape[1], LANES), jnp.float32),
            pltpu.VMEM((peers * TILE, LANES), jnp.float32),
        ],
        scalars=1,
        flops=100_000_000,
    )
    lines = [
        [g * members + o * inner + i for g in range(groups) for o in range(OUTER)]
        for i in range(inner)
    ]
    both = ("dp", "expert")
    far_pair = swap(far_in, "expert", pair_bit)
    att_got = lax.all_to_all(
        att_blocks, both, split_axis=0, concat_axis=0, axis_index_groups=lines, tiled=True
    )
    units = shared_gate.shape[1] // members
    padded = -(-units // TILE) * TILE
    depth = shared_gate.shape[0]
    line, line_gate = lax.optimization_barrier((line, shared_gate))
    *spread, down_a, down_b = call(
        partial(spread_kernel, units),
        [low((inner, 2 * padded, depth))] * OUTER + [low((units, shared_down.shape[1]))] * 2,
        [place_ids, line_gate.T, shared_up.T, shared_down],
        scalars=1,
    )
    far_pair, *spread = lax.optimization_barrier((far_pair, *spread))
    pieces = [line, own_pair, far_pair]
    pieces = pieces + [swap(piece, "expert", 1) for piece in pieces]
    kept_sums, sent_sums, router_blocks, routes_plane = call(
        project_kernel,
        [
            low((OUTER, pre_rows, D + LANES)),
            low((OUTER, pre_rows, D + LANES * (1 + members // (2 * OUTER)))),
        ]
        + [low((members, TILE, LANES))] * 2,
        [place_ids, att_got, *pieces],
        scratch=[
            pltpu.VMEM((peers * pre_rows + TILE, heads_block), jnp.bfloat16),
            pltpu.VMEM((peers * TILE, LANES), jnp.float32),
            pltpu.VMEM((heads_block, value_dim), jnp.bfloat16),
        ],
        scalars=1,
        flops=300_000_000,
        moved=tuple(range(2, 2 + len(pieces))),
    )
    other_sums = swap(sent_sums, "dp", 1)

    shared_got = line_swaps(spread, inner)
    pre_total = homes * pre_rows
    total = pre_total + homes
    slots = homes * capacity
    resid = jnp.concatenate([pre_resid, fold_row(dec_resid)], axis=1)
    gain = jnp.concatenate(
        [jnp.broadcast_to(norm_gain[None], (TILE, D)), norm_gain.reshape(TILE, LANES)], axis=1
    )
    sums = call(pair_kernel, [low(resid.shape)] * OUTER, [kept_sums, other_sums], flops=1_000_000)
    sums_got = line_swaps(sums, inner)
    _, other_routes = lax.optimization_barrier((sums[0], other_sums))
    select, scatter, chosen = call(
        route_kernel,
        [low((slots, total)), low((total, slots)), low((total, LANES))],
        [place_ids, routes_plane, other_routes],
        scalars=1,
        vmem=16,
    )
    select, scatter, chosen, *sums_got = lax.optimization_barrier(
        (select, scatter, chosen, *sums_got)
    )
    _, *shared_got = lax.optimization_barrier((sums[0], *shared_got))
    kept = jnp.concatenate([block[:pair_bit] for block in shared_got], axis=0)
    sent = jnp.concatenate([block[pair_bit:] for block in shared_got], axis=0)
    far = swap(sent, "expert", pair_bit)
    shared_kept = jnp.concatenate([kept[::pair_bit], far[::pair_bit]], axis=0)
    shared_sent = jnp.concatenate([kept[1::pair_bit], far[1::pair_bit]], axis=0)
    shared_far = swap(shared_sent, "expert", 1)
    middle = OUTER // 2
    hidden, normed = call(
        norm_kernel, [low(resid.shape)] * 2, [resid, gain, *sums_got], flops=20_000_000_000
    )

    line = line_swaps([normed] * OUTER, inner)
    middle = OUTER // 2
    row_pieces = []
    for part in (line[:middle], line[middle:]):
        row_pieces.append(jnp.concatenate(part, axis=0))
    piece_a, piece_b = row_pieces
    a_pair, b_group = swap(piece_a, "expert", pair_bit), swap(piece_b, "dp", 1)
    a_group, b_pair = swap(piece_a, "dp", 1), swap(piece_b, "expert", pair_bit)
    a_both, b_both = swap(a_pair, "dp", 1), swap(b_group, "expert", pair_bit)
    row_pieces = [piece_a, piece_b, a_pair, b_pair, a_group, b_group, a_both, b_both]
    row_pieces = row_pieces + [swap(piece, "expert", 1) for piece in row_pieces]

    width = gate_weight.shape[2]
    gate_rows, up_rows = gate_weight.swapaxes(1, 2), up_weight.swapaxes(1, 2)
    expert_act, pre_tokens, dec_tokens = call(
        expert_kernel,
        [low((slots, width)), low((pre_total, D)), low((homes, D))],
        [select, gate_rows, up_rows, *row_pieces],
        scratch=[pltpu.VMEM((pre_total, LANES), jnp.float32)],
        flops=2_000_000_000,
        vmem=20,
    )
    expert_act_other = swap(expert_act, "dp", 1)
    shared_act, slot_weight = call(
        partial(shared_kernel, units, members),
        [low((total // 2, LANES)), jax.ShapeDtypeStruct((slots, LANES), jnp.float32)],
        [
            place_ids, shared_kept, shared_far, router_blocks, select, chosen, pre_tokens,
            dec_tokens,
        ],
        scratch=[
            pltpu.VMEM((LANES, D), jnp.bfloat16),
            pltpu.VMEM((members * TILE, LANES), jnp.float32),
        ],
        scalars=1,
        flops=500_000_000,
        vmem=12,
    )
    shared_act_other = swap(shared_act, "dp", 1)
    shared_act, down_a, down_b = lax.optimization_barrier((shared_act, down_a, down_b))
    half = members // 2
    down_a = lax.ppermute(
        down_a,
        "expert",
        [(i, 2 * i if i < half else 2 * (i - half) + 1) for i in range(members)],
    )
    down_b = lax.ppermute(
        down_b,
        "expert",
        [(i, 2 * i + 1 if i < half else 2 * (i - half)) for i in range(members)],
    )
    col_width = down_weight.shape[2]
    kept, sent = call(
        down_kernel,
        [low((homes // 2, TILE, col_width + LANES))] * 2,
        [
            place_ids, expert_act, expert_act_other, shared_act, shared_act_other,
            down_weight, down_a, down_b, scatter, slot_weight,
        ],
        scratch=[pltpu.VMEM((pre_total, LANES), jnp.float32)],
        scalars=1,
        flops=1_000_000_000,
        vmem=20,
    )
    pair_sum = (kept.astype(jnp.float32) + swap(sent, "expert", 1).astype(jnp.float32)).astype(
        jnp.bfloat16
    )
    halves = [
        [g * members + 2 * i + b for g in range(groups) for i in range(members // 2)]
        for b in range(2)
    ]
    home_got = lax.all_to_all(
        pair_sum, both, split_axis=0, concat_axis=0, axis_index_groups=halves, tiled=True
    )
    return tuple(
        call(finish_kernel, [low(pre_resid.shape), low(dec_resid.shape)], [home_got, hidden])
    )


def fits(mesh, heads, ff):
    groups, members = mesh.shape["dp"], mesh.shape["expert"]
    return (
        groups == 2
        and members % (2 * OUTER) == 0
        and (heads // groups) % OUTER == 0
        and ff % (groups * members) == 0
    )


def solution(mesh):
    in_specs = (
        P(("dp", "expert"), None, None),
        P(("dp", "expert"), None),
        P(("dp", "expert"), None),
        P(("dp", "expert"), None, None),
        P(("dp", "expert"), None),
        P(("dp", "expert"), None),
        P(("dp", "expert")),
        P(("dp", "expert"), None, None),
        P(),
        P("dp", "expert", None),
        P("dp", "expert", None),
        P(),
        P(None, "expert"),
        P(("dp", "expert"), None),
        P("expert", None, "dp"),
        P("expert", None, "dp"),
        P("expert", None, "dp"),
        P("expert", "dp"),
        P("expert", "dp"),
        P("expert", "dp"),
    )
    out_specs = (P(("dp", "expert"), None), P(("dp", "expert"), None))

    def layer(*args):
        plan = token_shards if fits(mesh, args[9].shape[0], args[17].shape[1]) else shards
        return jax.shard_map(
            plan, mesh=mesh, in_specs=in_specs, out_specs=out_specs, check_vma=False
        )(*args)

    return layer
```
